32 devices in a mesh: dp: 4 (over y, x), tensor: 8 (over z, core).
Axes of the slice: x: 2, y: 2, z: 4, core: 2. Of those that a mesh axis runs over, the one named last changes fastest.
Arguments:
- tokens: bfloat16 [8192, 2048], P(('dp', 'tensor')), may hold values from -6 to 6
- cotangent: bfloat16 [8192, 2048], P(('dp', 'tensor'))
- kv_later: bfloat16 [8192, 256], P(('dp', 'tensor')), may hold values from -6 to 6
- lengths: int32 [4, 4], P('dp'), may hold values from 1 to 1984, as said below
- query_weight: float32 [2048, 2048], P('dp', 'tensor'), may hold values from -0.125 to 0.125
- query_moment: float32 [2048, 2048], P('dp', 'tensor'), may hold values from -0.0009765625 to 0.0009765625
- query_average: float32 [2048, 2048], P('dp', 'tensor'), may hold values from -0.125 to 0.125
- keyvalue_weight: float32 [2048, 256], P('dp'), may hold values from -0.125 to 0.125
- keyvalue_moment: float32 [2048, 256], P('dp'), may hold values from -0.0009765625 to 0.0009765625
- keyvalue_average: float32 [2048, 256], P('dp'), may hold values from -0.125 to 0.125
- output_weight: float32 [2048, 2048], P('tensor', 'dp')
- output_moment: float32 [2048, 2048], P('tensor', 'dp'), may hold values from -0.0009765625 to 0.0009765625
- output_average: float32 [2048, 2048], P('tensor', 'dp'), may hold values from -1 to 1
- gateup_weight: float32 [2, 2048, 5632], P(None, 'dp', 'tensor'), may hold values from -0.125 to 0.125
- gateup_moment: float32 [2, 2048, 5632], P(None, 'dp', 'tensor'), may hold values from -0.0009765625 to 0.0009765625
- gateup_average: float32 [2, 2048, 5632], P(None, 'dp', 'tensor'), may hold values from -0.125 to 0.125
- down_weight: float32 [5632, 2048], P('tensor', 'dp')
- down_moment: float32 [5632, 2048], P('tensor', 'dp'), may hold values from -0.0009765625 to 0.0009765625
- down_average: float32 [5632, 2048], P('tensor', 'dp'), may hold values from -0.078125 to 0.078125
- norm_gains: float32 [2, 2048], P(None, 'dp')
- gains_moment: float32 [2, 2048], P(None, 'dp'), may hold values from -0.0009765625 to 0.0009765625
- gains_average: float32 [2, 2048], P(None, 'dp'), may hold values from 0.5 to 1.5
Outputs:
- mixed: float32 [8192, 2048], P(('dp', 'tensor'))
- mixed_low: bfloat16 [8192, 2048], P(('dp', 'tensor'))
- tokens_grad: float32 [8192, 2048], P(('dp', 'tensor'))
- grad_norm: float32 [], replicated
- query_grad: float32 [2048, 2048], P('dp', 'tensor')
- query_moment_new: float32 [2048, 2048], P('dp', 'tensor')
- query_average_new: float32 [2048, 2048], P('dp', 'tensor')
- query_new: float32 [2048, 2048], P('dp', 'tensor')
- query_new_low: bfloat16 [2048, 2048], P('dp', 'tensor')
- keyvalue_grad: float32 [2048, 256], P('dp')
- keyvalue_moment_new: float32 [2048, 256], P('dp')
- keyvalue_average_new: float32 [2048, 256], P('dp')
- keyvalue_new: float32 [2048, 256], P('dp')
- keyvalue_new_low: bfloat16 [2048, 256], P('dp')
- output_grad: float32 [2048, 2048], P('tensor', 'dp')
- output_moment_new: float32 [2048, 2048], P('tensor', 'dp')
- output_average_new: float32 [2048, 2048], P('tensor', 'dp')
- output_new: float32 [2048, 2048], P('tensor', 'dp')
- output_new_low: bfloat16 [2048, 2048], P('tensor', 'dp')
- gateup_grad: float32 [2, 2048, 5632], P(None, 'dp', 'tensor')
- gateup_moment_new: float32 [2, 2048, 5632], P(None, 'dp', 'tensor')
- gateup_average_new: float32 [2, 2048, 5632], P(None, 'dp', 'tensor')
- gateup_new: float32 [2, 2048, 5632], P(None, 'dp', 'tensor')
- gateup_new_low: bfloat16 [2, 2048, 5632], P(None, 'dp', 'tensor')
- down_grad: float32 [5632, 2048], P('tensor', 'dp')
- down_moment_new: float32 [5632, 2048], P('tensor', 'dp')
- down_average_new: float32 [5632, 2048], P('tensor', 'dp')
- down_new: float32 [5632, 2048], P('tensor', 'dp')
- down_new_low: bfloat16 [5632, 2048], P('tensor', 'dp')
- gains_grad: float32 [2, 2048], P(None, 'dp')
- gains_moment_new: float32 [2, 2048], P(None, 'dp')
- gains_average_new: float32 [2, 2048], P(None, 'dp')
- gains_new: float32 [2, 2048], P(None, 'dp')
- gains_new_low: bfloat16 [2, 2048], P(None, 'dp')
The draws below stay inside these ranges and needn't reach their ends.
Inputs may be any that keep to these rules, and one draw needn't show every extreme that they name: `lengths`: each row sums to 2048; one document of each row has exactly 1984 tokens and the others share the rest.
All inputs are finite; a program needn't handle non-finite values.
Results may differ from the reference program's by a relative error of at most 0.025.
Values may be sent and summed in bfloat16 or wider, within the bound.
A program may use at most 256 MiB of HBM per device.

```python
import math
import jax
import jax.numpy as jnp
from jax import lax

D = 2048
HEADS = 16
HD = 128
FF = 5632
SEQ = 2048
DOCS = 4
STEP = 10
SEQS = 4
TOKENS = 8192


def slope(shape, axis, top_factor):
    place = lax.broadcasted_iota(jnp.float32, shape, axis) / shape[axis]
    return 1.0 + (top_factor - 1.0) * place


def draw_cotangent(key, part):
    key = jax.random.fold_in(key, 3)
    shape = (TOKENS, D)
    base = jax.random.normal(key, shape, jnp.float32)
    top_factor = 3.0
    level = 0.5
    return (base * slope(shape, 1, top_factor) * level).astype(jnp.bfloat16)


def draw_output_weight(key, part):
    key = jax.random.fold_in(key, 5)
    shape = (HEADS * HD, D)
    base = jax.random.normal(key, shape, jnp.float32)
    top_factor = 3.0
    level = 0.5
    return base * slope(shape, 0, top_factor) * level * (HEADS * HD * 32 // SEQ) ** (-0.5)


def draw_down_weight(key, part):
    key = jax.random.fold_in(key, 7)
    shape = (FF, D)
    base = jax.random.normal(key, shape, jnp.float32)
    top_factor = 3.0
    level = 0.5
    return base * slope(shape, 0, top_factor) * level * FF ** (-0.5)


def draw_norm_gains(key, part):
    key = jax.random.fold_in(key, 9)
    shape = (2, D)
    base = jax.random.uniform(key, shape, jnp.float32, 0.8, 1.2)
    top_factor = 3.0
    level = 0.6
    return base * slope(shape, 1, top_factor) * level


def draw_lengths(key, part):
    key = jax.random.fold_in(key, 11)
    rest_total = SEQ // 32

    def one_row(row_key):
        cut_key, place_key = jax.random.split(row_key)
        cuts = jnp.sort(jax.random.permutation(cut_key, rest_total - 1)[:DOCS - 2] + 1).astype(jnp.int32)
        edges = jnp.concatenate([jnp.zeros((1,), jnp.int32), cuts, jnp.full((1,), rest_total, jnp.int32)])
        short_docs = edges[1:] - edges[:-1]
        long_place = jax.random.randint(place_key, (), 0, DOCS)
        slots = jnp.arange(DOCS, dtype=jnp.int32)
        short_index = jnp.clip(slots - (slots > long_place).astype(jnp.int32), 0, DOCS - 2)
        return jnp.where(slots == long_place, SEQ - rest_total, short_docs[short_index]).astype(jnp.int32)
    return jax.vmap(one_row)(jax.random.split(key, SEQS)).astype(jnp.int32)


def steps_of(stream_key, shape, cuts, smallest, high):
    def one(dim, shards_of):
        draws = jax.random.uniform(jax.random.fold_in(jax.random.fold_in(stream_key, 6), dim), (shards_of,), jnp.float32, smallest / len(cuts), high / len(cuts))
        return jnp.repeat(jnp.exp(draws), shape[dim] // shards_of).reshape((-1,) + (1,) * (len(shape) - dim - 1))

    gain = one(*cuts[0])
    for cut in cuts[1:]:
        gain = gain * one(*cut)
    return gain


def scatter_about(own_key, shape, width, limit, pieces=(), held_as=jnp.bfloat16):
    factor_of = steps_of(own_key, shape, pieces, -0.22, 0.18) if pieces else 1.0
    values = jax.random.normal(own_key, shape, jnp.float32) * width * factor_of
    return jnp.minimum(jnp.maximum(values, -limit), limit).astype(held_as)


def setup_inputs(seed: int = 0) -> dict:
    splits = jax.random.split(jax.random.key(seed), 23)
    return {
        "tokens": scatter_about(splits[0], (TOKENS, D), 1.0, 6.0, ((0, 32),)),
        "cotangent": draw_cotangent(jax.random.fold_in(splits[22], 71), 0),
        "kv_later": scatter_about(splits[2], (TOKENS, 2 * HD), 1.0, 6.0, ((0, 32),)),
        "lengths": draw_lengths(jax.random.fold_in(splits[22], 71), 0),
        "query_weight": scatter_about(splits[4], (D, HEADS * HD), D ** -0.5, 0.125, ((0, 4), (1, 8)), jnp.float32),
        "query_moment": scatter_about(splits[5], (D, HEADS * HD), ((2 * D * HEADS * HD + 2 * D * HD + 3 * D * FF + 2 * D) ** -0.5), 0.0009765625, ((0, 4), (1, 8)), jnp.float32),
        "query_average": scatter_about(splits[6], (D, HEADS * HD), D ** -0.5, 0.125, ((0, 4), (1, 8)), jnp.float32),
        "keyvalue_weight": scatter_about(splits[7], (D, 2 * HD), D ** -0.5, 0.125, ((0, 4),), jnp.float32),
        "keyvalue_moment": scatter_about(splits[8], (D, 2 * HD), ((2 * D * HEADS * HD + 2 * D * HD + 3 * D * FF + 2 * D) ** -0.5), 0.0009765625, ((0, 4),), jnp.float32),
        "keyvalue_average": scatter_about(splits[9], (D, 2 * HD), D ** -0.5, 0.125, ((0, 4),), jnp.float32),
        "output_weight": draw_output_weight(jax.random.fold_in(splits[22], 71), 0),
        "output_moment": scatter_about(splits[11], (HEADS * HD, D), ((2 * D * HEADS * HD + 2 * D * HD + 3 * D * FF + 2 * D) ** -0.5), 0.0009765625, ((0, 8), (1, 4)), jnp.float32),
        "output_average": scatter_about(splits[12], (HEADS * HD, D), (HEADS * HD * 32 // SEQ) ** -0.5, 1.0, ((0, 8), (1, 4)), jnp.float32),
        "gateup_weight": scatter_about(splits[13], (2, D, FF), D ** -0.5, 0.125, ((1, 4), (2, 8)), jnp.float32),
        "gateup_moment": scatter_about(splits[14], (2, D, FF), ((2 * D * HEADS * HD + 2 * D * HD + 3 * D * FF + 2 * D) ** -0.5), 0.0009765625, ((1, 4), (2, 8)), jnp.float32),
        "gateup_average": scatter_about(splits[15], (2, D, FF), D ** -0.5, 0.125, ((1, 4), (2, 8)), jnp.float32),
        "down_weight": draw_down_weight(jax.random.fold_in(splits[22], 71), 0),
        "down_moment": scatter_about(splits[17], (FF, D), ((2 * D * HEADS * HD + 2 * D * HD + 3 * D * FF + 2 * D) ** -0.5), 0.0009765625, ((0, 8), (1, 4)), jnp.float32),
        "down_average": scatter_about(splits[18], (FF, D), FF ** -0.5, 0.078125, ((0, 8), (1, 4)), jnp.float32),
        "norm_gains": draw_norm_gains(jax.random.fold_in(splits[22], 71), 0),
        "gains_moment": scatter_about(splits[20], (2, D), ((2 * D * HEADS * HD + 2 * D * HD + 3 * D * FF + 2 * D) ** -0.5), 0.0009765625, ((1, 4),), jnp.float32),
        "gains_average": jnp.clip(1.0 + 0.1 * jax.random.normal(splits[21], (2, D), jnp.float32), 0.5, 1.5),
    }


EPSILON = 1e-05
MASKED = -1000000000.0
CLIP = 1.0
MOMENTUM = 0.9
LEARNING_RATES = (12.0, 12.0, 480.0, 48.0, 12.0, 960.0)
AVERAGE_TOP = 0.999
ROPE_BASE = 10000.0
HIGHEST_PRECISION = lax.Precision.HIGHEST

@jax.custom_vjp
def low(v):
    return lax.optimization_barrier(v.astype(jnp.bfloat16)).astype(jnp.float32)

@jax.custom_vjp
def low_back(v):
    return v

def low_keep(v):
    return (low(v), None)

def low_pass(kept, grad):
    return (grad,)

def back_keep(v):
    return (v, None)

def back_low(kept, grad):
    return (low(grad),)
low.defvjp(low_keep, low_pass)
low_back.defvjp(back_keep, back_low)

def rms_normed(field, gain_row):
    return field * lax.rsqrt(lax.optimization_barrier(jnp.mean(field * field, axis=-1, keepdims=True)) + EPSILON) * gain_row

def doc_layout(doc_lengths, length):
    endings = jnp.cumsum(doc_lengths).astype(jnp.int32)
    beginnings = (endings - doc_lengths).astype(jnp.int32)
    places = jnp.arange(length, dtype=jnp.int32)
    segment = lax.optimization_barrier(jnp.sum((places[:, None] >= endings[None, :]).astype(jnp.int32), axis=1)).astype(jnp.int32)
    picked = segment[:, None] == jnp.arange(doc_lengths.shape[0], dtype=jnp.int32)[None, :]
    position = places - lax.optimization_barrier(jnp.sum(jnp.where(picked, beginnings[None, :], 0), axis=1)).astype(jnp.int32)
    return (segment, position)

def rotary_tables(position):
    half_size = HD // 2
    frequency = jnp.exp(jnp.arange(half_size, dtype=jnp.float32) * (-2.0 * math.log(ROPE_BASE) / HD))
    angles = position.astype(jnp.float32)[:, None] * frequency[None, :]
    return (jnp.cos(angles), jnp.sin(angles))

def rotate(field, cosine, sine):
    half_size = field.shape[-1] // 2
    front_part = field[..., :half_size]
    back_part = field[..., half_size:]
    return jnp.concatenate([front_part * cosine - back_part * sine, front_part * sine + back_part * cosine], axis=-1)

def visible(begin_row, block_size, segment):
    length = segment.shape[0]
    query_places = begin_row + jnp.arange(block_size, dtype=jnp.int32)
    key_places = jnp.arange(length, dtype=jnp.int32)
    query_segment = lax.dynamic_slice_in_dim(segment, begin_row, block_size)
    return (query_segment[:, None] == segment[None, :]) & (key_places[None, :] <= query_places[:, None])

def attend(queries, keys_low, values_low, segment):
    length = keys_low.shape[0]
    block_size = min(512, length)
    block_count = length // block_size
    scale_factor = 1.0 / math.sqrt(HD)
    query_blocks = queries.reshape(HEADS, block_count, block_size, HD).transpose(1, 0, 2, 3)
    starts = jnp.arange(block_count, dtype=jnp.int32) * block_size

    def one_block(query_block, begin_row):
        scores = low_back(jnp.einsum('hqd,kd->hqk', query_block, keys_low, precision=HIGHEST_PRECISION) * scale_factor)
        scores = jnp.where(visible(begin_row, block_size, segment)[None], scores, MASKED)
        row_max = lax.optimization_barrier(jnp.max(scores, axis=-1, keepdims=True))
        log_total = row_max + jnp.log(lax.optimization_barrier(jnp.sum(jnp.exp(scores - row_max), axis=-1, keepdims=True)))
        attn_probs = low(jnp.exp(scores - log_total))
        return low(low_back(jnp.einsum('hqk,kd->hqd', attn_probs, values_low, precision=HIGHEST_PRECISION)))
    checked = jax.checkpoint(one_block)

    def block_step(block_item):
        return checked(block_item[0], block_item[1])
    attended = lax.map(block_step, (query_blocks, starts))
    return attended.transpose(1, 0, 2, 3).reshape(HEADS, length, HD)

def layer(weights, tokens_in, segment, cosine, sine):
    query_weight, keyvalue_weight, output_weight, gateup_weight, down_weight, norm_gains = weights
    length = tokens_in.shape[0]
    normed_one = low(rms_normed(tokens_in, norm_gains[0]))
    query_pre = low_back(jnp.dot(normed_one, query_weight, precision=HIGHEST_PRECISION))
    kv_pre = low_back(jnp.dot(normed_one, keyvalue_weight, precision=HIGHEST_PRECISION))
    queries = low(rotate(query_pre.reshape(length, HEADS, HD).transpose(1, 0, 2), cosine, sine))
    keys_low = low(rotate(kv_pre[:, :HD], cosine, sine))
    values_low = low(kv_pre[:, HD:])
    attended = attend(queries, keys_low, values_low, segment)
    attn_rows = attended.transpose(1, 0, 2).reshape(length, HEADS * HD)
    hidden_one = tokens_in + low_back(jnp.dot(attn_rows, output_weight, precision=HIGHEST_PRECISION))
    normed_two = low(rms_normed(hidden_one, norm_gains[1]))
    gate = low_back(jnp.dot(normed_two, gateup_weight[0], precision=HIGHEST_PRECISION))
    up_part = low_back(jnp.dot(normed_two, gateup_weight[1], precision=HIGHEST_PRECISION))
    middle = low(jax.nn.silu(gate) * up_part)
    mixed = hidden_one + jnp.dot(middle, down_weight, precision=HIGHEST_PRECISION)
    return (mixed, keys_low, values_low)

def advance(grad_raw, weight, moment, average, factor, rate):
    average_decay = min(AVERAGE_TOP, (1.0 + STEP) / (10.0 + STEP))
    clipped = grad_raw * factor
    moment_new = MOMENTUM * moment + clipped
    weight_new = weight - rate * (clipped + MOMENTUM * moment_new)
    average_new = average_decay * average + (1.0 - average_decay) * weight_new
    return (clipped, moment_new, average_new, weight_new, weight_new.astype(jnp.bfloat16))

def reference(tokens, cotangent, kv_later, lengths, query_weight, query_moment, query_average, keyvalue_weight, keyvalue_moment, keyvalue_average, output_weight, output_moment, output_average, gateup_weight, gateup_moment, gateup_average, down_weight, down_moment, down_average, norm_gains, gains_moment, gains_average):
    masters = (query_weight, keyvalue_weight, output_weight, gateup_weight, down_weight, norm_gains)
    lowered = tuple((low(weight) for weight in masters))
    token_seqs = tokens.astype(jnp.float32).reshape(SEQS, SEQ, D)
    grad_seqs_in = cotangent.astype(jnp.float32).reshape(SEQS, SEQ, D)
    later_seqs = kv_later.astype(jnp.float32).reshape(SEQS, SEQ, 2 * HD)

    def one_sequence(totals, seq_item):
        token_seq, grad_seq, later_seq, doc_lengths = seq_item
        segment, position = doc_layout(doc_lengths, SEQ)
        cosine, sine = rotary_tables(position)

        def run(weights, tokens_in):
            return layer(weights, tokens_in, segment, cosine, sine)
        outputs, pull = jax.vjp(run, lowered, token_seq)
        weight_grads, token_grad = pull((grad_seq, later_seq[:, :HD], later_seq[:, HD:]))
        totals = jax.tree.map(lambda held_sum, fresh_sum: held_sum + fresh_sum, totals, weight_grads)
        return (totals, (outputs[0], token_grad))
    start_totals = jax.tree.map(jnp.zeros_like, lowered)
    grads, (mixed_seqs, grad_token_seqs) = lax.scan(one_sequence, start_totals, (token_seqs, grad_seqs_in, later_seqs, lengths))
    squares = jnp.float32(0.0)
    for grad_item in grads:
        squares = squares + jnp.sum(grad_item * grad_item)
    grad_norm = jnp.sqrt(squares)
    factor = jnp.minimum(1.0, CLIP / (grad_norm + 1e-06))
    moments = (query_moment, keyvalue_moment, output_moment, gateup_moment, down_moment, gains_moment)
    averages = (query_average, keyvalue_average, output_average, gateup_average, down_average, gains_average)
    updated = [advance(grads[index], masters[index], moments[index], averages[index], factor, LEARNING_RATES[index]) for index in range(6)]
    mixed = mixed_seqs.reshape(TOKENS, D)
    tokens_grad = grad_token_seqs.reshape(TOKENS, D)
    return (mixed, mixed.astype(jnp.bfloat16), tokens_grad, grad_norm, updated[0][0], updated[0][1], updated[0][2], updated[0][3], updated[0][4], updated[1][0], updated[1][1], updated[1][2], updated[1][3], updated[1][4], updated[2][0], updated[2][1], updated[2][2], updated[2][3], updated[2][4], updated[3][0], updated[3][1], updated[3][2], updated[3][3], updated[3][4], updated[4][0], updated[4][1], updated[4][2], updated[4][3], updated[4][4], updated[5][0], updated[5][1], updated[5][2], updated[5][3], updated[5][4])
```

```python
import functools
import math

import jax
import jax.numpy as jnp
from jax import lax
from jax.experimental import pallas as pl
from jax.experimental.pallas import tpu as pltpu
from jax.sharding import PartitionSpec as P

HD = 128
STEP = 10


EPSILON = 1e-05
MASKED = -1000000000.0
CLIP = 1.0
MOMENTUM = 0.9
LEARNING_RATES = (12.0, 12.0, 480.0, 48.0, 12.0, 960.0)
AVERAGE_TOP = 0.999
ROPE_BASE = 10000.0

MESH = pl.DeviceIdType.MESH
LOW = jnp.bfloat16
F32 = jnp.float32


def dot_nn(a, b):
    return jnp.dot(a, b, preferred_element_type=F32)


def dot_nt(a, b):
    return lax.dot_general(a, b, (((1,), (1,)), ((), ())), preferred_element_type=F32)


def dot_tn(a, b):
    return lax.dot_general(a, b, (((0,), (0,)), ((), ())), preferred_element_type=F32)


class Place:
    def __init__(self, nd, nt):
        self.nd, self.nt = nd, nt
        self.nx = 2 if nd % 2 == 0 else 1
        self.ny = nd // self.nx
        self.nz = nt // 2
        self.dp = lax.axis_index("dp")
        self.t = lax.axis_index("tensor")
        self.y = self.dp // self.nx
        self.x = lax.rem(self.dp, self.nx)
        self.z = self.t // 2
        self.c = lax.rem(self.t, 2)

    def x_peer(self):
        return self.y * self.nx + (1 - self.x)

    def y_peer(self, step):
        return lax.rem(self.y + step, self.ny) * self.nx + self.x

    def xy_peer(self, step):
        return lax.rem(self.y + step, self.ny) * self.nx + (1 - self.x)

    def sibling(self):
        return self.z * 2 + (1 - self.c)


def remote(src, dst, send, recv, dp, t):
    return pltpu.make_async_remote_copy(src, dst, send, recv, device_id=(dp, t), device_id_type=MESH)


def greet(at, dps=True, zs=True, core=True):
    bar = pltpu.get_barrier_semaphore()
    count = 0
    targets = []
    if dps:
        targets.append((at.x_peer(), at.t))
        targets += [(at.y_peer(s), at.t) for s in range(1, at.ny)]
    if core:
        targets.append((at.dp, at.sibling()))
    for target in targets:
        pl.semaphore_signal(bar, inc=1, device_id=target, device_id_type=MESH)
        count += 1
    if zs:
        @pl.when(at.z > 0)
        def _():
            pl.semaphore_signal(bar, inc=1, device_id=(at.dp, at.t - 2), device_id_type=MESH)

        @pl.when(at.z < at.nz - 1)
        def _():
            pl.semaphore_signal(bar, inc=1, device_id=(at.dp, at.t + 2), device_id_type=MESH)

        count = count + (at.z > 0).astype(jnp.int32) + (at.z < at.nz - 1).astype(jnp.int32)
    pl.semaphore_wait(bar, count)


def far_first(k, z, nz):
    j = nz - 1 - k
    m = jnp.minimum(z, nz - 1 - z)
    s = (j + 1) // 2
    two = jnp.where(lax.rem(j, 2) == 1, z - s, z + s)
    one = jnp.where(z < nz - 1 - z, j, nz - 1 - j)
    return jnp.where(j <= 2 * m, two, one)


class Gather:
    def __init__(self, at, src, dst, xs, ys, xf, yf, recv, kind):
        self.at, self.src, self.dst, self.kind = at, src, dst, kind
        self.xs, self.ys, self.xf, self.yf, self.recv = xs, ys, xf, yf, recv

    def own(self):
        at = self.at
        out = [remote(self.src, self.dst(at.dp), self.xs, self.recv.at[at.dp], at.x_peer(), at.t)]
        for s in range(1, at.ny):
            out.append(remote(self.src, self.dst(at.dp), self.ys.at[s - 1], self.recv.at[at.dp], at.y_peer(s), at.t))
        return out

    def passed(self):
        at = self.at
        out = []
        for s in range(1, at.ny):
            if self.kind == 0:
                o = at.x_peer()
                out.append(remote(self.dst(o), self.dst(o), self.yf.at[s - 1], self.recv.at[o], at.y_peer(s), at.t))
            else:
                o = at.y_peer(s)
                out.append(remote(self.dst(o), self.dst(o), self.xf.at[s - 1], self.recv.at[o], at.x_peer(), at.t))
        return out

    def arrived(self, o):
        remote(self.src, self.dst(o), self.xs, self.recv.at[o], self.at.x_peer(), self.at.t).wait_recv()

    def start(self):
        for cp in self.own():
            cp.start()

    def forward(self):
        at = self.at
        if self.kind == 0:
            self.arrived(at.x_peer())
        else:
            for s in range(1, at.ny):
                self.arrived(at.y_peer(s))
        for cp in self.passed():
            cp.start()

    def finish(self):
        at = self.at
        if self.kind == 0:
            for s in range(1, at.ny):
                self.arrived(at.y_peer(s))
        else:
            self.arrived(at.x_peer())
        for s in range(1, at.ny):
            self.arrived(at.xy_peer(s))

    def drain(self):
        for cp in self.own() + self.passed():
            cp.wait_send()


def mlp_kernel(nd, nt, xn_in, dy_in, wgu_in, wd_in,
               dxn_out, dwgu_out, dwd_out, out_out,
               xall, dyv, wgu, wd, mid, dg, du, psend, pown, precv, zrecv, stage,
               lsem, wx, wy, wxf, wyf, wr, ar, ac, asr, asl, ps, pr, zs, zr, osem, wsem):
    at = Place(nd, nt)
    nz = at.nz
    R, D = xn_in.shape
    Dd = wgu_in.shape[1]
    F = wgu_in.shape[2]
    Fh = F // 2
    rows = lambda t: pl.ds(pl.multiple_of(t * R, R), R)
    dcols = lambda o: pl.ds(pl.multiple_of(o * Dd, Dd), Dd)

    own_loads = [
        pltpu.make_async_copy(xn_in, xall.at[rows(at.t)], lsem.at[0]),
        pltpu.make_async_copy(dy_in, dyv, lsem.at[1]),
        pltpu.make_async_copy(wgu_in, wgu.at[:, dcols(at.dp)], lsem.at[2]),
        pltpu.make_async_copy(wd_in, wd.at[at.dp], lsem.at[3]),
    ]
    for cp in own_loads:
        cp.start()
    greet(at)

    gathers = []
    for p in range(2):
        gathers.append(Gather(at, wgu_in.at[p], lambda o, p=p: wgu.at[p, dcols(o)],
                              wx.at[p], wy.at[p], wxf.at[p], wyf.at[p], wr.at[p], p))
    for p in range(2):
        gathers.append(Gather(at, wd_in.at[pl.ds(p * Fh, Fh)], lambda o, p=p: wd.at[o, pl.ds(p * Fh, Fh)],
                              wx.at[2 + p], wy.at[2 + p], wxf.at[2 + p], wyf.at[2 + p], wr.at[2 + p], p))

    def right(o):
        return remote(xall.at[rows(o)], xall.at[rows(o)], asr.at[o], ar.at[o], at.dp, at.t + 2)

    def left(o):
        return remote(xall.at[rows(o)], xall.at[rows(o)], asl.at[o], ar.at[o], at.dp, at.t - 2)

    def across(o):
        return remote(xall.at[rows(o)], xall.at[rows(o)], ac.at[o], ar.at[o], at.dp, at.sibling())

    own_loads[0].wait()
    across(at.t).start()
    pl.when(at.z < nz - 1)(lambda: right(at.t).start())
    pl.when(at.z > 0)(lambda: left(at.t).start())
    for g in gathers[:2]:
        g.start()
    for g in gathers[2:]:
        g.start()

    def line_step(s):
        @pl.when(at.z - s >= 0)
        def _():
            o = at.t - 2 * s
            across(o).wait_recv()
            pl.when(at.z < nz - 1)(lambda: right(o).start())
            across(o).start()

        @pl.when(at.z + s < nz)
        def _():
            o = at.t + 2 * s
            across(o).wait_recv()
            pl.when(at.z > 0)(lambda: left(o).start())
            across(o).start()

    for g in gathers[:2]:
        g.forward()
    line_step(1)
    for g in gathers[2:]:
        g.forward()
    for s in range(2, nz):
        line_step(s)
    for cp in own_loads[1:]:
        cp.wait()
    for g in gathers:
        g.finish()
    for zz in range(nz):
        across(2 * zz + (1 - at.c)).wait_recv()

    def swap(d, slot):
        return remote(psend.at[slot], precv.at[d], ps.at[slot], pr.at[d], at.dp, at.sibling())

    def push_right(d):
        return remote(pown.at[d], zrecv.at[d], zs.at[d], zr.at[d], at.dp, at.t + 2)

    def push_left(d):
        slot = jnp.where(d == at.z - 1, nz, d)
        return remote(pown.at[d], zrecv.at[slot], zs.at[d], zr.at[slot], at.dp, at.t - 2)

    def came(slot):
        remote(pown.at[0], zrecv.at[slot], zs.at[0], zr.at[slot], at.dp, at.sibling()).wait_recv()

    is_end = (at.z == 0) | (at.z == nz - 1)

    def tile(tt, put):
        r = rows(tt)
        x = xall[r, :]
        gate = dot_nn(x, wgu[0])
        up = dot_nn(x, wgu[1])
        dmid = dot_nt(dyv[r, dcols(0)], wd[0])
        for o in range(1, nd):
            dmid = dmid + dot_nt(dyv[r, pl.ds(o * Dd, Dd)], wd[o])
        sig = 1.0 / (1.0 + jnp.exp(-gate))
        silu = gate * sig
        mid[r, :] = (silu * up).astype(LOW)
        du[r, :] = (dmid * silu).astype(LOW)
        dg[r, :] = (dmid * up * (sig * (1.0 + gate * (1.0 - sig)))).astype(LOW)
        put((dot_nt(dg[r, :], wgu[0]) + dot_nt(du[r, :], wgu[1])).astype(LOW))

    def chain(k):
        d = far_first(k, at.z, nz)
        swap(d, 0).wait_recv()

        @pl.when(is_end)
        def _():
            pown[d] = (pown[d].astype(F32) + precv[d].astype(F32)).astype(LOW)

        @pl.when(jnp.logical_not(is_end))
        def _():
            came(d)
            pown[d] = (pown[d].astype(F32) + precv[d].astype(F32) + zrecv[d].astype(F32)).astype(LOW)

        pl.when(d > at.z)(lambda: push_right(d).start())
        pl.when(d < at.z)(lambda: push_left(d).start())

    def half(i, _):
        k, own = i // 2, lax.rem(i, 2)
        d = far_first(k, at.z, nz)
        slot = lax.rem(k, 2)
        pl.when((own == 0) & (k >= 2))(lambda: swap(d, slot).wait_send())

        def put(v):
            @pl.when(own == 0)
            def _():
                psend[slot] = v
                swap(d, slot).start()

            @pl.when(own == 1)
            def _():
                pown[d] = v

        tile(2 * d + jnp.where(own == 0, 1 - at.c, at.c), put)
        late = jnp.where(is_end, k, k - 2)
        pl.when((own == 1) & (late >= 0) & (late < nz - 1))(lambda: chain(late))
        return 0

    lax.fori_loop(0, 2 * nz, half, 0)
    for k in range(max(0, nz - 2), nz):
        swap(0, k % 2).wait_send()

    W = min(256, D)

    def out_copy(slot, dst):
        return pltpu.make_async_copy(stage.at[slot], dst, osem.at[slot])

    def wtile(i, g):
        slot = lax.rem(i, 2)
        cols = pl.ds(pl.multiple_of(i * W, W), W)
        pl.when(i >= 2)(lambda: out_copy(slot, dwgu_out.at[g, cols]).wait())
        stage[slot] = dot_tn(xall[:, cols], (dg if g == 0 else du)[...]).astype(LOW)
        out_copy(slot, dwgu_out.at[g, cols]).start()

    def wgrad(g):
        n = D // W
        lax.fori_loop(0, n, lambda i, _: (wtile(i, g), 0)[1], 0)
        for s in range(2):
            out_copy(s, dwgu_out.at[g, pl.ds(0, W)]).wait()

    def dwd_copy(o):
        return pltpu.make_async_copy(wd.at[o], dwd_out.at[o], wsem.at[o])

    def otile(i, _):
        slot = lax.rem(i, 2)
        r = rows(i)
        pl.when(i >= 2)(lambda: pltpu.make_async_copy(psend.at[slot], out_out.at[r], osem.at[slot]).wait())

        def part(o, _):
            psend[slot, :, dcols(o)] = dot_nn(mid[r, :], wd[o]).astype(LOW)
            return 0

        lax.fori_loop(0, nd, part, 0)
        pltpu.make_async_copy(psend.at[slot], out_out.at[r], osem.at[slot]).start()
        return 0

    wgrad(0)
    if nz >= 2:
        pl.when(jnp.logical_not(is_end))(lambda: chain(jnp.int32(nz - 2)))
    wgrad(1)
    lax.fori_loop(0, nt, otile, 0)
    for s in range(2):
        pltpu.make_async_copy(psend.at[s], out_out.at[rows(0)], osem.at[s]).wait()
    for g in gathers:
        g.drain()
    def dtile(o, _):
        wd[o] = dot_tn(mid[...], dyv[:, dcols(o)]).astype(LOW)
        dwd_copy(o).start()
        return 0

    lax.fori_loop(0, nd, dtile, 0)
    for o in range(nd):
        dwd_copy(o).wait()

    swap(at.z, 0).wait_recv()
    dxn_out[...] = pown[at.z].astype(F32) + precv[at.z].astype(F32)

    @pl.when(at.z > 0)
    def _():
        came(at.z)
        dxn_out[...] = dxn_out[...] + zrecv[at.z].astype(F32)

    @pl.when(at.z < nz - 1)
    def _():
        came(nz)
        dxn_out[...] = dxn_out[...] + zrecv[nz].astype(F32)

    for zz in range(nz):
        @pl.when(zz != at.z)
        def _(zz=zz):
            remote(pown.at[zz], zrecv.at[zz], zs.at[zz], zr.at[zz], at.dp, at.sibling()).wait_send()
    for zz in range(nz):
        o = 2 * zz + at.c
        across(o).wait_send()
        pl.when((at.z < nz - 1) & (zz <= at.z))(lambda o=o: right(o).wait_send())
        pl.when((at.z > 0) & (zz >= at.z))(lambda o=o: left(o).wait_send())


def mlp(nd, nt, xn, dy_all, wgu, wd):
    R, D = xn.shape
    S = dy_all.shape[0]
    Dd, F = wgu.shape[1:]
    nz = nt // 2
    ny = nd // 2
    dma = lambda *s: pltpu.SemaphoreType.DMA(s)
    hbm = pl.BlockSpec(memory_space=pltpu.HBM)
    vm = pl.BlockSpec(memory_space=pltpu.VMEM)
    return pl.pallas_call(
        functools.partial(mlp_kernel, nd, nt),
        out_shape=(
            jax.ShapeDtypeStruct((R, D), F32),
            jax.ShapeDtypeStruct((2, D, F), LOW),
            jax.ShapeDtypeStruct((nd, F, Dd), LOW),
            jax.ShapeDtypeStruct((S, D), LOW),
        ),
        in_specs=[hbm] * 4,
        out_specs=(vm, hbm, hbm, hbm),
        scratch_shapes=[
            pltpu.VMEM((S, D), LOW), pltpu.VMEM((S, D), LOW), pltpu.VMEM((2, D, F), LOW), pltpu.VMEM((nd, F, Dd), LOW),
            pltpu.VMEM((S, F), LOW), pltpu.VMEM((S, F), LOW), pltpu.VMEM((S, F), LOW),
            pltpu.VMEM((2, R, D), LOW), pltpu.VMEM((nz, R, D), LOW), pltpu.VMEM((nz, R, D), LOW), pltpu.VMEM((nz + 1, R, D), LOW),
            pltpu.VMEM((2, min(256, D), F), LOW),
            dma(4), dma(4), dma(4, ny - 1), dma(4, ny - 1), dma(4, ny - 1), dma(4, nd),
            dma(nt), dma(nt), dma(nt), dma(nt), dma(2), dma(nz), dma(nz), dma(nz + 1), dma(2), dma(nd),
        ],
        compiler_params=pltpu.CompilerParams(collective_id=1, has_side_effects=True, vmem_limit_bytes=63 << 20),
        cost_estimate=pl.CostEstimate(flops=12 * S * D * F, bytes_accessed=40 << 20, transcendentals=S * F),
        name="mlp",
    )(xn, dy_all, wgu, wd)


def rms_normed(field, gain_row):
    return field * lax.rsqrt(jnp.mean(field * field, axis=-1, keepdims=True) + EPSILON) * gain_row


def doc_layout(doc_lengths, length):
    endings = jnp.cumsum(doc_lengths)
    beginnings = endings - doc_lengths
    places = jnp.arange(length, dtype=jnp.int32)
    segment = jnp.sum((places[:, None] >= endings[None, :]).astype(jnp.int32), axis=1)
    picked = segment[:, None] == jnp.arange(doc_lengths.shape[0], dtype=jnp.int32)[None, :]
    position = places - jnp.sum(jnp.where(picked, beginnings[None, :], 0), axis=1)
    return (segment, position)


def rotary_tables(position):
    half_size = HD // 2
    frequency = jnp.exp(
        jnp.arange(half_size, dtype=jnp.float32) * (-2.0 * math.log(ROPE_BASE) / HD)
    )
    angles = position.astype(jnp.float32)[:, None] * frequency[None, :]
    return (jnp.cos(angles), jnp.sin(angles))


def rotate(field, cosine, sine):
    half_size = field.shape[-1] // 2
    front_part = field[..., :half_size]
    back_part = field[..., half_size:]
    return jnp.concatenate(
        [front_part * cosine - back_part * sine, front_part * sine + back_part * cosine], axis=-1
    )


def visible(begin_row, block_size, segment):
    length = segment.shape[0]
    query_places = begin_row + jnp.arange(block_size, dtype=jnp.int32)
    key_places = jnp.arange(length, dtype=jnp.int32)
    query_segment = lax.dynamic_slice_in_dim(segment, begin_row, block_size)
    return (query_segment[:, None] == segment[None, :]) & (
        key_places[None, :] <= query_places[:, None]
    )


def inner_rows(left_side, right_side):
    return lax.dot_general(
        left_side, right_side, (((0,), (0,)), ((), ())), preferred_element_type=jnp.float32
    )


def outer_cols(left_side, right_side):
    return lax.dot_general(
        left_side, right_side, (((1,), (1,)), ((), ())), preferred_element_type=jnp.float32
    )


def advance(grad_raw, weight, moment, average, factor, rate):
    average_decay = min(AVERAGE_TOP, (1.0 + STEP) / (10.0 + STEP))
    clipped = grad_raw * factor
    moment_new = MOMENTUM * moment + clipped
    weight_new = weight - rate * (clipped + MOMENTUM * moment_new)
    average_new = average_decay * average + (1.0 - average_decay) * weight_new
    return (clipped, moment_new, average_new, weight_new, weight_new.astype(jnp.bfloat16))


def local(
    tokens,
    cotangent,
    kv_later,
    lengths,
    query_weight,
    query_moment,
    query_average,
    keyvalue_weight,
    keyvalue_moment,
    keyvalue_average,
    output_weight,
    output_moment,
    output_average,
    gateup_weight,
    gateup_moment,
    gateup_average,
    down_weight,
    down_moment,
    down_average,
    norm_gains,
    gains_moment,
    gains_average,
):
    masters = (query_weight, keyvalue_weight, output_weight, gateup_weight, down_weight, norm_gains)
    lowered = tuple((weight.astype(jnp.bfloat16) for weight in masters))
    full_query, full_kv, full_output, full_gains = (
        lax.all_gather(lowered[0], "dp", axis=0, tiled=True),
        lax.all_gather(lowered[1], "dp", axis=0, tiled=True),
        lax.all_gather(lowered[2], "dp", axis=1, tiled=True),
        lax.all_gather(lowered[5], "dp", axis=1, tiled=True),
    )
    gain_rows = full_gains.astype(jnp.float32)
    row_count = tokens.shape[0]
    seq_len = row_count * lax.axis_size("tensor")
    own_begin = lax.axis_index("tensor") * row_count
    head_count = full_query.shape[1] // HD
    block_size = min(512, seq_len)
    block_count = seq_len // block_size
    scale_factor = 1.0 / math.sqrt(HD)
    segment, position = doc_layout(lengths[0], seq_len)
    cosine, sine = rotary_tables(position)
    own_cosine = lax.dynamic_slice_in_dim(cosine, own_begin, row_count, 0)
    own_sine = lax.dynamic_slice_in_dim(sine, own_begin, row_count, 0)
    own_tokens = tokens.astype(jnp.float32)
    normed_one = rms_normed(own_tokens, gain_rows[0]).astype(jnp.bfloat16)
    normed_all = lax.all_gather(normed_one, "tensor", axis=0, tiled=True)
    query_pre = jnp.dot(normed_all, full_query, preferred_element_type=jnp.float32)
    kv_pre = jnp.dot(normed_all, full_kv, preferred_element_type=jnp.float32)
    queries = rotate(
        query_pre.reshape(seq_len, head_count, HD).transpose(1, 0, 2), cosine, sine
    ).astype(jnp.bfloat16)
    keys_low = rotate(kv_pre[:, :HD], cosine, sine).astype(jnp.bfloat16)
    values_low = kv_pre[:, HD:].astype(jnp.bfloat16)
    query_blocks = queries.reshape(head_count, block_count, block_size, HD).transpose(1, 0, 2, 3)
    starts = jnp.arange(block_count, dtype=jnp.int32) * block_size

    def block_scores(query_block, begin_row):
        scores = (
            jnp.einsum("hqd,kd->hqk", query_block, keys_low, preferred_element_type=jnp.float32)
            * scale_factor
        )
        return jnp.where(visible(begin_row, block_size, segment)[None], scores, MASKED)

    def forward_block(block_item):
        query_block, begin_row = block_item
        scores = block_scores(query_block, begin_row)
        row_max = jnp.max(scores, axis=-1, keepdims=True)
        log_total = row_max + jnp.log(jnp.sum(jnp.exp(scores - row_max), axis=-1, keepdims=True))
        attn_probs = jnp.exp(scores - log_total)
        mixed_block = jnp.einsum(
            "hqk,kd->hqd",
            attn_probs.astype(jnp.bfloat16),
            values_low,
            preferred_element_type=jnp.float32,
        ).astype(jnp.bfloat16)
        result = (mixed_block, log_total)
        return result

    attended, saved = lax.map(forward_block, (query_blocks, starts))
    attn_rows = attended.transpose(0, 2, 1, 3).reshape(seq_len, head_count * HD)
    hidden_one = own_tokens + lax.psum_scatter(
        jnp.dot(attn_rows, full_output, preferred_element_type=jnp.float32).astype(jnp.bfloat16),
        "tensor",
        scatter_dimension=0,
        tiled=True,
    ).astype(jnp.float32)
    normed_two = rms_normed(hidden_one, gain_rows[1]).astype(jnp.bfloat16)
    grad_rows = lax.all_gather(cotangent, "tensor", axis=0, tiled=True)
    nd, nt = lax.axis_size("dp"), lax.axis_size("tensor")
    grad_normed_two, part_gateup, part_down, mlp_rows = mlp(
        nd, nt, normed_two, grad_rows, lowered[3], lowered[4]
    )
    mixed = hidden_one + lax.psum_scatter(
        mlp_rows, "tensor", scatter_dimension=0, tiled=True
    ).astype(jnp.float32)
    _, second_pull = jax.vjp(rms_normed, hidden_one, gain_rows[1])
    grad_hidden_norm, gain_grad_two = second_pull(grad_normed_two)
    grad_hidden = cotangent.astype(jnp.float32) + grad_hidden_norm
    grad_branch = lax.all_gather(grad_hidden.astype(jnp.bfloat16), "tensor", axis=0, tiled=True)
    grad_output = inner_rows(attn_rows, grad_branch)
    grad_attended = outer_cols(grad_branch, full_output).astype(jnp.bfloat16)
    grad_blocks = grad_attended.reshape(block_count, block_size, head_count, HD).transpose(
        0, 2, 1, 3
    )

    def backward_block(running, block_item):
        key_grad, value_grad = running
        query_block, grad_block, saved_item, begin_row = block_item
        attn_probs = jnp.exp(block_scores(query_block, begin_row) - saved_item)
        value_grad = value_grad + jnp.einsum(
            "hqk,hqd->kd",
            attn_probs.astype(jnp.bfloat16),
            grad_block,
            preferred_element_type=jnp.float32,
        )
        prob_grad = jnp.einsum(
            "hqd,kd->hqk", grad_block, values_low, preferred_element_type=jnp.float32
        )
        score_grad = (
            attn_probs * (prob_grad - jnp.sum(prob_grad * attn_probs, axis=-1, keepdims=True))
        ).astype(jnp.bfloat16)
        query_grad = (
            jnp.einsum("hqk,kd->hqd", score_grad, keys_low, preferred_element_type=jnp.float32)
            * scale_factor
        )
        key_grad = (
            key_grad
            + jnp.einsum("hqk,hqd->kd", score_grad, query_block, preferred_element_type=jnp.float32)
            * scale_factor
        )
        return ((key_grad, value_grad), query_grad)

    zero_rows = jnp.zeros((seq_len, HD), jnp.float32)
    (key_grad, value_grad), query_grads = lax.scan(
        backward_block, (zero_rows, zero_rows), (query_blocks, grad_blocks, saved, starts)
    )
    query_grads = query_grads.transpose(1, 0, 2, 3).reshape(head_count, seq_len, HD)
    grad_query_pre = (
        rotate(query_grads, cosine, -sine)
        .transpose(1, 0, 2)
        .reshape(seq_len, head_count * HD)
        .astype(jnp.bfloat16)
    )
    grad_query = inner_rows(normed_all, grad_query_pre)
    normed_part = outer_cols(grad_query_pre, full_query)
    summed_normed, summed_keys, summed_values = (
        lax.psum_scatter(
            normed_part.astype(jnp.bfloat16), "tensor", scatter_dimension=0, tiled=True
        ).astype(jnp.float32),
        lax.psum_scatter(
            key_grad.astype(jnp.bfloat16), "tensor", scatter_dimension=0, tiled=True
        ).astype(jnp.float32),
        lax.psum_scatter(
            value_grad.astype(jnp.bfloat16), "tensor", scatter_dimension=0, tiled=True
        ).astype(jnp.float32),
    )
    later_rows = kv_later.astype(jnp.float32)
    key_total = summed_keys + later_rows[:, :HD]
    value_total = summed_values + later_rows[:, HD:]
    grad_kv_pre = jnp.concatenate(
        [rotate(key_total, own_cosine, -own_sine), value_total], axis=-1
    ).astype(jnp.bfloat16)
    grad_normed_one = summed_normed + outer_cols(grad_kv_pre, full_kv)
    grad_keyvalue_part = inner_rows(normed_one, grad_kv_pre)
    _, first_pull = jax.vjp(rms_normed, own_tokens, gain_rows[0])
    grad_token_norm, gain_grad_one = first_pull(grad_normed_one)
    tokens_grad = grad_hidden + grad_token_norm
    kv_total, gains_total = lax.psum(
        (grad_keyvalue_part, jnp.stack([gain_grad_one, gain_grad_two])), ("dp", "tensor")
    )
    dp_index = lax.axis_index("dp")
    kv_shard = keyvalue_weight.shape[0]
    gains_shard = norm_gains.shape[1]
    grad_keyvalue = lax.dynamic_slice_in_dim(kv_total, dp_index * kv_shard, kv_shard, 0)
    grad_gains = lax.dynamic_slice_in_dim(gains_total, dp_index * gains_shard, gains_shard, 1)
    own_query = lax.psum_scatter(grad_query.astype(LOW), "dp", scatter_dimension=0, tiled=True).astype(F32)
    own_output = lax.psum_scatter(grad_output.astype(LOW), "dp", scatter_dimension=1, tiled=True).astype(F32)
    own_gateup = lax.psum_scatter(part_gateup, "dp", scatter_dimension=1, tiled=True).astype(F32)
    own_down = lax.psum_scatter(part_down, "dp", scatter_dimension=0, tiled=False).astype(F32)
    split_squares = (
        jnp.sum(own_query * own_query)
        + jnp.sum(own_output * own_output)
        + jnp.sum(own_gateup * own_gateup)
        + jnp.sum(own_down * own_down)
    )
    shared_squares = jnp.sum(grad_keyvalue * grad_keyvalue) + jnp.sum(grad_gains * grad_gains)
    local_squares = split_squares + shared_squares / lax.axis_size("tensor")
    grad_norm = jnp.sqrt(lax.psum(local_squares, ("dp", "tensor")))
    factor = jnp.minimum(1.0, CLIP / (grad_norm + 1e-06))
    query_set = advance(
        own_query, query_weight, query_moment, query_average, factor, LEARNING_RATES[0]
    )
    keyvalue_set = advance(
        grad_keyvalue, keyvalue_weight, keyvalue_moment, keyvalue_average, factor, LEARNING_RATES[1]
    )
    output_set = advance(
        own_output, output_weight, output_moment, output_average, factor, LEARNING_RATES[2]
    )
    gateup_set = advance(
        own_gateup, gateup_weight, gateup_moment, gateup_average, factor, LEARNING_RATES[3]
    )
    down_set = advance(own_down, down_weight, down_moment, down_average, factor, LEARNING_RATES[4])
    gains_set = advance(
        grad_gains, norm_gains, gains_moment, gains_average, factor, LEARNING_RATES[5]
    )
    return (
        mixed,
        mixed.astype(jnp.bfloat16),
        tokens_grad,
        grad_norm,
        query_set[0],
        query_set[1],
        query_set[2],
        query_set[3],
        query_set[4],
        keyvalue_set[0],
        keyvalue_set[1],
        keyvalue_set[2],
        keyvalue_set[3],
        keyvalue_set[4],
        output_set[0],
        output_set[1],
        output_set[2],
        output_set[3],
        output_set[4],
        gateup_set[0],
        gateup_set[1],
        gateup_set[2],
        gateup_set[3],
        gateup_set[4],
        down_set[0],
        down_set[1],
        down_set[2],
        down_set[3],
        down_set[4],
        gains_set[0],
        gains_set[1],
        gains_set[2],
        gains_set[3],
        gains_set[4],
    )


def solution(mesh):
    return jax.shard_map(
        local,
        mesh=mesh,
        in_specs=(
            P(("dp", "tensor"), None),
            P(("dp", "tensor"), None),
            P(("dp", "tensor"), None),
            P("dp", None),
            P("dp", "tensor"),
            P("dp", "tensor"),
            P("dp", "tensor"),
            P("dp", None),
            P("dp", None),
            P("dp", None),
            P("tensor", "dp"),
            P("tensor", "dp"),
            P("tensor", "dp"),
            P(None, "dp", "tensor"),
            P(None, "dp", "tensor"),
            P(None, "dp", "tensor"),
            P("tensor", "dp"),
            P("tensor", "dp"),
            P("tensor", "dp"),
            P(None, "dp"),
            P(None, "dp"),
            P(None, "dp"),
        ),
        out_specs=(
            P(("dp", "tensor"), None),
            P(("dp", "tensor"), None),
            P(("dp", "tensor"), None),
            P(),
            P("dp", "tensor"),
            P("dp", "tensor"),
            P("dp", "tensor"),
            P("dp", "tensor"),
            P("dp", "tensor"),
            P("dp", None),
            P("dp", None),
            P("dp", None),
            P("dp", None),
            P("dp", None),
            P("tensor", "dp"),
            P("tensor", "dp"),
            P("tensor", "dp"),
            P("tensor", "dp"),
            P("tensor", "dp"),
            P(None, "dp", "tensor"),
            P(None, "dp", "tensor"),
            P(None, "dp", "tensor"),
            P(None, "dp", "tensor"),
            P(None, "dp", "tensor"),
            P("tensor", "dp"),
            P("tensor", "dp"),
            P("tensor", "dp"),
            P("tensor", "dp"),
            P("tensor", "dp"),
            P(None, "dp"),
            P(None, "dp"),
            P(None, "dp"),
            P(None, "dp"),
            P(None, "dp"),
        ),
        check_vma=False,
    )
```

```python
import functools
import math

import jax
import jax.numpy as jnp
from jax import lax
from jax.experimental import pallas as pl
from jax.experimental.pallas import tpu as pltpu
from jax.sharding import PartitionSpec as P

HD = 128
STEP = 10


EPSILON = 1e-05
MASKED = -1000000000.0
CLIP = 1.0
MOMENTUM = 0.9
LEARNING_RATES = (12.0, 12.0, 480.0, 48.0, 12.0, 960.0)
AVERAGE_TOP = 0.999
ROPE_BASE = 10000.0
MESH = pl.DeviceIdType.MESH
LOW = jnp.bfloat16
F32 = jnp.float32


def dot_nn(a, b):
    return jnp.dot(a, b, preferred_element_type=F32)


def dot_nt(a, b):
    return lax.dot_general(a, b, (((1,), (1,)), ((), ())), preferred_element_type=F32)


def dot_tn(a, b):
    return lax.dot_general(a, b, (((0,), (0,)), ((), ())), preferred_element_type=F32)


class Place:
    def __init__(self, nd, nt):
        self.nd, self.nt = nd, nt
        self.nx = 2 if nd % 2 == 0 else 1
        self.ny = nd // self.nx
        self.nz = nt // 2
        self.dp = lax.axis_index("dp")
        self.t = lax.axis_index("tensor")
        self.y = self.dp // self.nx
        self.x = lax.rem(self.dp, self.nx)
        self.z = self.t // 2
        self.c = lax.rem(self.t, 2)

    def x_peer(self):
        return self.y * self.nx + (1 - self.x)

    def y_peer(self, step):
        return lax.rem(self.y + step, self.ny) * self.nx + self.x

    def xy_peer(self, step):
        return lax.rem(self.y + step, self.ny) * self.nx + (1 - self.x)

    def sibling(self):
        return self.z * 2 + (1 - self.c)


def remote(src, dst, send, recv, dp, t):
    return pltpu.make_async_remote_copy(src, dst, send, recv, device_id=(dp, t), device_id_type=MESH)


def greet(at, dps=True, zs=True, core=True):
    bar = pltpu.get_barrier_semaphore()
    count = 0
    targets = []
    if dps:
        targets.append((at.x_peer(), at.t))
        targets += [(at.y_peer(s), at.t) for s in range(1, at.ny)]
    if core:
        targets.append((at.dp, at.sibling()))
    for target in targets:
        pl.semaphore_signal(bar, inc=1, device_id=target, device_id_type=MESH)
        count += 1
    if zs:
        @pl.when(at.z > 0)
        def _():
            pl.semaphore_signal(bar, inc=1, device_id=(at.dp, at.t - 2), device_id_type=MESH)

        @pl.when(at.z < at.nz - 1)
        def _():
            pl.semaphore_signal(bar, inc=1, device_id=(at.dp, at.t + 2), device_id_type=MESH)

        count = count + (at.z > 0).astype(jnp.int32) + (at.z < at.nz - 1).astype(jnp.int32)
    pl.semaphore_wait(bar, count)


def far_first(k, z, nz):
    j = nz - 1 - k
    m = jnp.minimum(z, nz - 1 - z)
    s = (j + 1) // 2
    two = jnp.where(lax.rem(j, 2) == 1, z - s, z + s)
    one = jnp.where(z < nz - 1 - z, j, nz - 1 - j)
    return jnp.where(j <= 2 * m, two, one)


class Gather:
    def __init__(self, at, src, dst, xs, ys, xf, yf, recv, kind):
        self.at, self.src, self.dst, self.kind = at, src, dst, kind
        self.xs, self.ys, self.xf, self.yf, self.recv = xs, ys, xf, yf, recv

    def own(self):
        at = self.at
        out = [remote(self.src, self.dst(at.dp), self.xs, self.recv.at[at.dp], at.x_peer(), at.t)]
        for s in range(1, at.ny):
            out.append(remote(self.src, self.dst(at.dp), self.ys.at[s - 1], self.recv.at[at.dp], at.y_peer(s), at.t))
        return out

    def passed(self):
        at = self.at
        out = []
        for s in range(1, at.ny):
            if self.kind == 0:
                o = at.x_peer()
                out.append(remote(self.dst(o), self.dst(o), self.yf.at[s - 1], self.recv.at[o], at.y_peer(s), at.t))
            else:
                o = at.y_peer(s)
                out.append(remote(self.dst(o), self.dst(o), self.xf.at[s - 1], self.recv.at[o], at.x_peer(), at.t))
        return out

    def arrived(self, o):
        remote(self.src, self.dst(o), self.xs, self.recv.at[o], self.at.x_peer(), self.at.t).wait_recv()

    def start(self):
        for cp in self.own():
            cp.start()

    def forward(self):
        at = self.at
        if self.kind == 0:
            self.arrived(at.x_peer())
        else:
            for s in range(1, at.ny):
                self.arrived(at.y_peer(s))
        for cp in self.passed():
            cp.start()

    def finish(self):
        at = self.at
        if self.kind == 0:
            for s in range(1, at.ny):
                self.arrived(at.y_peer(s))
        else:
            self.arrived(at.x_peer())
        for s in range(1, at.ny):
            self.arrived(at.xy_peer(s))

    def either(self, name):
        kind = self.kind
        for value in range(2):
            self.kind = value
            pl.when(kind == value)(getattr(self, name))
        self.kind = kind

    def finish_any(self):
        self.either("finish")

    def forward_any(self):
        self.either("forward")

    def drain_any(self):
        self.either("drain")

    def drain(self):
        for cp in self.own() + self.passed():
            cp.wait_send()


def mlp_kernel(nd, nt, xn_in, dy_in, wgu_in, wd_in,
               dxn_out, mine_g, land_g, mine_u, land_u, mine_d, land_d, mine_e, land_e, out_out,
               xall, dyv, wgu, wd, mid, dg, du, psend, pown, precv, zrecv,
               lsem, wx, wy, wxf, wyf, wr, ar, ac, asr, asl, ps, pr, zs, zr, osem, p1l, p1s, p1r):
    at = Place(nd, nt)
    nz = at.nz
    R, D = xn_in.shape
    Dd = wgu_in.shape[1]
    F = wgu_in.shape[2]
    Fh = F // 2
    rows = lambda t: pl.ds(pl.multiple_of(t * R, R), R)
    dcols = lambda o: pl.ds(pl.multiple_of(o * Dd, Dd), Dd)

    own_loads = [
        pltpu.make_async_copy(xn_in, xall.at[rows(at.t)], lsem.at[0]),
        pltpu.make_async_copy(dy_in, dyv, lsem.at[1]),
        pltpu.make_async_copy(wgu_in, wgu.at[:, dcols(at.dp)], lsem.at[2]),
        pltpu.make_async_copy(wd_in, wd.at[at.dp], lsem.at[3]),
    ]
    for cp in own_loads:
        cp.start()
    greet(at)

    gathers = []
    for p in range(2):
        gathers.append(Gather(at, wgu_in.at[p], lambda o, p=p: wgu.at[p, dcols(o)],
                              wx.at[p], wy.at[p], wxf.at[p], wyf.at[p], wr.at[p], p))
    for p in range(2):
        gathers.append(Gather(at, wd_in.at[pl.ds(p * Fh, Fh)], lambda o, p=p: wd.at[o, pl.ds(p * Fh, Fh)],
                              wx.at[2 + p], wy.at[2 + p], wxf.at[2 + p], wyf.at[2 + p], wr.at[2 + p], p))

    def right(o):
        return remote(xall.at[rows(o)], xall.at[rows(o)], asr.at[o], ar.at[o], at.dp, at.t + 2)

    def left(o):
        return remote(xall.at[rows(o)], xall.at[rows(o)], asl.at[o], ar.at[o], at.dp, at.t - 2)

    def across(o):
        return remote(xall.at[rows(o)], xall.at[rows(o)], ac.at[o], ar.at[o], at.dp, at.sibling())

    own_loads[0].wait()
    across(at.t).start()
    pl.when(at.z < nz - 1)(lambda: right(at.t).start())
    pl.when(at.z > 0)(lambda: left(at.t).start())
    for g in gathers[:2]:
        g.start()
    for g in gathers[2:]:
        g.start()

    def line_step(s):
        @pl.when(at.z - s >= 0)
        def _():
            o = at.t - 2 * s
            across(o).wait_recv()
            pl.when(at.z < nz - 1)(lambda: right(o).start())
            across(o).start()

        @pl.when(at.z + s < nz)
        def _():
            o = at.t + 2 * s
            across(o).wait_recv()
            pl.when(at.z > 0)(lambda: left(o).start())
            across(o).start()

    for g in gathers[:2]:
        g.forward()
    line_step(1)
    for g in gathers[2:]:
        g.forward()
    for s in range(2, nz):
        line_step(s)
    for cp in own_loads[1:]:
        cp.wait()
    for g in gathers:
        g.finish()
    for zz in range(nz):
        across(2 * zz + (1 - at.c)).wait_recv()

    def swap(d, slot):
        return remote(psend.at[slot], precv.at[d], ps.at[slot], pr.at[d], at.dp, at.sibling())

    def push_right(d):
        return remote(pown.at[d], zrecv.at[d], zs.at[d], zr.at[d], at.dp, at.t + 2)

    def push_left(d):
        slot = jnp.where(d == at.z - 1, nz, d)
        return remote(pown.at[d], zrecv.at[slot], zs.at[d], zr.at[slot], at.dp, at.t - 2)

    def came(slot):
        remote(pown.at[0], zrecv.at[slot], zs.at[0], zr.at[slot], at.dp, at.sibling()).wait_recv()

    is_end = (at.z == 0) | (at.z == nz - 1)

    def tile(tt, put):
        r = rows(tt)
        x = xall[r, :]
        gate = dot_nn(x, wgu[0])
        up = dot_nn(x, wgu[1])
        dmid = dot_nt(dyv[r, dcols(0)], wd[0])
        for o in range(1, nd):
            dmid = dmid + dot_nt(dyv[r, pl.ds(o * Dd, Dd)], wd[o])
        sig = 1.0 / (1.0 + jnp.exp(-gate))
        silu = gate * sig
        mid[r, :] = (silu * up).astype(LOW)
        du[r, :] = (dmid * silu).astype(LOW)
        dg[r, :] = (dmid * up * (sig * (1.0 + gate * (1.0 - sig)))).astype(LOW)
        put((dot_nt(dg[r, :], wgu[0]) + dot_nt(du[r, :], wgu[1])).astype(LOW))

    def chain(k):
        d = far_first(k, at.z, nz)
        swap(d, 0).wait_recv()

        @pl.when(is_end)
        def _():
            pown[d] = (pown[d].astype(F32) + precv[d].astype(F32)).astype(LOW)

        @pl.when(jnp.logical_not(is_end))
        def _():
            came(d)
            pown[d] = (pown[d].astype(F32) + precv[d].astype(F32) + zrecv[d].astype(F32)).astype(LOW)

        pl.when(d > at.z)(lambda: push_right(d).start())
        pl.when(d < at.z)(lambda: push_left(d).start())

    def half(i, _):
        k, own = i // 2, lax.rem(i, 2)
        d = far_first(k, at.z, nz)
        slot = lax.rem(k, 2)
        pl.when((own == 0) & (k >= 2))(lambda: swap(d, slot).wait_send())

        def put(v):
            @pl.when(own == 0)
            def _():
                psend[slot] = v
                swap(d, slot).start()

            @pl.when(own == 1)
            def _():
                pown[d] = v

        tile(2 * d + jnp.where(own == 0, 1 - at.c, at.c), put)
        late = jnp.where(is_end, k, k - 2)
        pl.when((own == 1) & (late >= 0) & (late < nz - 1))(lambda: chain(late))
        return 0

    lax.fori_loop(0, 2 * nz, half, 0)
    for k in range(max(0, nz - 2), nz):
        swap(0, k % 2).wait_send()

    for g in gathers:
        g.drain()
    for zz in range(nz):
        o = 2 * zz + at.c
        across(o).wait_send()
        pl.when((at.z < nz - 1) & (zz <= at.z))(lambda o=o: right(o).wait_send())
        pl.when((at.z > 0) & (zz >= at.z))(lambda o=o: left(o).wait_send())

    W = min(256, Dd)
    nx, ny = at.nx, at.ny

    def hop(n, src, o, mine, land):
        yy, xx = o // nx, lax.rem(o, nx)
        if n % 2 == 0:
            step = lax.rem(yy - at.y + ny, ny)
            slot = (step - 1) * nx + xx
            stays, place, peer = yy == at.y, xx, yy * nx + at.x
        else:
            slot, stays, place, peer = yy, xx == at.x, yy, at.y * nx + xx
        local = pltpu.make_async_copy(src, mine.at[place], p1l.at[n, place])
        slot = jnp.where(stays, 0, slot)
        away = remote(src, land.at[slot], p1s.at[n, slot], p1r.at[n, slot], jnp.where(stays, at.x_peer(), peer), at.t)
        return stays, local, away

    def order(n, i):
        if n % 2 == 0:
            return lax.rem(at.y + 1 + i // nx, ny) * nx + lax.rem(i, nx)
        return lax.rem(i, ny) * nx + jnp.where(i < ny, 1 - at.x, at.x)

    def send(n, src, o, mine, land):
        stays, local, away = hop(n, src, o, mine, land)
        pl.when(stays)(lambda: local.start())
        pl.when(jnp.logical_not(stays))(lambda: away.start())

    def settle(n, src, mine, land):
        for i in range(nd):
            stays, local, away = hop(n, src, order(n, i), mine, land)

            @pl.when(stays)
            def _():
                local.wait()

            @pl.when(jnp.logical_not(stays))
            def _():
                away.wait_send()
                away.wait_recv()

    def wgrad(n, mine, land):
        def block(i, _):
            o = order(n, i)

            def wtile(w, _):
                cols = pl.ds(pl.multiple_of(o * Dd + w * W, W), W)
                wgu[n, cols, :] = dot_tn(xall[:, cols], (du if n else dg)[...]).astype(LOW)
                return 0

            lax.fori_loop(0, Dd // W, wtile, 0)
            send(n, wgu.at[n, dcols(o)], o, mine, land)
            return 0

        lax.fori_loop(0, nd, block, 0)

    def dgrad(n, mine, land):
        half = pl.ds((n - 2) * Fh, Fh)

        def block(i, _):
            o = order(n, i)
            if n == 2:
                xall[pl.ds(0, F), dcols(o)] = dot_tn(mid[...], dyv[:, dcols(o)]).astype(LOW)
            send(n, xall.at[half, dcols(o)], o, mine, land)
            return 0

        lax.fori_loop(0, nd, block, 0)

    def otile(i, _):
        slot = lax.rem(i, 2)
        r = rows(i)
        pl.when(i >= 2)(lambda: pltpu.make_async_copy(psend.at[slot], out_out.at[r], osem.at[slot]).wait())

        def part(o, _):
            psend[slot, :, dcols(o)] = dot_nn(mid[r, :], wd[o]).astype(LOW)
            return 0

        lax.fori_loop(0, nd, part, 0)
        pltpu.make_async_copy(psend.at[slot], out_out.at[r], osem.at[slot]).start()
        return 0

    wgrad(0, mine_g, land_g)
    if nz >= 2:
        pl.when(jnp.logical_not(is_end))(lambda: chain(jnp.int32(nz - 2)))
    wgrad(1, mine_u, land_u)
    dgrad(2, mine_d, land_d)
    dgrad(3, mine_e, land_e)
    lax.fori_loop(0, nt, otile, 0)
    for s in range(2):
        pltpu.make_async_copy(psend.at[s], out_out.at[rows(0)], osem.at[s]).wait()

    swap(at.z, 0).wait_recv()
    dxn_out[...] = pown[at.z].astype(F32) + precv[at.z].astype(F32)

    @pl.when(at.z > 0)
    def _():
        came(at.z)
        dxn_out[...] = dxn_out[...] + zrecv[at.z].astype(F32)

    @pl.when(at.z < nz - 1)
    def _():
        came(nz)
        dxn_out[...] = dxn_out[...] + zrecv[nz].astype(F32)

    for zz in range(nz):
        @pl.when(zz != at.z)
        def _(zz=zz):
            remote(pown.at[zz], zrecv.at[zz], zs.at[zz], zr.at[zz], at.dp, at.sibling()).wait_send()
    settle(0, wgu.at[0, dcols(0)], mine_g, land_g)
    settle(1, wgu.at[1, dcols(0)], mine_u, land_u)
    settle(2, xall.at[pl.ds(0, Fh), dcols(0)], mine_d, land_d)
    settle(3, xall.at[pl.ds(0, Fh), dcols(0)], mine_e, land_e)


def mlp(nd, nt, xn, dy_all, wgu, wd):
    R, D = xn.shape
    S = dy_all.shape[0]
    Dd, F = wgu.shape[1:]
    nz = nt // 2
    ny = nd // 2
    dma = lambda *s: pltpu.SemaphoreType.DMA(s)
    shape = lambda *s: jax.ShapeDtypeStruct(s, LOW)
    Fh = F // 2
    slots = max(2 * (ny - 1), ny)
    hbm = pl.BlockSpec(memory_space=pltpu.HBM)
    vm = pl.BlockSpec(memory_space=pltpu.VMEM)
    return pl.pallas_call(
        functools.partial(mlp_kernel, nd, nt),
        out_shape=(
            jax.ShapeDtypeStruct((R, D), F32),
            shape(2, Dd, F), shape(2 * (ny - 1), Dd, F), shape(ny, Dd, F), shape(ny, Dd, F),
            shape(2, Fh, Dd), shape(2 * (ny - 1), Fh, Dd), shape(ny, Fh, Dd), shape(ny, Fh, Dd),
            shape(S, D),
        ),
        in_specs=[hbm] * 4,
        out_specs=(vm,) + (hbm,) * 9,
        scratch_shapes=[
            pltpu.VMEM((S, D), LOW), pltpu.VMEM((S, D), LOW), pltpu.VMEM((2, D, F), LOW), pltpu.VMEM((nd, F, Dd), LOW),
            pltpu.VMEM((S, F), LOW), pltpu.VMEM((S, F), LOW), pltpu.VMEM((S, F), LOW),
            pltpu.VMEM((2, R, D), LOW), pltpu.VMEM((nz, R, D), LOW), pltpu.VMEM((nz, R, D), LOW), pltpu.VMEM((nz + 1, R, D), LOW),
            dma(4), dma(4), dma(4, ny - 1), dma(4, ny - 1), dma(4, ny - 1), dma(4, nd),
            dma(nt), dma(nt), dma(nt), dma(nt), dma(2), dma(nz), dma(nz), dma(nz + 1), dma(2), dma(4, max(2, ny)), dma(4, slots), dma(4, slots),
        ],
        compiler_params=pltpu.CompilerParams(collective_id=1, has_side_effects=True, vmem_limit_bytes=63 << 20),
        cost_estimate=pl.CostEstimate(flops=12 * S * D * F, bytes_accessed=40 << 20, transcendentals=S * F),
        name="mlp",
    )(xn, dy_all, wgu, wd)


def swap_halves(u):
    h = u.shape[-1] // 2
    return jnp.concatenate([u[:, h:], u[:, :h]], axis=1)


def near_first(k, z, nz):
    return far_first(nz - 1 - k, z, nz)


def greet_all(at):
    bar = pltpu.get_barrier_semaphore()
    for s in range(1, at.nd):
        pl.semaphore_signal(bar, inc=1, device_id=(lax.rem(at.dp + s, at.nd), at.t), device_id_type=MESH)
    for s in range(1, at.nt):
        pl.semaphore_signal(bar, inc=1, device_id=(at.dp, lax.rem(at.t + s, at.nt)), device_id_type=MESH)
    pl.semaphore_wait(bar, at.nd - 1 + at.nt - 1)


class Line:
    def __init__(self, at, view, right, left, recv, across=None):
        self.at, self.view, self.rs, self.ls, self.recv, self.across = at, view, right, left, recv, across

    def right(self, o):
        return remote(self.view(o), self.view(o), self.rs.at[o], self.recv.at[o], self.at.dp, self.at.t + 2)

    def left(self, o):
        return remote(self.view(o), self.view(o), self.ls.at[o], self.recv.at[o], self.at.dp, self.at.t - 2)

    def pass_on(self, o, to_right, to_left):
        at = self.at
        if to_right:
            pl.when(at.z < at.nz - 1)(lambda: self.right(o).start())
        if to_left:
            pl.when(at.z > 0)(lambda: self.left(o).start())
        if self.across is not None:
            self.across(o).start()

    def start(self):
        self.pass_on(self.at.z, True, True)

    def arrived(self, o):
        remote(self.view(o), self.view(o), self.rs.at[o], self.recv.at[o], self.at.dp, self.at.sibling()).wait_recv()

    def step(self, s):
        at = self.at

        @pl.when(at.z - s >= 0)
        def _():
            self.arrived(at.z - s)
            self.pass_on(at.z - s, True, False)

        @pl.when(at.z + s < at.nz)
        def _():
            self.arrived(at.z + s)
            self.pass_on(at.z + s, False, True)

    def drain(self):
        at = self.at
        for o in range(at.nz):
            pl.when((at.z < at.nz - 1) & (o <= at.z))(lambda o=o: self.right(o).wait_send())
            pl.when((at.z > 0) & (o >= at.z))(lambda o=o: self.left(o).wait_send())
            if self.across is not None:
                self.across(o).wait_send()


def attend_kernel(nd, nt, tok, gain, wq_in, wkv_in, wo_in, cosf, sins, lo_in,
                  h1_out, xn2_out, gfull, lse_out,
                  xn1_out, wq_out, wo_out, wkv_out, kv_out, q_out, o_out,
                  xn1, wq, wo, wkv, kvs, qs, os_, pback, precv,
                  lsem, gs, gr, vx, vy, vxf, vyf, vr, qx, qy, qxf, qyf, qr, ox, oy, oxf, oyf, orr,
                  qlr, qll, qlv, olr, oll, olv, klr, kll, klv, klc, klcr, cs, cr, outs):
    at = Place(nd, nt)
    nz = at.nz
    R, D = tok.shape
    Dd, HC = wq_in.shape
    TQ = min(256, 2 * R)
    rows = lambda t: pl.ds(pl.multiple_of(t * R, R), R)
    drows = lambda o: pl.ds(pl.multiple_of(o * Dd, Dd), Dd)
    hcols = lambda j: pl.ds(pl.multiple_of(j * HC, HC), HC)

    loads = [
        pltpu.make_async_copy(wkv_in, wkv.at[drows(at.dp)], lsem.at[0]),
        pltpu.make_async_copy(wq_in, wq.at[at.z, drows(at.dp)], lsem.at[1]),
        pltpu.make_async_copy(wo_in, wo.at[at.dp, hcols(at.z)], lsem.at[2]),
    ]
    for cp in loads:
        cp.start()
    gfull[at.dp] = gain[...]
    greet_all(at)

    def gain_copy(s):
        return remote(gain, gfull.at[at.dp], gs.at[s - 1], gr.at[s - 1], lax.rem(at.dp + s, nd), at.t)

    for s in range(1, nd):
        gain_copy(s).start()
    Dh = Dd // 2
    gkv = [Gather(at, wkv_in.at[pl.ds(p * Dh, Dh)], lambda o, p=p: wkv.at[pl.ds(pl.multiple_of(o * Dd + p * Dh, Dh), Dh)],
                  vx.at[p], vy.at[p], vxf.at[p], vyf.at[p], vr.at[p], p) for p in range(2)]

    def gq(k):
        j = near_first(k, at.z, nz)
        return Gather(at, wq.at[j, drows(at.dp)], lambda o: wq.at[j, drows(o)], qx.at[k], qy.at[k], qxf.at[k], qyf.at[k], qr.at[k], lax.rem(k, 2) if not isinstance(k, int) else k % 2)

    def go(k):
        j = near_first(k, at.z, nz)
        return Gather(at, wo.at[at.dp, hcols(j)], lambda o: wo.at[o, hcols(j)], ox.at[k], oy.at[k], oxf.at[k], oyf.at[k], orr.at[k], lax.rem(k, 2) if not isinstance(k, int) else k % 2)

    lq = Line(at, lambda o: wq.at[o, drows(at.dp)], qlr, qll, qlv)
    lo = Line(at, lambda o: wo.at[at.dp, hcols(o)], olr, oll, olv)

    def kv_view(o):
        return kvs.at[rows(2 * o + at.c)]

    def kv_across(o):
        return remote(kv_view(o), kv_view(o), klc.at[o], klcr.at[o], at.dp, at.sibling())

    lkv = Line(at, kv_view, klr, kll, klv, kv_across)

    for g in gkv:
        g.start()
    loads[1].wait()
    lq.start()
    gq(0).start()

    for s in range(1, nd):
        gain_copy(s).wait_recv()

    def scaled(v, row, write):
        r = lax.rsqrt(jnp.mean(v * v, axis=-1, keepdims=True) + EPSILON)
        for o in range(nd):
            cols = pl.ds(o * Dd, Dd)
            write(cols, (v[:, o * Dd:(o + 1) * Dd] * r * gfull[o, row:row + 1, :]).astype(LOW))

    mine = rows(at.c)

    def put_xn1(cols, v):
        xn1[mine, cols] = v

    scaled(tok[...].astype(F32), 0, put_xn1)
    xn1_across = remote(xn1.at[mine], xn1.at[mine], cs.at[0], cr.at[0], at.dp, at.sibling())
    xn1_across.start()

    for g in gkv:
        g.forward()
    loads[0].wait()
    for g in gkv:
        g.finish()
    kvpre = dot_nn(xn1[mine, :], wkv[...])
    kk = kvpre[:, :HD]
    kvs[rows(at.t), pl.ds(0, HD)] = (kk * cosf[mine, :] + swap_halves(kk) * sins[mine, :]).astype(LOW)
    kvs[rows(at.t), pl.ds(HD, HD)] = kvpre[:, HD:].astype(LOW)
    lkv.start()
    loads[2].wait()
    lo.start()
    for s in range(1, nz):
        lq.step(s)
        gq(s).start()
        gq(s - 1).forward()
        lkv.step(s)
    gq(nz - 1).forward()
    xn1_across.wait_recv()
    go(0).start()
    for s in range(1, nz):
        lo.step(s)
        go(s).start()
    for o in range(nz):
        kv_across(o).wait_recv()

    scale = 1.0 / math.sqrt(HD)
    S = kvs.shape[0]
    lane = lax.broadcasted_iota(jnp.int32, (TQ, 128), 1)

    def pair(k, _):
        j = near_first(k, at.z, nz)
        g = gq(k)
        g.finish_any()
        qpre = dot_nn(xn1[...], wq[j])
        for hh in range(HC // HD):
            u = qpre[:, hh * HD:(hh + 1) * HD]
            qs[:, pl.ds(pl.multiple_of(j * HC + hh * HD, HD), HD)] = (u * cosf[...] + swap_halves(u) * sins[...]).astype(LOW)

        def head(i, _):
            hh, tq = lax.rem(i, HC // HD), i // (HC // HD)
            rr = pl.ds(pl.multiple_of(tq * TQ, TQ), TQ)
            cols = pl.ds(pl.multiple_of(j * HC + hh * HD, HD), HD)
            s = dot_nt(qs[rr, cols], kvs[:, pl.ds(0, HD)])
            place = lax.broadcasted_iota(jnp.int32, (TQ, S), 1)
            here = at.z * 2 * R + tq * TQ + lax.broadcasted_iota(jnp.int32, (TQ, 1), 0)
            s = jnp.where((place >= lo_in[rr, :]) & (place <= here), s * scale, MASKED)
            m = jnp.max(s, axis=-1, keepdims=True)
            p = jnp.exp(s - m)
            total = jnp.sum(p, axis=-1, keepdims=True)
            att = dot_nn(p.astype(LOW), kvs[:, pl.ds(HD, HD)])
            os_[rr, cols] = (att / total).astype(LOW)
            hid = j * (HC // HD) + hh
            lse_out[rr, :] = jnp.where(lane == hid, m + jnp.log(total), lse_out[rr, :])
            return 0

        lax.fori_loop(0, (HC // HD) * (2 * R // TQ), head, 0)
        go(k).forward_any()
        return 0

    lse_out[...] = jnp.zeros_like(lse_out)
    lax.fori_loop(0, nz, pair, 0)
    keep = [
        pltpu.make_async_copy(xn1, xn1_out, outs.at[0]),
        pltpu.make_async_copy(wq, wq_out, outs.at[1]),
        pltpu.make_async_copy(wkv, wkv_out, outs.at[2]),
        pltpu.make_async_copy(kvs, kv_out, outs.at[3]),
        pltpu.make_async_copy(qs, q_out, outs.at[4]),
        pltpu.make_async_copy(os_, o_out, outs.at[5]),
    ]
    for cp in keep:
        cp.start()

    lax.fori_loop(0, nz, lambda k, _: (go(k).finish_any(), 0)[1], 0)
    keep.append(pltpu.make_async_copy(wo, wo_out, outs.at[6]))
    keep[-1].start()
    theirs = rows(1 - at.c)
    for o in range(nd):
        pback[:, pl.ds(o * Dd, Dd)] = dot_nn(os_[theirs, :], wo[o]).astype(LOW)
    back = remote(pback, precv, cs.at[1], cr.at[1], at.dp, at.sibling())
    back.start()
    for o in range(nd):
        cols = pl.ds(o * Dd, Dd)
        h1_out[:, cols] = tok[:, cols].astype(F32) + dot_nn(os_[mine, :], wo[o])
    back.wait_recv()
    h1_out[...] = h1_out[...] + precv[...].astype(F32)

    def put_xn2(cols, v):
        xn2_out[:, cols] = v

    scaled(h1_out[...], 1, put_xn2)

    for s in range(1, nd):
        gain_copy(s).wait_send()
    for g in gkv:
        g.drain()
    xn1_across.wait_send()
    back.wait_send()
    lq.drain()
    lo.drain()
    lkv.drain()

    def drain(k, _):
        gq(k).drain_any()
        go(k).drain_any()
        return 0

    lax.fori_loop(0, nz, drain, 0)
    for cp in keep:
        cp.wait()


def attend(nd, nt, tok, gain, wq, wkv, wo, cosf, sins, lo):
    R, D = tok.shape
    Dd, HC = wq.shape
    S = R * nt
    nz, ny = nt // 2, nd // 2
    dma = lambda *s: pltpu.SemaphoreType.DMA(s)
    hbm = pl.BlockSpec(memory_space=pltpu.HBM)
    vm = pl.BlockSpec(memory_space=pltpu.VMEM)
    shapes = [((R, D), F32), ((R, D), LOW), ((nd, 8, Dd), F32), ((2 * R, 128), F32),
              ((2 * R, D), LOW), ((nz, D, HC), LOW), ((nd, nz * HC, Dd), LOW), ((D, 2 * HD), LOW), ((S, 2 * HD), LOW),
              ((2 * R, nz * HC), LOW), ((2 * R, nz * HC), LOW)]
    yg = lambda n: [dma(n), dma(n, ny - 1), dma(n, ny - 1), dma(n, ny - 1), dma(n, nd)]
    return pl.pallas_call(
        functools.partial(attend_kernel, nd, nt),
        out_shape=tuple(jax.ShapeDtypeStruct(*s) for s in shapes),
        in_specs=[vm, vm, hbm, hbm, hbm, vm, vm, vm],
        out_specs=(vm, vm, vm, vm) + (hbm,) * 7,
        scratch_shapes=[pltpu.VMEM(*s) for s in shapes[4:]] + [pltpu.VMEM((R, D), LOW), pltpu.VMEM((R, D), LOW)]
        + [dma(3), dma(nd - 1), dma(nd - 1)] + yg(2) + yg(nz) + yg(nz)
        + [dma(nz)] * 3 + [dma(nz)] * 3 + [dma(nz)] * 5 + [dma(2), dma(2), dma(7)],
        compiler_params=pltpu.CompilerParams(collective_id=2, has_side_effects=True, vmem_limit_bytes=63 << 20),
        cost_estimate=pl.CostEstimate(flops=20 << 30, bytes_accessed=40 << 20, transcendentals=8 * 512 * 2048),
        name="attend",
    )(tok, gain, wq, wkv, wo, cosf, sins, lo)


class Scatter:
    def __init__(self, at, kind, view, land, land2, ss, rs, ss2, rs2):
        self.at, self.kind, self.view = at, kind, view
        self.land, self.land2 = land, land2
        self.ss, self.rs, self.ss2, self.rs2 = ss, rs, ss2, rs2

    def first(self):
        at = self.at
        out = []
        if self.kind == 0:
            for s in range(1, at.ny):
                for xx in range(at.nx):
                    slot = (s - 1) * at.nx + xx
                    o = lax.rem(at.y + s, at.ny) * at.nx + xx
                    out.append(remote(self.view(o), self.land(slot), self.ss.at[slot], self.rs.at[slot], at.y_peer(s), at.t))
        else:
            for yy in range(at.ny):
                o = yy * at.nx + 1 - at.x
                out.append(remote(self.view(o), self.land(yy), self.ss.at[yy], self.rs.at[yy], at.x_peer(), at.t))
        return out

    def second(self):
        at = self.at
        if self.kind == 0:
            return [remote(self.view(at.x_peer()), self.land2(0), self.ss2.at[0], self.rs2.at[0], at.x_peer(), at.t)]
        return [remote(self.view(at.y_peer(s)), self.land2(s - 1), self.ss2.at[s - 1], self.rs2.at[s - 1], at.y_peer(s), at.t)
                for s in range(1, at.ny)]

    def start(self):
        for cp in self.first():
            cp.start()

    def add(self, o, slots):
        total = self.view(o)[...].astype(F32)
        for slot in slots:
            total = total + self.land(slot)[...].astype(F32)
        self.view(o)[...] = total.astype(LOW)

    def middle(self):
        at = self.at
        for cp in self.first():
            cp.wait_recv()
        if self.kind == 0:
            self.add(at.x_peer(), [(s - 1) * at.nx + 1 - at.x for s in range(1, at.ny)])
        else:
            for s in range(1, at.ny):
                self.add(at.y_peer(s), [lax.rem(at.y + s, at.ny)])
        for cp in self.second():
            cp.start()
        if self.kind == 0:
            self.add(at.dp, [(s - 1) * at.nx + at.x for s in range(1, at.ny)])
        else:
            self.add(at.dp, [at.y])

    def total(self):
        total = self.view(self.at.dp)[...].astype(F32)
        for i, cp in enumerate(self.second()):
            cp.wait_recv()
            total = total + self.land2(i)[...].astype(F32)
        return total

    def drain(self):
        for cp in self.first() + self.second():
            cp.wait_send()

    def either(self, name, put=None):
        kind = self.kind
        for value in range(2):
            self.kind = value
            call = getattr(self, name)
            if put is None:
                pl.when(kind == value)(call)
            else:
                pl.when(kind == value)(lambda call=call: put(call()))
        self.kind = kind


def grads_kernel(nd, nt, dy, tok, gfull, cosf, sins, lo_row, lse, later,
                 h1_in, dxn2_in, xn1_in, wq_in, wo_in, wkv_in, kv_in, q_in, o_in,
                 mine_g, land_g, mine_u, land_u, mine_d, land_d, mine_e, land_e,
                 tgrad, gq_out, go_out, gkv_out, gg_out, norm_out, keep_g, keep_u, keep_d, keep_e, got_g, got_u, got_d, got_e,
                 xn1, wq, wo, wkv, kvs, qs, os_, dos, dh1b, dxn1, lset, dkv, dq,
                 bg, bu, bd, be, lg, lu, ld, le, tg, tu, td, te,
                 ql, ql2, ol, ol2, qz, oz, qlz, olz, kvb, kland, kz, xrecv, wl, wd2, w2, w2l, wfin, gl, gpart, u2, u2l, gfin, share, norms, normd,
                 lsem, xsem, fs, fr, qss, qsr, qss2, qsr2, oss, osr, oss2, osr2, qzs, qzr, ozs, ozr,
                 ks, kr, kzs, kzr, ws, wr, w2s, w2r, w3s, w3r, us, ur, u2s, u2r, u3s, u3r, ns, nr, n2s, n2r, outs):
    at = Place(nd, nt)
    nz, nx, ny = at.nz, at.nx, at.ny
    R, D = tok.shape
    Dd = wo.shape[2]
    HC = wq.shape[2]
    Ds = wl.shape[1]
    NH = HC // HD
    KT = 2 * R
    S = kvs.shape[0]
    rows = lambda t: pl.ds(pl.multiple_of(t * R, R), R)
    drows = lambda o: pl.ds(pl.multiple_of(o * Dd, Dd), Dd)
    hcols = lambda j: pl.ds(pl.multiple_of(j * HC, HC), HC)
    mine, theirs = rows(at.c), rows(1 - at.c)
    scale = 1.0 / math.sqrt(HD)

    pieces = [(bg, mine_g), (bu, mine_u), (bd, mine_d), (be, mine_e), (tg, land_g), (tu, land_u), (td, land_d), (te, land_e),
              (wo, wo_in), (os_, o_in), (qs, q_in), (kvs, kv_in), (xn1, xn1_in), (wq, wq_in), (wkv, wkv_in),
              (dxn1.at[pl.ds(0, R)], h1_in), (dxn1.at[pl.ds(R, R)], dxn2_in)]
    loads = [pltpu.make_async_copy(src, dst, lsem.at[i]) for i, (dst, src) in enumerate(pieces)]
    for cp in loads:
        cp.start()
    greet_all(at)

    def rms_back(v_of, e_of, row, put):
        chunks = [pl.ds(o * Dd, Dd) for o in range(nd)]
        squares = jnp.zeros((R, 1), F32)
        inner = jnp.zeros((R, 1), F32)
        for o, cols in enumerate(chunks):
            v = v_of(cols)
            squares = squares + jnp.sum(v * v, axis=-1, keepdims=True)
            inner = inner + jnp.sum(e_of(cols) * gfull[o, row:row + 1, :] * v, axis=-1, keepdims=True)
        r = lax.rsqrt(squares / D + EPSILON)
        inner = inner * (r * r * r) / D
        for o, cols in enumerate(chunks):
            v, e = v_of(cols), e_of(cols)
            gpart[row:row + 1, cols] = jnp.sum(e * v * r, axis=0, keepdims=True)
            put(cols, r * (e * gfull[o, row:row + 1, :]) - v * inner)

    gpart[...] = jnp.zeros_like(gpart)

    def put_dh1(cols, v):
        total = dy[:, cols].astype(F32) + v
        tgrad[:, cols] = total
        dh1b[mine, cols] = total.astype(LOW)

    loads[15].wait()
    loads[16].wait()
    rms_back(lambda cols: dxn1[pl.ds(0, R), cols], lambda cols: dxn1[pl.ds(R, R), cols], 1, put_dh1)
    swap_dh1 = remote(dh1b.at[mine], dh1b.at[mine], xsem.at[0], xsem.at[1], at.dp, at.sibling())
    swap_dh1.start()

    big = []
    for n, (buf, got, second) in enumerate([(bg, tg, lg), (bu, tu, lu), (bd, td, ld), (be, te, le)]):
        loads[n].wait()
        loads[4 + n].wait()
        if n % 2 == 0:
            keep, keep_slots = at.x, [(s - 1) * nx + at.x for s in range(1, ny)]
            away = [(1 - at.x, [(s - 1) * nx + 1 - at.x for s in range(1, ny)], at.x_peer())]
        else:
            keep, keep_slots = at.y, [at.y]
            away = [(lax.rem(at.y + s, ny), [lax.rem(at.y + s, ny)], at.y_peer(s)) for s in range(1, ny)]
        copies = []
        for i, (place, slots, peer) in enumerate(away):
            total = buf[place].astype(F32)
            for slot in slots:
                total = total + got[slot].astype(F32)
            buf[place] = total.astype(LOW)
            copies.append(remote(buf.at[place], second.at[i], fs.at[n, i], fr.at[n, i], peer, at.t))
            copies[-1].start()
        total = buf[keep].astype(F32)
        for slot in keep_slots:
            total = total + got[slot].astype(F32)
        buf[keep] = total.astype(LOW)
        big.append((buf, keep, second, copies))

    for i in range(8, 15):
        loads[i].wait()
    swap_dh1.wait_recv()
    def do_pair(j, _):
        acc = dot_nt(dh1b[:, pl.ds(0, Dd)], wo[0, hcols(j), :])
        for o in range(1, nd):
            acc = acc + dot_nt(dh1b[:, pl.ds(o * Dd, Dd)], wo[o, hcols(j), :])
        dos[:, hcols(j)] = acc.astype(LOW)
        return 0

    lax.fori_loop(0, nz, do_pair, 0)

    def kind_of(k):
        return k % 2 if isinstance(k, int) else lax.rem(k, 2)

    def so(k):
        j = far_first(k, at.z, nz)
        return Scatter(at, kind_of(k), lambda o: wo.at[o, hcols(j)], lambda i: ol.at[k, i], lambda i: ol2.at[k, i],
                       oss.at[k], osr.at[k], oss2.at[k], osr2.at[k])

    def sq(k):
        j = far_first(k, at.z, nz)
        return Scatter(at, kind_of(k), lambda o: wq.at[j, drows(o)], lambda i: ql.at[k, i], lambda i: ql2.at[k, i],
                       qss.at[k], qsr.at[k], qss2.at[k], qsr2.at[k])

    def wo_unit(k, _):
        j = far_first(k, at.z, nz)

        def part(o, _):
            wo[o, hcols(j), :] = dot_tn(os_[:, hcols(j)], dh1b[:, drows(o)]).astype(LOW)
            return 0

        lax.fori_loop(0, nd, part, 0)
        so(k).either("start")
        return 0

    lax.fori_loop(0, nz, wo_unit, 0)

    lset[...] = lse[...].T
    dkv[...] = jnp.zeros_like(dkv)
    dxn1[...] = jnp.zeros_like(dxn1)
    here = at.z * KT + lax.broadcasted_iota(jnp.int32, (1, KT), 1)
    low_row = lo_row[0:1, :]

    def unit(k, _):
        j = far_first(k, at.z, nz)
        for hh in range(NH):
            cols = pl.ds(pl.multiple_of(j * HC + hh * HD, HD), HD)
            hid = j * NH + hh
            lrow = lset[pl.ds(hid, 1), :]
            qh = qs[:, cols]
            doh = dos[:, cols]
            delta = jnp.sum((doh.astype(F32) * os_[:, cols].astype(F32)).T, axis=0, keepdims=True)
            dq[...] = jnp.zeros_like(dq)

            def tile(b, _):
                kr_ = pl.ds(pl.multiple_of(b * KT, KT), KT)
                kt = kvs[kr_, pl.ds(0, HD)]
                vt = kvs[kr_, pl.ds(HD, HD)]
                s = dot_nt(kt, qh)
                place = b * KT + lax.broadcasted_iota(jnp.int32, (KT, KT), 0)
                s = jnp.where((place >= low_row) & (place <= here), s * scale, MASKED)
                p = jnp.exp(s - lrow)
                dkv[kr_, pl.ds(HD, HD)] += dot_nn(p.astype(LOW), doh)
                ds = (p * (dot_nt(vt, doh) - delta)).astype(LOW)
                dkv[kr_, pl.ds(0, HD)] += dot_nn(ds, qh)
                dq[...] += dot_tn(ds, kt)
                return 0

            lax.fori_loop(0, at.z + 1, tile, 0)
            u = dq[...] * scale
            qs[:, cols] = (u * cosf[...] - swap_halves(u) * sins[...]).astype(LOW)
        dqp = qs[:, hcols(j)]

        def back(o, _):
            dxn1[:, drows(o)] += dot_nt(dqp, wq[j, drows(o), :])
            wq[j, drows(o), :] = dot_tn(xn1[:, drows(o)], dqp).astype(LOW)
            return 0

        lax.fori_loop(0, nd, back, 0)
        sq(k).either("start")
        so(k).either("middle")
        return 0

    lax.fori_loop(0, nz, unit, 0)

    dkv[:, pl.ds(0, HD)] = dkv[:, pl.ds(0, HD)] * scale
    kvb[...] = dkv[...].astype(LOW)
    kswap = [remote(kvb.at[rows(2 * zz + 1 - at.c)], kland.at[zz], ks.at[zz], kr.at[zz], at.dp, at.sibling()) for zz in range(nz)]
    for cp in kswap:
        cp.start()
    swap_dh1.wait_send()
    dh1b[mine, :] = dxn1[theirs, :].astype(LOW)
    xswap = remote(dh1b.at[mine], xrecv, xsem.at[2], xsem.at[3], at.dp, at.sibling())
    xswap.start()

    def kpush(s):
        zz = lax.rem(at.z + s, nz)
        return remote(kvb.at[rows(2 * zz + at.c)], kz.at[s - 1], kzs.at[s - 1], kzr.at[s - 1], at.dp, 2 * zz + at.c)

    for s in range(1, nz + 1):
        zz = lax.rem(at.z + s, nz)
        r = rows(2 * zz + at.c)
        remote(kvb.at[rows(0)], kland.at[zz], ks.at[zz], kr.at[zz], at.dp, at.sibling()).wait_recv()
        dkv[r, :] = dkv[r, :] + kland[zz].astype(F32)
        if s < nz:
            kvb[r, :] = dkv[r, :].astype(LOW)
            kpush(s).start()

    lax.fori_loop(0, nz, lambda k, _: (sq(k).either("middle"), 0)[1], 0)
    total = dkv[rows(at.t), :] + later[...].astype(F32)
    for s in range(1, nz):
        kpush(s).wait_recv()
        total = total + kz[s - 1].astype(F32)
    dk = total[:, :HD]
    dk = dk * cosf[mine, :] - swap_halves(dk) * sins[mine, :]
    dkvp = jnp.concatenate([dk, total[:, HD:]], axis=1).astype(LOW)


    def wpush(s):
        tt = lax.rem(at.t + s, nt)
        return remote(wd2.at[pl.ds(pl.multiple_of(tt * Ds, Ds), Ds)], wl.at[at.t], ws.at[s - 1], wr.at[at.t], at.dp, tt)

    def upush(s):
        tt = lax.rem(at.t + s, nt)
        return remote(gpart.at[:, pl.ds(pl.multiple_of(tt * Ds, Ds), Ds)], gl.at[at.t], us.at[s - 1], ur.at[at.t], at.dp, tt)

    for o in range(nd):
        wd2[pl.ds(o * Dd, Dd), :] = dot_tn(xn1[mine, pl.ds(o * Dd, Dd)], dkvp).astype(LOW)
    for s in range(1, nt):
        wpush(s).start()

    xswap.wait_recv()
    for o in range(nd):
        cols = pl.ds(o * Dd, Dd)
        dxn1[mine, cols] = dxn1[mine, cols] + xrecv[:, cols].astype(F32) + dot_nt(dkvp, wkv[cols, :])

    def put_tokens(cols, v):
        tgrad[:, cols] = tgrad[:, cols] + v

    rms_back(lambda cols: tok[:, cols].astype(F32), lambda cols: dxn1[mine, cols], 0, put_tokens)
    for s in range(1, nt):
        upush(s).start()

    def zpush(k, buf, land, ss, rs):
        j = far_first(k, at.z, nz)
        return remote(buf.at[k], land.at[at.z], ss.at[k], rs.at[at.z], at.dp, 2 * j + at.c)

    def o_total(k, _):
        def put(v):
            oz[k] = v.astype(LOW)

        so(k).either("total", put)
        pl.when(k < nz - 1)(lambda: zpush(k, oz, olz, ozs, ozr).start())
        return 0

    def q_total(k, _):
        def put(v):
            qz[k] = v.astype(LOW)

        sq(k).either("total", put)
        pl.when(k < nz - 1)(lambda: zpush(k, qz, qlz, qzs, qzr).start())
        return 0

    lax.fori_loop(0, nz, o_total, 0)

    per = nt // nd
    wl[at.t] = wd2[pl.ds(pl.multiple_of(at.t * Ds, Ds), Ds), :]
    gl[at.t] = gpart[:, pl.ds(pl.multiple_of(at.t * Ds, Ds), Ds)]
    for s in range(1, nt):
        o = lax.rem(at.t + s, nt)
        remote(wd2.at[pl.ds(0, Ds)], wl.at[o], ws.at[s - 1], wr.at[o], at.dp, o).wait_recv()
        remote(gpart.at[:, pl.ds(0, Ds)], gl.at[o], us.at[s - 1], ur.at[o], at.dp, o).wait_recv()
    wsum = wl[0].astype(F32)
    usum = gl[0]
    for o in range(1, nt):
        wsum = wsum + wl[o].astype(F32)
        usum = usum + gl[o]
    owner = at.t // per
    is_owner = at.dp == owner
    slot = jnp.where(is_owner, at.t - at.dp * per, 0)
    w2[...] = wsum.astype(LOW)
    u2[...] = usum
    to = jnp.where(is_owner, lax.rem(at.dp + 1, nd), owner)
    give_w = remote(w2, w2l.at[at.dp], w2s.at[0], w2r.at[at.dp], to, at.t)
    give_u = remote(u2, u2l.at[at.dp], u2s.at[0], u2r.at[at.dp], to, at.t)

    def spread(s):
        tt = lax.rem(at.t + s, nt)
        return [remote(wfin.at[slot], wfin.at[slot], w3s.at[s - 1], w3r.at[slot], at.dp, tt),
                remote(gfin.at[slot], gfin.at[slot], u3s.at[s - 1], u3r.at[slot], at.dp, tt)]

    @pl.when(jnp.logical_not(is_owner))
    def _():
        give_w.start()
        give_u.start()

    lax.fori_loop(0, nz, q_total, 0)

    def square(v):
        return jnp.sum(v * v, axis=(0, 1), keepdims=True)

    share[...] = jnp.zeros_like(share)

    @pl.when(is_owner)
    def _():
        w2l[at.dp] = w2[...]
        u2l[at.dp] = u2[...]
        for s in range(1, nd):
            o = lax.rem(at.dp + s, nd)
            remote(w2, w2l.at[o], w2s.at[0], w2r.at[o], o, at.t).wait_recv()
            remote(u2, u2l.at[o], u2s.at[0], u2r.at[o], o, at.t).wait_recv()
        wtot = w2l[0].astype(F32)
        utot = u2l[0]
        for o in range(1, nd):
            wtot = wtot + w2l[o].astype(F32)
            utot = utot + u2l[o]
        wfin[slot] = wtot.astype(LOW)
        gfin[slot] = utot
        shared = square(wtot.astype(LOW).astype(F32)) + square(utot)
        share[...] = jnp.broadcast_to(shared, share.shape)
        for s in range(1, nt):
            for cp in spread(s):
                cp.start()

    squares = jnp.zeros((1, 1), F32)
    out_copies = []
    for n, (buf, keep, second, copies) in enumerate(big):
        total = buf[keep].astype(F32)
        for i, cp in enumerate(copies):
            cp.wait_recv()
            total = total + second[i].astype(F32)
        squares = squares + square(total)
        out_copies.append(pltpu.make_async_copy(second, (got_g, got_u, got_d, got_e)[n], outs.at[n]))
        out_copies.append(pltpu.make_async_copy(buf.at[keep], (keep_g, keep_u, keep_d, keep_e)[n], outs.at[4 + n]))
        for cp in out_copies[-2:]:
            cp.start()
    own_k = nz - 1
    for buf, land, ss, rs, out in ((oz, olz, ozs, ozr, go_out), (qz, qlz, qzs, qzr, gq_out)):
        total = buf[own_k].astype(F32)
        for s in range(1, nz):
            zz = lax.rem(at.z + s, nz)
            remote(buf.at[0], land.at[zz], ss.at[0], rs.at[zz], at.dp, at.sibling()).wait_recv()
            total = total + land[zz].astype(F32)
        squares = squares + square(total)
        out[...] = total
    squares = squares + share[0:1, 0:1]

    norms[at.t] = jnp.broadcast_to(squares, norms.shape[1:])

    def npush(s):
        return remote(norms.at[at.t], norms.at[at.t], ns.at[s - 1], nr.at[at.t], at.dp, lax.rem(at.t + s, nt))

    def n2push(s):
        return remote(normd.at[at.dp], normd.at[at.dp], n2s.at[s - 1], n2r.at[at.dp], lax.rem(at.dp + s, nd), at.t)

    for s in range(1, nt):
        npush(s).start()
    for q in range(per):
        t_from = at.dp * per + q

        @pl.when(at.t != t_from)
        def _(q=q, t_from=t_from):
            remote(wfin.at[q], wfin.at[q], w3s.at[0], w3r.at[q], at.dp, at.sibling()).wait_recv()
            remote(gfin.at[q], gfin.at[q], u3s.at[0], u3r.at[q], at.dp, at.sibling()).wait_recv()

        gkv_out[pl.ds(q * Ds, Ds), :] = wfin[q].astype(F32)
        gg_out[:, pl.ds(q * Ds, Ds)] = gfin[q]
    for s in range(1, nt):
        o = lax.rem(at.t + s, nt)
        remote(norms.at[o], norms.at[o], ns.at[s - 1], nr.at[o], at.dp, o).wait_recv()
    group = norms[0]
    for o in range(1, nt):
        group = group + norms[o]
    normd[at.dp] = group
    for s in range(1, nd):
        n2push(s).start()
    for s in range(1, nd):
        o = lax.rem(at.dp + s, nd)
        remote(normd.at[o], normd.at[o], n2s.at[s - 1], n2r.at[o], o, at.t).wait_recv()
    group = normd[0]
    for o in range(1, nd):
        group = group + normd[o]
    norm_out[...] = jnp.sqrt(group)

    for cp in out_copies:
        cp.wait()
    xswap.wait_send()
    for _, _, _, copies in big:
        for cp in copies:
            cp.wait_send()
    for cp in kswap:
        cp.wait_send()
    for s in range(1, nz):
        kpush(s).wait_send()
    for s in range(1, nt):
        wpush(s).wait_send()
        upush(s).wait_send()
        npush(s).wait_send()
    for s in range(1, nd):
        n2push(s).wait_send()

    def drain(k, _):
        so(k).either("drain")
        sq(k).either("drain")

        @pl.when(k < nz - 1)
        def _():
            zpush(k, oz, olz, ozs, ozr).wait_send()
            zpush(k, qz, qlz, qzs, qzr).wait_send()

        return 0

    lax.fori_loop(0, nz, drain, 0)

    @pl.when(jnp.logical_not(is_owner))
    def _():
        give_w.wait_send()
        give_u.wait_send()

    @pl.when(is_owner)
    def _():
        for s in range(1, nt):
            for cp in spread(s):
                cp.wait_send()


def grads(nd, nt, small, big_in, pieces):
    R, D = small[1].shape
    nz, ny = nt // 2, nd // 2
    h1, dxn2, xn1, wq, wo, wkv, kv, q, o = big_in
    Dd, HC = wo.shape[2], wq.shape[2]
    F = pieces[0].shape[2]
    Fh = F // 2
    S = R * nt
    Ds = D // nt
    W2 = 2 * HD
    slots = max(2 * (ny - 1), ny)
    hops = max(1, ny - 1)
    dma = lambda *s: pltpu.SemaphoreType.DMA(s)
    hbm = pl.BlockSpec(memory_space=pltpu.HBM)
    vm = pl.BlockSpec(memory_space=pltpu.VMEM)
    b = lambda *s: pltpu.VMEM(s, LOW)
    f = lambda *s: pltpu.VMEM(s, F32)
    shapes = [(R, D), (Dd, HC), (HC, Dd), (Dd, W2), (8, Dd), (8, 128)]
    lows = [(Dd, F), (Dd, F), (Fh, Dd), (Fh, Dd), (1, Dd, F), (hops, Dd, F), (1, Fh, Dd), (hops, Fh, Dd)]
    return pl.pallas_call(
        functools.partial(grads_kernel, nd, nt),
        out_shape=tuple([jax.ShapeDtypeStruct(s, F32) for s in shapes] + [jax.ShapeDtypeStruct(s, LOW) for s in lows]),
        in_specs=[vm] * 8 + [hbm] * 17,
        out_specs=(vm,) * 6 + (hbm,) * 8,
        scratch_shapes=[
            b(2 * R, D), b(nz, D, HC), b(nd, nz * HC, Dd), b(D, W2), b(S, W2), b(2 * R, nz * HC), b(2 * R, nz * HC), b(2 * R, nz * HC),
            b(2 * R, D), f(2 * R, D), f(128, 2 * R), f(S, W2), f(2 * R, HD),
            b(2, Dd, F), b(ny, Dd, F), b(2, Fh, Dd), b(ny, Fh, Dd),
            b(1, Dd, F), b(hops, Dd, F), b(1, Fh, Dd), b(hops, Fh, Dd),
            b(2 * (ny - 1), Dd, F), b(ny, Dd, F), b(2 * (ny - 1), Fh, Dd), b(ny, Fh, Dd),
            b(nz, slots, Dd, HC), b(nz, hops, Dd, HC), b(nz, slots, HC, Dd), b(nz, hops, HC, Dd),
            b(nz, Dd, HC), b(nz, HC, Dd), b(nz, Dd, HC), b(nz, HC, Dd),
            b(S, W2), b(nz, R, W2), b(nz, R, W2), b(R, D),
            b(nt, Ds, W2), b(D, W2), b(Ds, W2), b(nd, Ds, W2), b(nt // nd, Ds, W2),
            f(nt, 8, Ds), f(8, D), f(8, Ds), f(nd, 8, Ds), f(nt // nd, 8, Ds), f(8, 128), f(nt, 8, 128), f(nd, 8, 128),
            dma(17), dma(4), dma(4, hops), dma(4, hops),
            dma(nz, slots), dma(nz, slots), dma(nz, hops), dma(nz, hops), dma(nz, slots), dma(nz, slots), dma(nz, hops), dma(nz, hops),
            dma(nz), dma(nz), dma(nz), dma(nz),
            dma(nz), dma(nz), dma(nz), dma(nz),
            dma(nt), dma(nt), dma(1), dma(nd), dma(nt), dma(nt // nd),
            dma(nt), dma(nt), dma(1), dma(nd), dma(nt), dma(nt // nd),
            dma(nt), dma(nt), dma(nd), dma(nd), dma(8),
        ],
        compiler_params=pltpu.CompilerParams(collective_id=3, has_side_effects=True, vmem_limit_bytes=63 << 20),
        cost_estimate=pl.CostEstimate(flops=30 << 30, bytes_accessed=40 << 20, transcendentals=8 * 512 * 2048),
        name="grads",
    )(*small, *big_in, *pieces)


def advance(grad_raw, weight, moment, average, factor, rate):
    average_decay = min(AVERAGE_TOP, (1.0 + STEP) / (10.0 + STEP))
    clipped = grad_raw * factor
    moment_new = MOMENTUM * moment + clipped
    weight_new = weight - rate * (clipped + MOMENTUM * moment_new)
    average_new = average_decay * average + (1.0 - average_decay) * weight_new
    return (clipped, moment_new, average_new, weight_new, weight_new.astype(jnp.bfloat16))


def local(
    tokens,
    cotangent,
    kv_later,
    lengths,
    query_weight,
    query_moment,
    query_average,
    keyvalue_weight,
    keyvalue_moment,
    keyvalue_average,
    output_weight,
    output_moment,
    output_average,
    gateup_weight,
    gateup_moment,
    gateup_average,
    down_weight,
    down_moment,
    down_average,
    norm_gains,
    gains_moment,
    gains_average,
):
    masters = (query_weight, keyvalue_weight, output_weight, gateup_weight, down_weight, norm_gains)
    low_query, low_kv, low_output, low_gateup, low_down, low_gains = (w.astype(LOW) for w in masters)
    nd, nt = lax.axis_size("dp"), lax.axis_size("tensor")
    row_count = tokens.shape[0]
    pair_rows = 2 * row_count

    doc_lengths = lengths[0]
    endings = jnp.cumsum(doc_lengths)
    beginnings = endings - doc_lengths
    places = (lax.axis_index("tensor") // 2) * pair_rows + jnp.arange(pair_rows, dtype=jnp.int32)
    segment = jnp.sum((places[:, None] >= endings[None, :]).astype(jnp.int32), axis=1)
    picked = segment[:, None] == jnp.arange(doc_lengths.shape[0], dtype=jnp.int32)[None, :]
    first = jnp.sum(jnp.where(picked, beginnings[None, :], 0), axis=1).astype(jnp.int32)
    half_size = HD // 2
    frequency = jnp.exp(jnp.arange(half_size, dtype=F32) * (-2.0 * math.log(ROPE_BASE) / HD))
    angles = (places - first).astype(F32)[:, None] * frequency[None, :]
    cosine, sine = jnp.cos(angles), jnp.sin(angles)
    cosine_full = jnp.concatenate([cosine, cosine], axis=1)
    sine_full = jnp.concatenate([-sine, sine], axis=1)
    gain_rows = jnp.pad(low_gains.astype(F32), ((0, 6), (0, 0)))

    grad_rows = lax.all_gather(cotangent, "tensor", axis=0, tiled=True)
    hidden_one, normed_two, gains_all, lse, normed_one, all_query, all_output, all_kv, kv_rows, queries, attended = attend(
        nd, nt, tokens, gain_rows, low_query, low_kv, low_output, cosine_full, sine_full, first[:, None]
    )
    grad_normed_two, *pieces, mlp_rows = mlp(nd, nt, normed_two, grad_rows, low_gateup, low_down)
    mixed = hidden_one + lax.psum_scatter(mlp_rows, "tensor", scatter_dimension=0, tiled=True).astype(F32)
    tokens_grad, own_query, own_output, grad_keyvalue, gains_sum, norm_tile, *halves = grads(
        nd,
        nt,
        (cotangent, tokens, gains_all, cosine_full, sine_full, jnp.broadcast_to(first[None, :], (8, pair_rows)), lse, kv_later),
        (hidden_one, grad_normed_two, normed_one, all_query, all_output, all_kv, kv_rows, queries, attended),
        pieces,
    )
    whole = [kept.astype(F32) + jnp.sum(got.astype(F32), axis=0) for kept, got in zip(halves[:4], halves[4:])]
    own_gateup = jnp.stack(whole[:2])
    own_down = jnp.concatenate(whole[2:], axis=0)
    grad_gains = gains_sum[:2]
    grad_norm = norm_tile[0, 0]
    factor = jnp.minimum(1.0, CLIP / (grad_norm + 1e-06))
    query_set = advance(
        own_query, query_weight, query_moment, query_average, factor, LEARNING_RATES[0]
    )
    keyvalue_set = advance(
        grad_keyvalue, keyvalue_weight, keyvalue_moment, keyvalue_average, factor, LEARNING_RATES[1]
    )
    output_set = advance(
        own_output, output_weight, output_moment, output_average, factor, LEARNING_RATES[2]
    )
    gateup_set = advance(
        own_gateup, gateup_weight, gateup_moment, gateup_average, factor, LEARNING_RATES[3]
    )
    down_set = advance(own_down, down_weight, down_moment, down_average, factor, LEARNING_RATES[4])
    gains_set = advance(
        grad_gains, norm_gains, gains_moment, gains_average, factor, LEARNING_RATES[5]
    )
    return (
        mixed,
        mixed.astype(jnp.bfloat16),
        tokens_grad,
        grad_norm,
        query_set[0],
        query_set[1],
        query_set[2],
        query_set[3],
        query_set[4],
        keyvalue_set[0],
        keyvalue_set[1],
        keyvalue_set[2],
        keyvalue_set[3],
        keyvalue_set[4],
        output_set[0],
        output_set[1],
        output_set[2],
        output_set[3],
        output_set[4],
        gateup_set[0],
        gateup_set[1],
        gateup_set[2],
        gateup_set[3],
        gateup_set[4],
        down_set[0],
        down_set[1],
        down_set[2],
        down_set[3],
        down_set[4],
        gains_set[0],
        gains_set[1],
        gains_set[2],
        gains_set[3],
        gains_set[4],
    )


def solution(mesh):
    return jax.shard_map(
        local,
        mesh=mesh,
        in_specs=(
            P(("dp", "tensor"), None),
            P(("dp", "tensor"), None),
            P(("dp", "tensor"), None),
            P("dp", None),
            P("dp", "tensor"),
            P("dp", "tensor"),
            P("dp", "tensor"),
            P("dp", None),
            P("dp", None),
            P("dp", None),
            P("tensor", "dp"),
            P("tensor", "dp"),
            P("tensor", "dp"),
            P(None, "dp", "tensor"),
            P(None, "dp", "tensor"),
            P(None, "dp", "tensor"),
            P("tensor", "dp"),
            P("tensor", "dp"),
            P("tensor", "dp"),
            P(None, "dp"),
            P(None, "dp"),
            P(None, "dp"),
        ),
        out_specs=(
            P(("dp", "tensor"), None),
            P(("dp", "tensor"), None),
            P(("dp", "tensor"), None),
            P(),
            P("dp", "tensor"),
            P("dp", "tensor"),
            P("dp", "tensor"),
            P("dp", "tensor"),
            P("dp", "tensor"),
            P("dp", None),
            P("dp", None),
            P("dp", None),
            P("dp", None),
            P("dp", None),
            P("tensor", "dp"),
            P("tensor", "dp"),
            P("tensor", "dp"),
            P("tensor", "dp"),
            P("tensor", "dp"),
            P(None, "dp", "tensor"),
            P(None, "dp", "tensor"),
            P(None, "dp", "tensor"),
            P(None, "dp", "tensor"),
            P(None, "dp", "tensor"),
            P("tensor", "dp"),
            P("tensor", "dp"),
            P("tensor", "dp"),
            P("tensor", "dp"),
            P("tensor", "dp"),
            P(None, "dp"),
            P(None, "dp"),
            P(None, "dp"),
            P(None, "dp"),
            P(None, "dp"),
        ),
        check_vma=False,
    )
```

```python
import functools
import math

import jax
import jax.numpy as jnp
from jax import lax
from jax.experimental import pallas as pl
from jax.experimental.pallas import tpu as pltpu
from jax.sharding import PartitionSpec as P

HD = 128
STEP = 10


EPSILON = 1e-05
MASKED = -1000000000.0
CLIP = 1.0
MOMENTUM = 0.9
LEARNING_RATES = (12.0, 12.0, 480.0, 48.0, 12.0, 960.0)
AVERAGE_TOP = 0.999
ROPE_BASE = 10000.0
MESH = pl.DeviceIdType.MESH
LOW = jnp.bfloat16
F32 = jnp.float32


def dot_nn(a, b):
    return jnp.dot(a, b, preferred_element_type=F32)


def dot_nt(a, b):
    return lax.dot_general(a, b, (((1,), (1,)), ((), ())), preferred_element_type=F32)


def dot_tn(a, b):
    return lax.dot_general(a, b, (((0,), (0,)), ((), ())), preferred_element_type=F32)


class Place:
    def __init__(self, nd, nt):
        self.nd, self.nt = nd, nt
        self.nx = 2 if nd % 2 == 0 else 1
        self.ny = nd // self.nx
        self.nz = nt // 2
        self.dp = lax.axis_index("dp")
        self.t = lax.axis_index("tensor")
        self.y = self.dp // self.nx
        self.x = lax.rem(self.dp, self.nx)
        self.z = self.t // 2
        self.c = lax.rem(self.t, 2)

    def x_peer(self):
        return self.y * self.nx + (1 - self.x)

    def y_peer(self, step):
        return lax.rem(self.y + step, self.ny) * self.nx + self.x

    def xy_peer(self, step):
        return lax.rem(self.y + step, self.ny) * self.nx + (1 - self.x)

    def sibling(self):
        return self.z * 2 + (1 - self.c)


def remote(src, dst, send, recv, dp, t):
    return pltpu.make_async_remote_copy(src, dst, send, recv, device_id=(dp, t), device_id_type=MESH)


def greet(at, dps=True, zs=True, core=True):
    bar = pltpu.get_barrier_semaphore()
    count = 0
    targets = []
    if dps:
        targets.append((at.x_peer(), at.t))
        targets += [(at.y_peer(s), at.t) for s in range(1, at.ny)]
    if core:
        targets.append((at.dp, at.sibling()))
    for target in targets:
        pl.semaphore_signal(bar, inc=1, device_id=target, device_id_type=MESH)
        count += 1
    if zs:
        @pl.when(at.z > 0)
        def _():
            pl.semaphore_signal(bar, inc=1, device_id=(at.dp, at.t - 2), device_id_type=MESH)

        @pl.when(at.z < at.nz - 1)
        def _():
            pl.semaphore_signal(bar, inc=1, device_id=(at.dp, at.t + 2), device_id_type=MESH)

        count = count + (at.z > 0).astype(jnp.int32) + (at.z < at.nz - 1).astype(jnp.int32)
    pl.semaphore_wait(bar, count)


def far_first(k, z, nz):
    j = nz - 1 - k
    m = jnp.minimum(z, nz - 1 - z)
    s = (j + 1) // 2
    two = jnp.where(lax.rem(j, 2) == 1, z - s, z + s)
    one = jnp.where(z < nz - 1 - z, j, nz - 1 - j)
    return jnp.where(j <= 2 * m, two, one)


def near_first(k, z, nz):
    return far_first(nz - 1 - k, z, nz)


class Gather:
    def __init__(self, at, src, dst, xs, ys, xf, yf, recv, kind):
        self.at, self.src, self.dst, self.kind = at, src, dst, kind
        self.xs, self.ys, self.xf, self.yf, self.recv = xs, ys, xf, yf, recv

    def own(self):
        at = self.at
        out = [remote(self.src, self.dst(at.dp), self.xs, self.recv.at[at.dp], at.x_peer(), at.t)]
        for s in range(1, at.ny):
            out.append(remote(self.src, self.dst(at.dp), self.ys.at[s - 1], self.recv.at[at.dp], at.y_peer(s), at.t))
        return out

    def passed(self):
        at = self.at
        out = []
        for s in range(1, at.ny):
            if self.kind == 0:
                o = at.x_peer()
                out.append(remote(self.dst(o), self.dst(o), self.yf.at[s - 1], self.recv.at[o], at.y_peer(s), at.t))
            else:
                o = at.y_peer(s)
                out.append(remote(self.dst(o), self.dst(o), self.xf.at[s - 1], self.recv.at[o], at.x_peer(), at.t))
        return out

    def arrived(self, o):
        remote(self.src, self.dst(o), self.xs, self.recv.at[o], self.at.x_peer(), self.at.t).wait_recv()

    def start(self):
        for cp in self.own():
            cp.start()

    def forward(self):
        at = self.at
        if self.kind == 0:
            self.arrived(at.x_peer())
        else:
            for s in range(1, at.ny):
                self.arrived(at.y_peer(s))
        for cp in self.passed():
            cp.start()

    def finish(self):
        at = self.at
        if self.kind == 0:
            for s in range(1, at.ny):
                self.arrived(at.y_peer(s))
        else:
            self.arrived(at.x_peer())
        for s in range(1, at.ny):
            self.arrived(at.xy_peer(s))

    def either(self, name):
        kind = self.kind
        for value in range(2):
            self.kind = value
            pl.when(kind == value)(getattr(self, name))
        self.kind = kind

    def finish_any(self):
        self.either("finish")

    def forward_any(self):
        self.either("forward")

    def drain_any(self):
        self.either("drain")

    def drain(self):
        for cp in self.own() + self.passed():
            cp.wait_send()


def mlp_kernel(nd, nt, xn_in, dy_in, w_all, w_in,
               dxn_out, mine_g, land_g, mine_u, land_u, down_out, out_out,
               both, wts, act, psend, pown, precv, zrecv, bsend, bown, bland,
               lsem, wx, wy, wxf, wyf, wr, ar, ac, asr, asl, ps, pr, zs, zr, bs, br, osem, dsem, p1l, p1s, p1r):
    at = Place(nd, nt)
    nz, nx, ny = at.nz, at.nx, at.ny
    R, D = xn_in.shape
    F, Dd = w_in.shape
    Fh = F // 2
    CH = zs.shape[1]
    CR = R // CH
    rows = lambda t: pl.ds(pl.multiple_of(t * R, R), R)
    dcols = lambda o: pl.ds(pl.multiple_of(o * Dd, Dd), Dd)
    xall, dyv = both.at[0], both.at[1]

    own_loads = [
        pltpu.make_async_copy(xn_in, xall.at[rows(at.t)], lsem.at[0]),
        pltpu.make_async_copy(dy_in, dyv, lsem.at[1]),
        pltpu.make_async_copy(w_all, wts.at[pl.ds(0, 2)], lsem.at[2]),
        pltpu.make_async_copy(w_in, wts.at[2, :, dcols(at.dp)], lsem.at[3]),
    ]
    for cp in own_loads:
        cp.start()
    greet(at)

    gathers = []
    for p in range(2):
        half = pl.ds(p * Fh, Fh)
        gathers.append(Gather(at, w_in.at[half], lambda o, half=half: wts.at[2, half, dcols(o)],
                              wx.at[p], wy.at[p], wxf.at[p], wyf.at[p], wr.at[p], p))

    def right(o):
        return remote(xall.at[rows(o)], xall.at[rows(o)], asr.at[o], ar.at[o], at.dp, at.t + 2)

    def left(o):
        return remote(xall.at[rows(o)], xall.at[rows(o)], asl.at[o], ar.at[o], at.dp, at.t - 2)

    def across(o):
        return remote(xall.at[rows(o)], xall.at[rows(o)], ac.at[o], ar.at[o], at.dp, at.sibling())

    own_loads[0].wait()
    pl.when(at.z < nz - 1)(lambda: right(at.t).start())
    pl.when(at.z > 0)(lambda: left(at.t).start())
    across(at.t).start()
    for g in gathers:
        g.start()

    def line_step(s):
        @pl.when(at.z - s >= 0)
        def _():
            o = at.t - 2 * s
            across(o).wait_recv()
            pl.when(at.z < nz - 1)(lambda: right(o).start())
            across(o).start()

        @pl.when(at.z + s < nz)
        def _():
            o = at.t + 2 * s
            across(o).wait_recv()
            pl.when(at.z > 0)(lambda: left(o).start())
            across(o).start()

    for g in gathers:
        g.forward()
    for cp in own_loads[1:]:
        cp.wait()

    is_end = (at.z == 0) | (at.z == nz - 1)
    piece = lambda c: pl.ds(pl.multiple_of(c * CR, CR), CR)

    def swap(d):
        return remote(psend, precv.at[d], ps.at[0], pr.at[d], at.dp, at.sibling())

    def push_right(d, c):
        return remote(pown.at[d, piece(c)], zrecv.at[d, piece(c)], zs.at[d, c], zr.at[d, c], at.dp, at.t + 2)

    def push_left(d, c):
        slot = jnp.where(d == at.z - 1, nz, d)
        return remote(pown.at[d, piece(c)], zrecv.at[slot, piece(c)], zs.at[d, c], zr.at[slot, c], at.dp, at.t - 2)

    def came(slot, c):
        remote(pown.at[0, piece(c)], zrecv.at[slot, piece(c)], zs.at[0, c], zr.at[slot, c], at.dp, at.sibling()).wait_recv()

    def relay(d, c, push):
        pl.when(c == 0)(lambda: swap(d).wait_recv())

        @pl.when(is_end)
        def _():
            pown[d, piece(c)] = (pown[d, piece(c)].astype(F32) + precv[d, piece(c)].astype(F32)).astype(LOW)

        @pl.when(jnp.logical_not(is_end))
        def _():
            came(d, c)
            pown[d, piece(c)] = (pown[d, piece(c)].astype(F32) + precv[d, piece(c)].astype(F32)
                                 + zrecv[d, piece(c)].astype(F32)).astype(LOW)

        push(d, c).start()

    def relays(s, c):
        pl.when(s > at.z)(lambda: relay(s, c, push_right))
        pl.when(nz - 1 - s < at.z)(lambda: relay(nz - 1 - s, c, push_left))

    def branch_swap(j):
        return remote(bsend, bland.at[j], bs.at[0], br.at[j], at.dp, at.sibling())

    def branch_copy(slot, j):
        return pltpu.make_async_copy(bown.at[slot], out_out.at[j], osem.at[slot])

    def branch_sum(k):
        j = near_first(k, at.z, nz)
        slot = lax.rem(k, 2)
        branch_swap(j).wait_recv()

        def part(c, _):
            bown[slot, piece(c)] = (bown[slot, piece(c)].astype(F32) + bland[j, piece(c)].astype(F32)).astype(LOW)
            return 0

        lax.fori_loop(0, CH, part, 0)
        branch_copy(slot, j).start()

    def forward(j):
        r = pl.ds(pl.multiple_of(j * 2 * R, 2 * R), 2 * R)
        for lo in range(0, F, 256):
            part = pl.ds(lo, min(256, F - lo))
            gate, up = dot_nt(xall[r, :], wts[0, part, :]), dot_nt(xall[r, :], wts[1, part, :])
            dmid = dot_nt(dyv[r, :], wts[2, part, :])
            sig = 1.0 / (1.0 + jnp.exp(-gate))
            silu = gate * sig
            act[2, r, part] = (silu * up).astype(LOW)
            act[1, r, part] = (dmid * silu).astype(LOW)
            act[0, r, part] = (dmid * up * (sig * (1.0 + gate * (1.0 - sig)))).astype(LOW)

    def block(k, _):
        pl.when((k == nz - 1) & (k >= 2))(lambda: line_step(k))
        j = near_first(k, at.z, nz)
        across(2 * j + 1 - at.c).wait_recv()
        slot = lax.rem(k, 2)
        forward(j)
        pl.when((k >= 1) & (k < nz - 2))(lambda: line_step(k + 1))
        pl.when(k >= 1)(lambda: swap(j).wait_send())
        r = pl.ds(pl.multiple_of(j * 2 * R, 2 * R), 2 * R)

        def back(o, _):
            cols = dcols(o)
            v = dot_nn(act[0, r, :], wts[0, :, cols]) + dot_nn(act[1, r, :], wts[1, :, cols])
            first = at.c == 0
            psend[:, cols] = jnp.where(first, v[R:], v[:R]).astype(LOW)
            pown[j, :, cols] = jnp.where(first, v[:R], v[R:]).astype(LOW)
            return 0

        lax.fori_loop(0, nd, back, 0)
        swap(j).start()
        s = jnp.where(is_end, k, k - 1)

        @pl.when((s >= 1) & (is_end | (s < nz - 2)))
        def _():
            lax.fori_loop(0, CH, lambda c, _: (relays(s, c), 0)[1], 0)

        pl.when(k >= 1)(lambda: branch_sum(k - 1))
        pl.when(k >= 1)(lambda: branch_swap(j).wait_send())
        pl.when(k >= 2)(lambda: branch_copy(slot, j).wait())

        def branch(o, _):
            cols = dcols(o)
            v = dot_nn(act[2, r, :], wts[2, :, cols])
            first = at.c == 0
            bsend[:, cols] = jnp.where(first, v[R:], v[:R]).astype(LOW)
            bown[slot, :, cols] = jnp.where(first, v[:R], v[R:]).astype(LOW)
            return 0

        lax.fori_loop(0, nd, branch, 0)
        branch_swap(j).start()
        return 0

    if nz > 1:
        line_step(1)
    for g in gathers:
        g.finish()
    lax.fori_loop(0, nz, block, 0)
    swap(0).wait_send()
    branch_swap(0).wait_send()
    branch_sum(jnp.int32(nz - 1))
    for g in gathers:
        g.drain()

    outs = ((mine_g, land_g), (mine_u, land_u))

    def source(n, o):
        return wts.at[n, :, dcols(o)]

    def down_copy(o):
        return pltpu.make_async_copy(wts.at[2, :, dcols(o)], down_out.at[:, dcols(o)], dsem.at[o])

    def hop(n, o):
        mine, land = outs[n]
        yy, xx = o // nx, lax.rem(o, nx)
        if n % 2 == 0:
            step = lax.rem(yy - at.y + ny, ny)
            slot = (step - 1) * nx + xx
            stays, place, peer = yy == at.y, xx, yy * nx + at.x
        else:
            slot, stays, place, peer = yy, xx == at.x, yy, at.y * nx + xx
        local = pltpu.make_async_copy(source(n, o), mine.at[place], p1l.at[n, place])
        slot = jnp.where(stays, 0, slot)
        away = remote(source(n, o), land.at[slot], p1s.at[n, slot], p1r.at[n, slot], jnp.where(stays, at.x_peer(), peer), at.t)
        return stays, local, away

    def order(n, i):
        if n % 2 == 0:
            return lax.rem(at.y + 1 + i // nx, ny) * nx + lax.rem(i, nx)
        return lax.rem(i, ny) * nx + jnp.where(i < ny, 1 - at.x, at.x)

    def send(n, o):
        stays, local, away = hop(n, o)
        pl.when(stays)(lambda: local.start())
        pl.when(jnp.logical_not(stays))(lambda: away.start())

    def settle(n):
        def one(i, _):
            stays, local, away = hop(n, order(n, i))

            @pl.when(stays)
            def _():
                local.wait()

            @pl.when(jnp.logical_not(stays))
            def _():
                away.wait_send()
                away.wait_recv()

            return 0

        lax.fori_loop(0, nd, one, 0)

    def wgrad(p, _):
        n, i = p // nd, lax.rem(p, nd)
        middle = jnp.logical_not(is_end)
        early, late = p - 1, p // 2 - 3
        pl.when(middle & (early >= 0) & (early < CH))(lambda: relays(jnp.int32(nz - 2), early))
        pl.when(middle & (lax.rem(p, 2) == 0) & (late >= 0) & (late < CH - 1))(lambda: relays(jnp.int32(nz - 1), late))
        o = jnp.where(n == 1, order(1, i), order(0, i))
        for lo in range(0, F, 384):
            part = pl.ds(lo, min(384, F - lo))
            wts[n, part, dcols(o)] = dot_tn(act[n, :, part], both[n // 2, :, dcols(o)]).astype(LOW)
        pl.when(n == 0)(lambda: send(0, o))
        pl.when(n == 1)(lambda: send(1, o))
        pl.when(n == 2)(lambda: down_copy(o).start())
        return 0

    lax.fori_loop(0, 3 * nd, wgrad, 0)
    pl.when(jnp.logical_not(is_end))(lambda: relays(jnp.int32(nz - 1), jnp.int32(CH - 1)))
    for slot in range(2):
        branch_copy(slot, 0).wait()

    swap(at.z).wait_recv()
    for c in range(CH):
        part = pl.ds(c * CR, CR)
        pl.when(at.z > 0)(lambda c=c: came(at.z, c))
        pl.when(at.z < nz - 1)(lambda c=c: came(nz, c))
        total = pown[at.z, part].astype(F32) + precv[at.z, part].astype(F32)
        total = total + jnp.where(at.z > 0, zrecv[at.z, part].astype(F32), 0.0)
        total = total + jnp.where(at.z < nz - 1, zrecv[nz, part].astype(F32), 0.0)
        dxn_out[part, :] = total.astype(LOW)

    for zz in range(nz):
        o = 2 * zz + at.c

        @pl.when(zz != at.z)
        def _(zz=zz):
            for c in range(CH):
                push_right(jnp.int32(zz), c).wait_send()

        across(o).wait_send()
        pl.when((at.z < nz - 1) & (zz <= at.z))(lambda o=o: right(o).wait_send())
        pl.when((at.z > 0) & (zz >= at.z))(lambda o=o: left(o).wait_send())
    for n in range(2):
        settle(n)
    for o in range(nd):
        down_copy(o).wait()


def mlp(nd, nt, xn, dy_all, w_all, w):
    R, D = xn.shape
    S = dy_all.shape[0]
    F, Dd = w.shape
    nz = nt // 2
    ny = nd // 2
    ch = 4
    dma = lambda *s: pltpu.SemaphoreType.DMA(s)
    shape = lambda *s: jax.ShapeDtypeStruct(s, LOW)
    b = lambda *s: pltpu.VMEM(s, LOW)
    slots = max(2 * (ny - 1), ny)
    hbm = pl.BlockSpec(memory_space=pltpu.HBM)
    vm = pl.BlockSpec(memory_space=pltpu.VMEM)
    return pl.pallas_call(
        functools.partial(mlp_kernel, nd, nt),
        out_shape=(
            shape(R, D),
            shape(2, F, Dd), shape(2 * (ny - 1), F, Dd), shape(ny, F, Dd), shape(ny, F, Dd),
            shape(F, D),
            shape(nz, R, D),
        ),
        in_specs=[hbm] * 4,
        out_specs=(vm,) + (hbm,) * 6,
        scratch_shapes=[
            b(2, S, D), b(3, F, D), b(3, S, F),
            b(R, D), b(nz, R, D), b(nz, R, D), b(nz + 1, R, D), b(R, D), b(2, R, D), b(nz, R, D),
            dma(4), dma(2), dma(2, ny - 1), dma(2, ny - 1), dma(2, ny - 1), dma(2, nd),
            dma(nt), dma(nt), dma(nt), dma(nt), dma(1), dma(nz), dma(nz, ch), dma(nz + 1, ch), dma(1), dma(nz), dma(2), dma(nd),
            dma(2, max(2, ny)), dma(2, slots), dma(2, slots),
        ],
        compiler_params=pltpu.CompilerParams(collective_id=1, has_side_effects=True, vmem_limit_bytes=63 << 20),
        cost_estimate=pl.CostEstimate(flops=12 * S * D * F, bytes_accessed=40 << 20, transcendentals=S * F),
        name="mlp",
    )(xn, dy_all, w_all, w)


def swap_halves(u):
    h = u.shape[-1] // 2
    return jnp.concatenate([u[:, h:], u[:, :h]], axis=1)


def greet_all(at):
    bar = pltpu.get_barrier_semaphore()
    for s in range(1, at.nd):
        pl.semaphore_signal(bar, inc=1, device_id=(lax.rem(at.dp + s, at.nd), at.t), device_id_type=MESH)
    for s in range(1, at.nt):
        pl.semaphore_signal(bar, inc=1, device_id=(at.dp, lax.rem(at.t + s, at.nt)), device_id_type=MESH)
    pl.semaphore_wait(bar, at.nd - 1 + at.nt - 1)


class Line:
    def __init__(self, at, view, right, left, recv, across=None):
        self.at, self.view, self.rs, self.ls, self.recv, self.across = at, view, right, left, recv, across

    def right(self, o):
        return remote(self.view(o), self.view(o), self.rs.at[o], self.recv.at[o], self.at.dp, self.at.t + 2)

    def left(self, o):
        return remote(self.view(o), self.view(o), self.ls.at[o], self.recv.at[o], self.at.dp, self.at.t - 2)

    def pass_on(self, o, to_right, to_left):
        at = self.at
        if to_right:
            pl.when(at.z < at.nz - 1)(lambda: self.right(o).start())
        if to_left:
            pl.when(at.z > 0)(lambda: self.left(o).start())
        if self.across is not None:
            self.across(o).start()

    def start(self):
        self.pass_on(self.at.z, True, True)

    def arrived(self, o):
        remote(self.view(o), self.view(o), self.rs.at[o], self.recv.at[o], self.at.dp, self.at.sibling()).wait_recv()

    def step(self, s):
        at = self.at

        @pl.when(at.z - s >= 0)
        def _():
            self.arrived(at.z - s)
            self.pass_on(at.z - s, True, False)

        @pl.when(at.z + s < at.nz)
        def _():
            self.arrived(at.z + s)
            self.pass_on(at.z + s, False, True)

    def drain(self):
        at = self.at
        for o in range(at.nz):
            pl.when((at.z < at.nz - 1) & (o <= at.z))(lambda o=o: self.right(o).wait_send())
            pl.when((at.z > 0) & (o >= at.z))(lambda o=o: self.left(o).wait_send())
            if self.across is not None:
                self.across(o).wait_send()


def attend_kernel(nd, nt, tok, gain, wq_in, wkv_in, wo_in, cosf, sins, lo_in, dy_in, w_in,
                  h1_out, xn2_out, gfull, lse_out,
                  xn1_out, wq_out, wo_out, wkv_out, kv_out, q_out, o_out, dy_all, w_all,
                  xn1, wq, wo, wkv, kvs, qs, os_, pback, precv,
                  lsem, gs, gr, vx, vy, vxf, vyf, vr, qx, qy, qxf, qyf, qr, ox, oy, oxf, oyf, orr,
                  qlr, qll, qlv, olr, oll, olv, klr, kll, klv, klc, klcr, cs, cr, outs,
                  ylr, yll, ylv, ylc, mx, my, mxf, myf, mr, fsem):
    at = Place(nd, nt)
    nz = at.nz
    R, D = tok.shape
    Dd, HC = wq_in.shape
    TQ = min(256, 2 * R)
    rows = lambda t: pl.ds(pl.multiple_of(t * R, R), R)
    drows = lambda o: pl.ds(pl.multiple_of(o * Dd, Dd), Dd)
    hcols = lambda j: pl.ds(pl.multiple_of(j * HC, HC), HC)

    loads = [
        pltpu.make_async_copy(wkv_in, wkv.at[drows(at.dp)], lsem.at[0]),
        pltpu.make_async_copy(wq_in, wq.at[at.z, drows(at.dp)], lsem.at[1]),
        pltpu.make_async_copy(wo_in, wo.at[at.dp, hcols(at.z)], lsem.at[2]),
    ]
    for cp in loads:
        cp.start()
    gfull[at.dp] = gain[...]
    greet_all(at)

    def gain_copy(s):
        return remote(gain, gfull.at[at.dp], gs.at[s - 1], gr.at[s - 1], lax.rem(at.dp + s, nd), at.t)

    for s in range(1, nd):
        gain_copy(s).start()
    Dh = Dd // 2
    gkv = [Gather(at, wkv_in.at[pl.ds(p * Dh, Dh)], lambda o, p=p: wkv.at[pl.ds(pl.multiple_of(o * Dd + p * Dh, Dh), Dh)],
                  vx.at[p], vy.at[p], vxf.at[p], vyf.at[p], vr.at[p], p) for p in range(2)]

    def gq(k):
        j = near_first(k, at.z, nz)
        return Gather(at, wq.at[j, drows(at.dp)], lambda o: wq.at[j, drows(o)], qx.at[k], qy.at[k], qxf.at[k], qyf.at[k], qr.at[k], lax.rem(k, 2) if not isinstance(k, int) else k % 2)

    def go(k):
        j = near_first(k, at.z, nz)
        return Gather(at, wo.at[at.dp, hcols(j)], lambda o: wo.at[o, hcols(j)], ox.at[k], oy.at[k], oxf.at[k], oyf.at[k], orr.at[k], lax.rem(k, 2) if not isinstance(k, int) else k % 2)

    lq = Line(at, lambda o: wq.at[o, drows(at.dp)], qlr, qll, qlv)
    lo = Line(at, lambda o: wo.at[at.dp, hcols(o)], olr, oll, olv)

    def kv_view(o):
        return kvs.at[rows(2 * o + at.c)]

    def kv_across(o):
        return remote(kv_view(o), kv_view(o), klc.at[o], klcr.at[o], at.dp, at.sibling())

    lkv = Line(at, kv_view, klr, kll, klv, kv_across)

    for_mlp = [pltpu.make_async_copy(dy_in, dy_all.at[rows(at.t)], fsem.at[0]),
               pltpu.make_async_copy(w_in.at[0], w_all.at[0, :, drows(at.dp)], fsem.at[1]),
               pltpu.make_async_copy(w_in.at[1], w_all.at[1, :, drows(at.dp)], fsem.at[2])]
    for cp in for_mlp:
        cp.start()
    gw = [Gather(at, w_in.at[p], lambda o, p=p: w_all.at[p, :, drows(o)], mx.at[p], my.at[p], mxf.at[p], myf.at[p], mr.at[p], p)
          for p in range(2)]

    def dy_view(o):
        return dy_all.at[rows(2 * o + at.c)]

    def dy_across(o):
        return remote(dy_view(o), dy_view(o), ylc.at[o], ylv.at[1, o], at.dp, at.sibling())

    ldy = Line(at, dy_view, ylr, yll, ylv.at[0], dy_across)
    for g in gkv:
        g.start()
    loads[1].wait()
    lq.start()
    gq(0).start()

    for s in range(1, nd):
        gain_copy(s).wait_recv()

    def scaled(v, row, write):
        r = lax.rsqrt(jnp.mean(v * v, axis=-1, keepdims=True) + EPSILON)
        for o in range(nd):
            cols = pl.ds(o * Dd, Dd)
            write(cols, (v[:, o * Dd:(o + 1) * Dd] * r * gfull[o, row:row + 1, :]).astype(LOW))

    mine = rows(at.c)

    def put_xn1(cols, v):
        xn1[mine, cols] = v

    scaled(tok[...].astype(F32), 0, put_xn1)
    xn1_across = remote(xn1.at[mine], xn1.at[mine], cs.at[0], cr.at[0], at.dp, at.sibling())
    xn1_across.start()

    for g in gkv:
        g.forward()
    loads[0].wait()
    for g in gkv:
        g.finish()
    kvpre = dot_nn(xn1[mine, :], wkv[...])
    kk = kvpre[:, :HD]
    kvs[rows(at.t), pl.ds(0, HD)] = (kk * cosf[mine, :] + swap_halves(kk) * sins[mine, :]).astype(LOW)
    kvs[rows(at.t), pl.ds(HD, HD)] = kvpre[:, HD:].astype(LOW)
    lkv.start()
    loads[2].wait()
    lo.start()
    for s in range(1, nz):
        lq.step(s)
        gq(s).start()
        gq(s - 1).forward()
        lkv.step(s)
    gq(nz - 1).forward()
    xn1_across.wait_recv()
    go(0).start()
    for s in range(1, nz):
        lo.step(s)
        go(s).start()
    for_mlp[0].wait()
    ldy.start()
    for o in range(nz):
        kv_across(o).wait_recv()

    scale = 1.0 / math.sqrt(HD)
    S = kvs.shape[0]
    lane = lax.broadcasted_iota(jnp.int32, (TQ, 128), 1)

    def pair(k, _):
        j = near_first(k, at.z, nz)
        g = gq(k)
        g.finish_any()
        qpre = dot_nn(xn1[...], wq[j])
        for hh in range(HC // HD):
            u = qpre[:, hh * HD:(hh + 1) * HD]
            qs[:, pl.ds(pl.multiple_of(j * HC + hh * HD, HD), HD)] = (u * cosf[...] + swap_halves(u) * sins[...]).astype(LOW)

        def head(i, _):
            hh, tq = lax.rem(i, HC // HD), i // (HC // HD)
            rr = pl.ds(pl.multiple_of(tq * TQ, TQ), TQ)
            cols = pl.ds(pl.multiple_of(j * HC + hh * HD, HD), HD)
            s = dot_nt(qs[rr, cols], kvs[:, pl.ds(0, HD)])
            place = lax.broadcasted_iota(jnp.int32, (TQ, S), 1)
            here = at.z * 2 * R + tq * TQ + lax.broadcasted_iota(jnp.int32, (TQ, 1), 0)
            s = jnp.where((place >= lo_in[rr, :]) & (place <= here), s * scale, MASKED)
            m = jnp.max(s, axis=-1, keepdims=True)
            p = jnp.exp(s - m)
            total = jnp.sum(p, axis=-1, keepdims=True)
            att = dot_nn(p.astype(LOW), kvs[:, pl.ds(HD, HD)])
            os_[rr, cols] = (att / total).astype(LOW)
            hid = j * (HC // HD) + hh
            lse_out[rr, :] = jnp.where(lane == hid, m + jnp.log(total), lse_out[rr, :])
            return 0

        lax.fori_loop(0, (HC // HD) * (2 * R // TQ), head, 0)
        go(k).forward_any()
        return 0

    lse_out[...] = jnp.zeros_like(lse_out)
    lax.fori_loop(0, nz, pair, 0)
    for g in gw:
        g.start()
    ldy.step(1)
    keep = [
        pltpu.make_async_copy(xn1, xn1_out, outs.at[0]),
        pltpu.make_async_copy(wq, wq_out, outs.at[1]),
        pltpu.make_async_copy(wkv, wkv_out, outs.at[2]),
        pltpu.make_async_copy(kvs, kv_out, outs.at[3]),
        pltpu.make_async_copy(qs, q_out, outs.at[4]),
        pltpu.make_async_copy(os_, o_out, outs.at[5]),
    ]
    for cp in keep:
        cp.start()

    lax.fori_loop(0, nz, lambda k, _: (go(k).finish_any(), 0)[1], 0)
    keep.append(pltpu.make_async_copy(wo, wo_out, outs.at[6]))
    keep[-1].start()
    theirs = rows(1 - at.c)
    for o in range(nd):
        pback[:, pl.ds(o * Dd, Dd)] = dot_nn(os_[theirs, :], wo[o]).astype(LOW)
    back = remote(pback, precv, cs.at[1], cr.at[1], at.dp, at.sibling())
    back.start()
    for o in range(nd):
        cols = pl.ds(o * Dd, Dd)
        h1_out[:, cols] = tok[:, cols].astype(F32) + dot_nn(os_[mine, :], wo[o])
    back.wait_recv()
    h1_out[...] = h1_out[...] + precv[...].astype(F32)

    def put_xn2(cols, v):
        xn2_out[:, cols] = v

    scaled(h1_out[...], 1, put_xn2)
    for g in gw:
        g.forward()
    for s in range(2, nz):
        ldy.step(s)
    for g in gw:
        g.finish()
    for o in range(nz):
        dy_across(o).wait_recv()
    for cp in for_mlp[1:]:
        cp.wait()
    for g in gw:
        g.drain()
    ldy.drain()

    for s in range(1, nd):
        gain_copy(s).wait_send()
    for g in gkv:
        g.drain()
    xn1_across.wait_send()
    back.wait_send()
    lq.drain()
    lo.drain()
    lkv.drain()

    def drain(k, _):
        gq(k).drain_any()
        go(k).drain_any()
        return 0

    lax.fori_loop(0, nz, drain, 0)
    for cp in keep:
        cp.wait()


def attend(nd, nt, tok, gain, wq, wkv, wo, cosf, sins, lo, dy, w):
    R, D = tok.shape
    Dd, HC = wq.shape
    S = R * nt
    nz, ny = nt // 2, nd // 2
    dma = lambda *s: pltpu.SemaphoreType.DMA(s)
    hbm = pl.BlockSpec(memory_space=pltpu.HBM)
    vm = pl.BlockSpec(memory_space=pltpu.VMEM)
    shapes = [((R, D), F32), ((R, D), LOW), ((nd, 8, Dd), F32), ((2 * R, 128), F32),
              ((2 * R, D), LOW), ((nz, D, HC), LOW), ((nd, nz * HC, Dd), LOW), ((D, 2 * HD), LOW), ((S, 2 * HD), LOW),
              ((2 * R, nz * HC), LOW), ((2 * R, nz * HC), LOW)]
    gathered = [((S, D), LOW), ((2, w.shape[1], D), LOW)]
    yg = lambda n: [dma(n), dma(n, ny - 1), dma(n, ny - 1), dma(n, ny - 1), dma(n, nd)]
    return pl.pallas_call(
        functools.partial(attend_kernel, nd, nt),
        out_shape=tuple(jax.ShapeDtypeStruct(*s) for s in shapes + gathered),
        in_specs=[vm, vm, hbm, hbm, hbm, vm, vm, vm, hbm, hbm],
        out_specs=(vm, vm, vm, vm) + (hbm,) * 9,
        scratch_shapes=[pltpu.VMEM(*s) for s in shapes[4:]] + [pltpu.VMEM((R, D), LOW), pltpu.VMEM((R, D), LOW)]
        + [dma(3), dma(nd - 1), dma(nd - 1)] + yg(2) + yg(nz) + yg(nz)
        + [dma(nz)] * 3 + [dma(nz)] * 3 + [dma(nz)] * 5 + [dma(2), dma(2), dma(7)]
        + [dma(nz), dma(nz), dma(2, nz), dma(nz)] + yg(2) + [dma(3)],
        compiler_params=pltpu.CompilerParams(collective_id=2, has_side_effects=True, vmem_limit_bytes=63 << 20),
        cost_estimate=pl.CostEstimate(flops=20 << 30, bytes_accessed=40 << 20, transcendentals=8 * 512 * 2048),
        name="attend",
    )(tok, gain, wq, wkv, wo, cosf, sins, lo, dy, w)


class Scatter:
    def __init__(self, at, kind, view, land, land2, ss, rs, ss2, rs2):
        self.at, self.kind, self.view = at, kind, view
        self.land, self.land2 = land, land2
        self.ss, self.rs, self.ss2, self.rs2 = ss, rs, ss2, rs2

    def first(self):
        at = self.at
        out = []
        if self.kind == 0:
            for s in range(1, at.ny):
                for xx in range(at.nx):
                    slot = (s - 1) * at.nx + xx
                    o = lax.rem(at.y + s, at.ny) * at.nx + xx
                    out.append(remote(self.view(o), self.land(slot), self.ss.at[slot], self.rs.at[slot], at.y_peer(s), at.t))
        else:
            for yy in range(at.ny):
                o = yy * at.nx + 1 - at.x
                out.append(remote(self.view(o), self.land(yy), self.ss.at[yy], self.rs.at[yy], at.x_peer(), at.t))
        return out

    def second(self):
        at = self.at
        if self.kind == 0:
            return [remote(self.view(at.x_peer()), self.land2(0), self.ss2.at[0], self.rs2.at[0], at.x_peer(), at.t)]
        return [remote(self.view(at.y_peer(s)), self.land2(s - 1), self.ss2.at[s - 1], self.rs2.at[s - 1], at.y_peer(s), at.t)
                for s in range(1, at.ny)]

    def start(self):
        for cp in self.first():
            cp.start()

    def add(self, o, slots):
        total = self.view(o)[...].astype(F32)
        for slot in slots:
            total = total + self.land(slot)[...].astype(F32)
        self.view(o)[...] = total.astype(LOW)

    def middle(self):
        at = self.at
        for cp in self.first():
            cp.wait_recv()
        if self.kind == 0:
            self.add(at.x_peer(), [(s - 1) * at.nx + 1 - at.x for s in range(1, at.ny)])
        else:
            for s in range(1, at.ny):
                self.add(at.y_peer(s), [lax.rem(at.y + s, at.ny)])
        for cp in self.second():
            cp.start()
        if self.kind == 0:
            self.add(at.dp, [(s - 1) * at.nx + at.x for s in range(1, at.ny)])
        else:
            self.add(at.dp, [at.y])

    def total(self):
        total = self.view(self.at.dp)[...].astype(F32)
        for i, cp in enumerate(self.second()):
            cp.wait_recv()
            total = total + self.land2(i)[...].astype(F32)
        return total

    def drain(self):
        for cp in self.first() + self.second():
            cp.wait_send()

    def either(self, name, put=None):
        kind = self.kind
        for value in range(2):
            self.kind = value
            call = getattr(self, name)
            if put is None:
                pl.when(kind == value)(call)
            else:
                pl.when(kind == value)(lambda call=call: put(call()))
        self.kind = kind


def grads_kernel(nd, nt, dy, tok, gfull, cosf, sins, lo_row, lse, later,
                 h1_in, dxn2_in, xn1_in, wq_in, wo_in, wkv_in, kv_in, q_in, o_in,
                 mine_g, land_g, mine_u, land_u, down_in,
                 tgrad, gq_out, go_out, gkv_out, gg_out, norm_out, keep_g, keep_u, keep_d, keep_e, got_g, got_u, got_d, got_e,
                 xn1, wq, wo, wkv, kvs, qs, os_, dos, dh1b, dxn1, lset, dkv, dq,
                 bg, bu, bd, be, lg, lu, ld, le, tg, tu, td, te,
                 ql, ql2, ol, ol2, qz, oz, qlz, olz, kvb, kland, kz, xrecv, wl, wcl, wd2, w2, w2l, wfin, gl, gpart, u2, u2l, gfin, share, norms, normd,
                 lsem, xsem, fs, fr, qss, qsr, qss2, qsr2, oss, osr, oss2, osr2, qzs, qzr, ozs, ozr,
                 ks, kr, kzs, kzr, ws, wr, wcs, wcr, w2s, w2r, w3s, w3r, us, ur, u2s, u2r, u3s, u3r, ns, nr, n2s, n2r, outs, hs, hr):
    at = Place(nd, nt)
    nz, nx, ny = at.nz, at.nx, at.ny
    R, D = tok.shape
    Dd = wo.shape[2]
    HC = wq.shape[2]
    Ds = wl.shape[1]
    NH = HC // HD
    KT = 2 * R
    S = kvs.shape[0]
    rows = lambda t: pl.ds(pl.multiple_of(t * R, R), R)
    drows = lambda o: pl.ds(pl.multiple_of(o * Dd, Dd), Dd)
    hcols = lambda j: pl.ds(pl.multiple_of(j * HC, HC), HC)
    mine, theirs = rows(at.c), rows(1 - at.c)
    scale = 1.0 / math.sqrt(HD)

    Fh = bd.shape[1]
    pieces = [(bg, mine_g), (bu, mine_u), (tg, land_g), (tu, land_u),
              (wo, wo_in), (os_, o_in), (qs, q_in), (kvs, kv_in), (xn1, xn1_in), (wq, wq_in), (wkv, wkv_in),
              (dxn1.at[pl.ds(0, R)], h1_in), (xrecv, dxn2_in)]
    down = lambda n, o: down_in.at[pl.ds(n * Fh, Fh), drows(o)]
    pieces += [(bd.at[xx], down(0, at.y * nx + xx)) for xx in range(nx)]
    pieces += [(be.at[yy], down(1, yy * nx + at.x)) for yy in range(ny)]
    loads = [pltpu.make_async_copy(src, dst, lsem.at[i]) for i, (dst, src) in enumerate(pieces)]
    for cp in loads[11:13] + loads[:11] + loads[13:]:
        cp.start()
    greet_all(at)

    down_hops = []
    for s in range(1, ny):
        for xx in range(nx):
            slot = (s - 1) * nx + xx
            o = lax.rem(at.y + s, ny) * nx + xx
            down_hops.append(remote(down(0, o), td.at[slot], hs.at[0, slot], hr.at[0, slot], at.y_peer(s), at.t))
    for yy in range(ny):
        down_hops.append(remote(down(1, yy * nx + 1 - at.x), te.at[yy], hs.at[1, yy], hr.at[1, yy], at.x_peer(), at.t))
    for cp in down_hops:
        cp.start()

    def rms_back(v_of, e_of, row, put):
        chunks = [pl.ds(o * Dd, Dd) for o in range(nd)]
        squares = jnp.zeros((R, 1), F32)
        inner = jnp.zeros((R, 1), F32)
        for o, cols in enumerate(chunks):
            v = v_of(cols)
            squares = squares + jnp.sum(v * v, axis=-1, keepdims=True)
            inner = inner + jnp.sum(e_of(cols) * gfull[o, row:row + 1, :] * v, axis=-1, keepdims=True)
        r = lax.rsqrt(squares / D + EPSILON)
        inner = inner * (r * r * r) / D
        for o, cols in enumerate(chunks):
            v, e = v_of(cols), e_of(cols)
            gpart[row:row + 1, cols] = jnp.sum(e * v * r, axis=0, keepdims=True)
            put(cols, r * (e * gfull[o, row:row + 1, :]) - v * inner)

    gpart[...] = jnp.zeros_like(gpart)

    def put_dh1(cols, v):
        total = dy[:, cols].astype(F32) + v
        tgrad[:, cols] = total
        dh1b[mine, cols] = total.astype(LOW)

    loads[11].wait()
    loads[12].wait()
    rms_back(lambda cols: dxn1[pl.ds(0, R), cols], lambda cols: xrecv[:, cols].astype(F32), 1, put_dh1)
    swap_dh1 = remote(dh1b.at[mine], dh1b.at[mine], xsem.at[0], xsem.at[1], at.dp, at.sibling())
    swap_dh1.start()

    for i in range(4, 11):
        loads[i].wait()
    swap_dh1.wait_recv()
    def do_pair(j, _):
        acc = dot_nt(dh1b[:, pl.ds(0, Dd)], wo[0, hcols(j), :])
        for o in range(1, nd):
            acc = acc + dot_nt(dh1b[:, pl.ds(o * Dd, Dd)], wo[o, hcols(j), :])
        dos[:, hcols(j)] = acc.astype(LOW)
        return 0

    lax.fori_loop(0, nz, do_pair, 0)

    def kind_of(k):
        return k % 2 if isinstance(k, int) else lax.rem(k, 2)

    def so(k):
        j = far_first(k, at.z, nz)
        return Scatter(at, kind_of(k), lambda o: wo.at[o, hcols(j)], lambda i: ol.at[k, i], lambda i: ol2.at[k, i],
                       oss.at[k], osr.at[k], oss2.at[k], osr2.at[k])

    def sq(k):
        j = far_first(k, at.z, nz)
        return Scatter(at, kind_of(k), lambda o: wq.at[j, drows(o)], lambda i: ql.at[k, i], lambda i: ql2.at[k, i],
                       qss.at[k], qsr.at[k], qss2.at[k], qsr2.at[k])

    def wo_unit(k, _):
        j = far_first(k, at.z, nz)

        def part(o, _):
            wo[o, hcols(j), :] = dot_tn(os_[:, hcols(j)], dh1b[:, drows(o)]).astype(LOW)
            return 0

        lax.fori_loop(0, nd, part, 0)
        so(k).either("start")
        return 0

    lax.fori_loop(0, nz, wo_unit, 0)

    def zpush(k, buf, land, ss, rs):
        j = far_first(k, at.z, nz)
        return remote(buf.at[k], land.at[at.z], ss.at[k], rs.at[at.z], at.dp, 2 * j + at.c)

    def o_total(k):
        def put(v):
            oz[k] = v.astype(LOW)

        so(k).either("total", put)
        pl.when(k < nz - 1)(lambda: zpush(k, oz, olz, ozs, ozr).start())

    def q_total(k):
        def put(v):
            qz[k] = v.astype(LOW)

        sq(k).either("total", put)
        pl.when(k < nz - 1)(lambda: zpush(k, qz, qlz, qzs, qzr).start())

    lset[...] = lse[...].T
    dkv[...] = jnp.zeros_like(dkv)
    dxn1[...] = jnp.zeros_like(dxn1)
    here = at.z * KT + lax.broadcasted_iota(jnp.int32, (1, KT), 1)
    low_row = lo_row[0:1, :]

    def unit(k, _):
        j = far_first(k, at.z, nz)
        for hh in range(NH):
            cols = pl.ds(pl.multiple_of(j * HC + hh * HD, HD), HD)
            hid = j * NH + hh
            lrow = lset[pl.ds(hid, 1), :]
            qh = qs[:, cols]
            doh = dos[:, cols]
            delta = jnp.sum((doh.astype(F32) * os_[:, cols].astype(F32)).T, axis=0, keepdims=True)
            dq[...] = jnp.zeros_like(dq)

            def tile(b, _):
                kr_ = pl.ds(pl.multiple_of(b * KT, KT), KT)
                kt = kvs[kr_, pl.ds(0, HD)]
                vt = kvs[kr_, pl.ds(HD, HD)]
                s = dot_nt(kt, qh)
                place = b * KT + lax.broadcasted_iota(jnp.int32, (KT, KT), 0)
                s = jnp.where((place >= low_row) & (place <= here), s * scale, MASKED)
                p = jnp.exp(s - lrow)
                dkv[kr_, pl.ds(HD, HD)] += dot_nn(p.astype(LOW), doh)
                ds = (p * (dot_nt(vt, doh) - delta)).astype(LOW)
                dkv[kr_, pl.ds(0, HD)] += dot_nn(ds, qh)
                dq[...] += dot_tn(ds, kt)
                return 0

            lax.fori_loop(0, at.z + 1, tile, 0)
            u = dq[...] * scale
            qs[:, cols] = (u * cosf[...] - swap_halves(u) * sins[...]).astype(LOW)
        dqp = qs[:, hcols(j)]

        def back(o, _):
            dxn1[:, drows(o)] += dot_nt(dqp, wq[j, drows(o), :])
            wq[j, drows(o), :] = dot_tn(xn1[:, drows(o)], dqp).astype(LOW)
            return 0

        lax.fori_loop(0, nd, back, 0)
        sq(k).either("start")
        pl.when(k >= 1)(lambda: so(k - 1).either("middle"))
        pl.when(k >= 2)(lambda: o_total(k - 2))
        return 0

    lax.fori_loop(0, nz, unit, 0)

    dkv[:, pl.ds(0, HD)] = dkv[:, pl.ds(0, HD)] * scale
    kvb[...] = dkv[...].astype(LOW)
    kswap = [remote(kvb.at[rows(2 * zz + 1 - at.c)], kland.at[zz], ks.at[zz], kr.at[zz], at.dp, at.sibling()) for zz in range(nz)]
    for cp in kswap:
        cp.start()
    swap_dh1.wait_send()
    dh1b[mine, :] = dxn1[theirs, :].astype(LOW)
    xswap = remote(dh1b.at[mine], xrecv, xsem.at[2], xsem.at[3], at.dp, at.sibling())
    xswap.start()

    def kpush(s):
        zz = lax.rem(at.z + s, nz)
        return remote(kvb.at[rows(2 * zz + at.c)], kz.at[s - 1], kzs.at[s - 1], kzr.at[s - 1], at.dp, 2 * zz + at.c)

    k_last = jnp.int32(nz - 1)
    so(k_last).either("middle")
    for s in range(1, nz + 1):
        zz = lax.rem(at.z + s, nz)
        r = rows(2 * zz + at.c)
        remote(kvb.at[rows(0)], kland.at[zz], ks.at[zz], kr.at[zz], at.dp, at.sibling()).wait_recv()
        dkv[r, :] = dkv[r, :] + kland[zz].astype(F32)
        if s < nz:
            kvb[r, :] = dkv[r, :].astype(LOW)
            kpush(s).start()

    lax.fori_loop(0, max(nz - 2, 1), lambda k, _: (sq(k).either("middle"), 0)[1], 0)
    if nz >= 2:
        o_total(jnp.int32(nz - 2))
    total = dkv[rows(at.t), :] + later[...].astype(F32)
    for s in range(1, nz):
        kpush(s).wait_recv()
        total = total + kz[s - 1].astype(F32)
    dk = total[:, :HD]
    dk = dk * cosf[mine, :] - swap_halves(dk) * sins[mine, :]
    dkvp = jnp.concatenate([dk, total[:, HD:]], axis=1).astype(LOW)


    slices = lambda t: pl.ds(pl.multiple_of(t * Ds, Ds), Ds)

    def wswap(zz):
        return remote(wd2.at[slices(2 * zz + 1 - at.c)], wcl.at[zz], wcs.at[zz], wcr.at[zz], at.dp, at.sibling())

    def wpush(s):
        zz = lax.rem(at.z + s, nz)
        return remote(wd2.at[slices(2 * zz + at.c)], wl.at[s - 1], ws.at[s - 1], wr.at[s - 1], at.dp, 2 * zz + at.c)

    def upush(s):
        tt = lax.rem(at.t + s, nt)
        return remote(gpart.at[:, slices(tt)], gl.at[at.t], us.at[s - 1], ur.at[at.t], at.dp, tt)

    for o in range(nd):
        wd2[pl.ds(o * Dd, Dd), :] = dot_tn(xn1[mine, pl.ds(o * Dd, Dd)], dkvp).astype(LOW)
    for zz in range(nz):
        wswap(zz).start()
    lax.fori_loop(max(nz - 2, 1), nz, lambda k, _: (sq(k).either("middle"), 0)[1], 0)
    big = []
    for n, (buf, got, second) in enumerate([(bg, tg, lg), (bu, tu, lu), (bd, td, ld), (be, te, le)]):
        if n < 2:
            loads[n].wait()
            loads[2 + n].wait()
        elif n == 2:
            for cp in loads[13:]:
                cp.wait()
            for cp in down_hops:
                cp.wait_recv()
        if n % 2 == 0:
            keep, keep_slots = at.x, [(s - 1) * nx + at.x for s in range(1, ny)]
            away = [(1 - at.x, [(s - 1) * nx + 1 - at.x for s in range(1, ny)], at.x_peer())]
        else:
            keep, keep_slots = at.y, [at.y]
            away = [(lax.rem(at.y + s, ny), [lax.rem(at.y + s, ny)], at.y_peer(s)) for s in range(1, ny)]
        copies = []
        for i, (place, slots, peer) in enumerate(away):
            total = buf[place].astype(F32)
            for slot in slots:
                total = total + got[slot].astype(F32)
            buf[place] = total.astype(LOW)
            copies.append(remote(buf.at[place], second.at[i], fs.at[n, i], fr.at[n, i], peer, at.t))
            copies[-1].start()
        total = buf[keep].astype(F32)
        for slot in keep_slots:
            total = total + got[slot].astype(F32)
        buf[keep] = total.astype(LOW)
        big.append((buf, keep, second, copies))

    for s in range(1, nz + 1):
        zz = lax.rem(at.z + s, nz)
        r = slices(2 * zz + at.c)
        remote(wd2.at[slices(0)], wcl.at[zz], wcs.at[zz], wcr.at[zz], at.dp, at.sibling()).wait_recv()
        wd2[r, :] = (wd2[r, :].astype(F32) + wcl[zz].astype(F32)).astype(LOW)
        if s < nz:
            wpush(s).start()
    o_total(k_last)

    xswap.wait_recv()
    for o in range(nd):
        cols = pl.ds(o * Dd, Dd)
        dxn1[mine, cols] = dxn1[mine, cols] + xrecv[:, cols].astype(F32) + dot_nt(dkvp, wkv[cols, :])

    def put_tokens(cols, v):
        tgrad[:, cols] = tgrad[:, cols] + v

    rms_back(lambda cols: tok[:, cols].astype(F32), lambda cols: dxn1[mine, cols], 0, put_tokens)
    for s in range(1, nt):
        upush(s).start()

    lax.fori_loop(0, max(nz - 2, 1), lambda k, _: (q_total(k), 0)[1], 0)

    per = nt // nd
    gl[at.t] = gpart[:, slices(at.t)]
    wsum = wd2[slices(at.t), :].astype(F32)
    for s in range(1, nz):
        wpush(s).wait_recv()
        wsum = wsum + wl[s - 1].astype(F32)
    for s in range(1, nt):
        o = lax.rem(at.t + s, nt)
        remote(gpart.at[:, pl.ds(0, Ds)], gl.at[o], us.at[s - 1], ur.at[o], at.dp, o).wait_recv()
    usum = gl[0]
    for o in range(1, nt):
        usum = usum + gl[o]
    owner = at.t // per
    is_owner = at.dp == owner
    slot = jnp.where(is_owner, at.t - at.dp * per, 0)
    w2[...] = wsum.astype(LOW)
    u2[...] = usum
    to = jnp.where(is_owner, lax.rem(at.dp + 1, nd), owner)
    give_w = remote(w2, w2l.at[at.dp], w2s.at[0], w2r.at[at.dp], to, at.t)
    give_u = remote(u2, u2l.at[at.dp], u2s.at[0], u2r.at[at.dp], to, at.t)

    def spread(q, i, t):
        return [remote(wfin.at[q], wfin.at[q], w3s.at[q, i], w3r.at[q], at.dp, t),
                remote(gfin.at[q], gfin.at[q], u3s.at[q, i], u3r.at[q], at.dp, t)]

    def spread_along(s):
        return spread(slot, s, 2 * lax.rem(at.z + s, nz) + at.c)

    @pl.when(jnp.logical_not(is_owner))
    def _():
        give_w.start()
        give_u.start()

    lax.fori_loop(max(nz - 2, 1), nz, lambda k, _: (q_total(k), 0)[1], 0)

    def square(v):
        return jnp.sum(v * v, axis=(0, 1), keepdims=True)

    share[...] = jnp.zeros_like(share)

    @pl.when(is_owner)
    def _():
        w2l[at.dp] = w2[...]
        u2l[at.dp] = u2[...]
        for s in range(1, nd):
            o = lax.rem(at.dp + s, nd)
            remote(w2, w2l.at[o], w2s.at[0], w2r.at[o], o, at.t).wait_recv()
            remote(u2, u2l.at[o], u2s.at[0], u2r.at[o], o, at.t).wait_recv()
        wtot = w2l[0].astype(F32)
        utot = u2l[0]
        for o in range(1, nd):
            wtot = wtot + w2l[o].astype(F32)
            utot = utot + u2l[o]
        wfin[slot] = wtot.astype(LOW)
        gfin[slot] = utot
        shared = square(wtot.astype(LOW).astype(F32)) + square(utot)
        share[...] = jnp.broadcast_to(shared, share.shape)
        for s in range(1, nz):
            for cp in spread_along(s):
                cp.start()

    squares = jnp.zeros((1, 1), F32)
    out_copies = []
    for n, (buf, keep, second, copies) in enumerate(big):
        total = buf[keep].astype(F32)
        for i, cp in enumerate(copies):
            cp.wait_recv()
            total = total + second[i].astype(F32)
        squares = squares + square(total)
        out_copies.append(pltpu.make_async_copy(second, (got_g, got_u, got_d, got_e)[n], outs.at[n]))
        out_copies.append(pltpu.make_async_copy(buf.at[keep], (keep_g, keep_u, keep_d, keep_e)[n], outs.at[4 + n]))
        for cp in out_copies[-2:]:
            cp.start()
    own_k = nz - 1
    for buf, land, ss, rs, out in ((oz, olz, ozs, ozr, go_out), (qz, qlz, qzs, qzr, gq_out)):
        total = buf[own_k].astype(F32)
        for s in range(1, nz):
            zz = lax.rem(at.z + s, nz)
            remote(buf.at[0], land.at[zz], ss.at[0], rs.at[zz], at.dp, at.sibling()).wait_recv()
            total = total + land[zz].astype(F32)
        squares = squares + square(total)
        out[...] = total
    squares = squares + share[0:1, 0:1]

    norms[at.t] = jnp.broadcast_to(squares, norms.shape[1:])

    def npush(s):
        return remote(norms.at[at.t], norms.at[at.t], ns.at[s - 1], nr.at[at.t], at.dp, lax.rem(at.t + s, nt))

    def n2push(s):
        return remote(normd.at[at.dp], normd.at[at.dp], n2s.at[s - 1], n2r.at[at.dp], lax.rem(at.dp + s, nd), at.t)

    for s in range(1, nt):
        npush(s).start()
    for s in range(1, nt):
        o = lax.rem(at.t + s, nt)
        remote(norms.at[o], norms.at[o], ns.at[s - 1], nr.at[o], at.dp, o).wait_recv()
    group = norms[0]
    for o in range(1, nt):
        group = group + norms[o]
    normd[at.dp] = group
    for s in range(1, nd):
        n2push(s).start()
    for s in range(1, nd):
        o = lax.rem(at.dp + s, nd)
        remote(normd.at[o], normd.at[o], n2s.at[s - 1], n2r.at[o], o, at.t).wait_recv()
    group = normd[0]
    for o in range(1, nd):
        group = group + normd[o]
    norm_out[...] = jnp.sqrt(group)

    for q in range(per):
        t_from = at.dp * per + q
        same = at.c == lax.rem(t_from, 2)

        def slice_came(q=q):
            for cp in spread(q, 0, at.sibling()):
                cp.wait_recv()

        pl.when(at.t != t_from)(slice_came)

        @pl.when(same)
        def _(q=q):
            for cp in spread(q, 0, at.sibling()):
                cp.start()

        gkv_out[pl.ds(q * Ds, Ds), :] = wfin[q].astype(F32)
        gg_out[:, pl.ds(q * Ds, Ds)] = gfin[q]

        @pl.when(same)
        def _(q=q):
            for cp in spread(q, 0, at.sibling()):
                cp.wait_send()

    for cp in out_copies:
        cp.wait()
    for cp in down_hops:
        cp.wait_send()
    xswap.wait_send()
    for _, _, _, copies in big:
        for cp in copies:
            cp.wait_send()
    for cp in kswap:
        cp.wait_send()
    for s in range(1, nz):
        kpush(s).wait_send()
    for zz in range(nz):
        wswap(zz).wait_send()
    for s in range(1, nz):
        wpush(s).wait_send()
    for s in range(1, nt):
        upush(s).wait_send()
        npush(s).wait_send()
    for s in range(1, nd):
        n2push(s).wait_send()

    def drain(k, _):
        so(k).either("drain")
        sq(k).either("drain")

        @pl.when(k < nz - 1)
        def _():
            zpush(k, oz, olz, ozs, ozr).wait_send()
            zpush(k, qz, qlz, qzs, qzr).wait_send()

        return 0

    lax.fori_loop(0, nz, drain, 0)

    @pl.when(jnp.logical_not(is_owner))
    def _():
        give_w.wait_send()
        give_u.wait_send()

    @pl.when(is_owner)
    def _():
        for s in range(1, nz):
            for cp in spread_along(s):
                cp.wait_send()


def grads(nd, nt, small, big_in, pieces):
    R, D = small[1].shape
    nz, ny = nt // 2, nd // 2
    h1, dxn2, xn1, wq, wo, wkv, kv, q, o = big_in
    Dd, HC = wo.shape[2], wq.shape[2]
    F = pieces[0].shape[1]
    Fh = F // 2
    S = R * nt
    Ds = D // nt
    W2 = 2 * HD
    slots = max(2 * (ny - 1), ny)
    hops = max(1, ny - 1)
    dma = lambda *s: pltpu.SemaphoreType.DMA(s)
    hbm = pl.BlockSpec(memory_space=pltpu.HBM)
    vm = pl.BlockSpec(memory_space=pltpu.VMEM)
    b = lambda *s: pltpu.VMEM(s, LOW)
    f = lambda *s: pltpu.VMEM(s, F32)
    shapes = [(R, D), (Dd, HC), (HC, Dd), (Dd, W2), (8, Dd), (8, 128)]
    lows = [(F, Dd), (F, Dd), (Fh, Dd), (Fh, Dd), (1, F, Dd), (hops, F, Dd), (1, Fh, Dd), (hops, Fh, Dd)]
    return pl.pallas_call(
        functools.partial(grads_kernel, nd, nt),
        out_shape=tuple([jax.ShapeDtypeStruct(s, F32) for s in shapes] + [jax.ShapeDtypeStruct(s, LOW) for s in lows]),
        in_specs=[vm] * 8 + [hbm] * 14,
        out_specs=(vm,) * 6 + (hbm,) * 8,
        scratch_shapes=[
            b(2 * R, D), b(nz, D, HC), b(nd, nz * HC, Dd), b(D, W2), b(S, W2), b(2 * R, nz * HC), b(2 * R, nz * HC), b(2 * R, nz * HC),
            b(2 * R, D), f(2 * R, D), f(128, 2 * R), f(S, W2), f(2 * R, HD),
            b(2, F, Dd), b(ny, F, Dd), b(2, Fh, Dd), b(ny, Fh, Dd),
            b(1, F, Dd), b(hops, F, Dd), b(1, Fh, Dd), b(hops, Fh, Dd),
            b(2 * (ny - 1), F, Dd), b(ny, F, Dd), b(2 * (ny - 1), Fh, Dd), b(ny, Fh, Dd),
            b(nz, slots, Dd, HC), b(nz, hops, Dd, HC), b(nz, slots, HC, Dd), b(nz, hops, HC, Dd),
            b(nz, Dd, HC), b(nz, HC, Dd), b(nz, Dd, HC), b(nz, HC, Dd),
            b(S, W2), b(nz, R, W2), b(nz, R, W2), b(R, D),
            b(nz, Ds, W2), b(nz, Ds, W2), b(D, W2), b(Ds, W2), b(nd, Ds, W2), b(nt // nd, Ds, W2),
            f(nt, 8, Ds), f(8, D), f(8, Ds), f(nd, 8, Ds), f(nt // nd, 8, Ds), f(8, 128), f(nt, 8, 128), f(nd, 8, 128),
            dma(13 + 2 + ny), dma(4), dma(4, hops), dma(4, hops),
            dma(nz, slots), dma(nz, slots), dma(nz, hops), dma(nz, hops), dma(nz, slots), dma(nz, slots), dma(nz, hops), dma(nz, hops),
            dma(nz), dma(nz), dma(nz), dma(nz),
            dma(nz), dma(nz), dma(nz), dma(nz),
            dma(nz), dma(nz), dma(nz), dma(nz), dma(1), dma(nd), dma(nt // nd, nz), dma(nt // nd),
            dma(nt), dma(nt), dma(1), dma(nd), dma(nt // nd, nz), dma(nt // nd),
            dma(nt), dma(nt), dma(nd), dma(nd), dma(8), dma(2, slots), dma(2, slots),
        ],
        compiler_params=pltpu.CompilerParams(collective_id=3, has_side_effects=True, vmem_limit_bytes=63 << 20),
        cost_estimate=pl.CostEstimate(flops=30 << 30, bytes_accessed=40 << 20, transcendentals=8 * 512 * 2048),
        name="grads",
    )(*small, *big_in, *pieces)


def advance(grad_raw, weight, moment, average, factor, rate):
    average_decay = min(AVERAGE_TOP, (1.0 + STEP) / (10.0 + STEP))
    clipped = grad_raw * factor
    moment_new = MOMENTUM * moment + clipped
    weight_new = weight - rate * (clipped + MOMENTUM * moment_new)
    average_new = average_decay * average + (1.0 - average_decay) * weight_new
    return (clipped, moment_new, average_new, weight_new, weight_new.astype(jnp.bfloat16))


def local(
    tokens,
    cotangent,
    kv_later,
    lengths,
    query_weight,
    query_moment,
    query_average,
    keyvalue_weight,
    keyvalue_moment,
    keyvalue_average,
    output_weight,
    output_moment,
    output_average,
    gateup_weight,
    gateup_moment,
    gateup_average,
    down_weight,
    down_moment,
    down_average,
    norm_gains,
    gains_moment,
    gains_average,
):
    masters = (query_weight, keyvalue_weight, output_weight, gateup_weight, down_weight, norm_gains)
    low_query, low_kv, low_output, _, _, low_gains = (w.astype(LOW) for w in masters)
    low_gateup = jnp.swapaxes(gateup_weight, 1, 2).astype(LOW)
    low_down = down_weight.astype(LOW)
    nd, nt = lax.axis_size("dp"), lax.axis_size("tensor")
    row_count = tokens.shape[0]
    pair_rows = 2 * row_count

    doc_lengths = lengths[0]
    endings = jnp.cumsum(doc_lengths)
    beginnings = endings - doc_lengths
    places = (lax.axis_index("tensor") // 2) * pair_rows + jnp.arange(pair_rows, dtype=jnp.int32)
    segment = jnp.sum((places[:, None] >= endings[None, :]).astype(jnp.int32), axis=1)
    picked = segment[:, None] == jnp.arange(doc_lengths.shape[0], dtype=jnp.int32)[None, :]
    first = jnp.sum(jnp.where(picked, beginnings[None, :], 0), axis=1).astype(jnp.int32)
    half_size = HD // 2
    frequency = jnp.exp(jnp.arange(half_size, dtype=F32) * (-2.0 * math.log(ROPE_BASE) / HD))
    angles = (places - first).astype(F32)[:, None] * frequency[None, :]
    cosine, sine = jnp.cos(angles), jnp.sin(angles)
    cosine_full = jnp.concatenate([cosine, cosine], axis=1)
    sine_full = jnp.concatenate([-sine, sine], axis=1)
    gain_rows = jnp.pad(low_gains.astype(F32), ((0, 6), (0, 0)))

    hidden_one, normed_two, gains_all, lse, normed_one, all_query, all_output, all_kv, kv_rows, queries, attended, grad_rows, gate_up = attend(
        nd, nt, tokens, gain_rows, low_query, low_kv, low_output, cosine_full, sine_full, first[:, None],
        cotangent, low_gateup
    )
    grad_normed_two, *pieces, mlp_rows = mlp(nd, nt, normed_two, grad_rows, gate_up, low_down)
    cores = [list(range(core, nt, 2)) for core in range(2)]
    mlp_own = lax.psum_scatter(mlp_rows, "tensor", scatter_dimension=0, axis_index_groups=cores, tiled=False)
    mixed = hidden_one + mlp_own.astype(F32)
    tokens_grad, own_query, own_output, grad_keyvalue, gains_sum, norm_tile, *halves = grads(
        nd,
        nt,
        (cotangent, tokens, gains_all, cosine_full, sine_full, jnp.broadcast_to(first[None, :], (8, pair_rows)), lse, kv_later),
        (hidden_one, grad_normed_two, normed_one, all_query, all_output, all_kv, kv_rows, queries, attended),
        pieces,
    )
    whole = [kept.astype(F32) + jnp.sum(got.astype(F32), axis=0) for kept, got in zip(halves[:4], halves[4:])]
    own_gateup = jnp.swapaxes(jnp.stack(whole[:2]), 1, 2)
    own_down = jnp.concatenate(whole[2:], axis=0)
    grad_gains = gains_sum[:2]
    grad_norm = norm_tile[0, 0]
    factor = jnp.minimum(1.0, CLIP / (grad_norm + 1e-06))
    query_set = advance(
        own_query, query_weight, query_moment, query_average, factor, LEARNING_RATES[0]
    )
    keyvalue_set = advance(
        grad_keyvalue, keyvalue_weight, keyvalue_moment, keyvalue_average, factor, LEARNING_RATES[1]
    )
    output_set = advance(
        own_output, output_weight, output_moment, output_average, factor, LEARNING_RATES[2]
    )
    gateup_set = advance(
        own_gateup, gateup_weight, gateup_moment, gateup_average, factor, LEARNING_RATES[3]
    )
    down_set = advance(own_down, down_weight, down_moment, down_average, factor, LEARNING_RATES[4])
    gains_set = advance(
        grad_gains, norm_gains, gains_moment, gains_average, factor, LEARNING_RATES[5]
    )
    return (
        mixed,
        mixed.astype(jnp.bfloat16),
        tokens_grad,
        grad_norm,
        query_set[0],
        query_set[1],
        query_set[2],
        query_set[3],
        query_set[4],
        keyvalue_set[0],
        keyvalue_set[1],
        keyvalue_set[2],
        keyvalue_set[3],
        keyvalue_set[4],
        output_set[0],
        output_set[1],
        output_set[2],
        output_set[3],
        output_set[4],
        gateup_set[0],
        gateup_set[1],
        gateup_set[2],
        gateup_set[3],
        gateup_set[4],
        down_set[0],
        down_set[1],
        down_set[2],
        down_set[3],
        down_set[4],
        gains_set[0],
        gains_set[1],
        gains_set[2],
        gains_set[3],
        gains_set[4],
    )


def solution(mesh):
    return jax.shard_map(
        local,
        mesh=mesh,
        in_specs=(
            P(("dp", "tensor"), None),
            P(("dp", "tensor"), None),
            P(("dp", "tensor"), None),
            P("dp", None),
            P("dp", "tensor"),
            P("dp", "tensor"),
            P("dp", "tensor"),
            P("dp", None),
            P("dp", None),
            P("dp", None),
            P("tensor", "dp"),
            P("tensor", "dp"),
            P("tensor", "dp"),
            P(None, "dp", "tensor"),
            P(None, "dp", "tensor"),
            P(None, "dp", "tensor"),
            P("tensor", "dp"),
            P("tensor", "dp"),
            P("tensor", "dp"),
            P(None, "dp"),
            P(None, "dp"),
            P(None, "dp"),
        ),
        out_specs=(
            P(("dp", "tensor"), None),
            P(("dp", "tensor"), None),
            P(("dp", "tensor"), None),
            P(),
            P("dp", "tensor"),
            P("dp", "tensor"),
            P("dp", "tensor"),
            P("dp", "tensor"),
            P("dp", "tensor"),
            P("dp", None),
            P("dp", None),
            P("dp", None),
            P("dp", None),
            P("dp", None),
            P("tensor", "dp"),
            P("tensor", "dp"),
            P("tensor", "dp"),
            P("tensor", "dp"),
            P("tensor", "dp"),
            P(None, "dp", "tensor"),
            P(None, "dp", "tensor"),
            P(None, "dp", "tensor"),
            P(None, "dp", "tensor"),
            P(None, "dp", "tensor"),
            P("tensor", "dp"),
            P("tensor", "dp"),
            P("tensor", "dp"),
            P("tensor", "dp"),
            P("tensor", "dp"),
            P(None, "dp"),
            P(None, "dp"),
            P(None, "dp"),
            P(None, "dp"),
            P(None, "dp"),
        ),
        check_vma=False,
    )
```

```python
import functools
import math

import jax
import jax.numpy as jnp
from jax import lax
from jax.experimental import pallas as pl
from jax.experimental.pallas import tpu as pltpu
from jax.sharding import PartitionSpec as P

HD = 128
STEP = 10


EPSILON = 1e-05
MASKED = -1000000000.0
CLIP = 1.0
MOMENTUM = 0.9
LEARNING_RATES = (12.0, 12.0, 480.0, 48.0, 12.0, 960.0)
AVERAGE_TOP = 0.999
ROPE_BASE = 10000.0
MESH = pl.DeviceIdType.MESH
LOW = jnp.bfloat16
F32 = jnp.float32


def dot_nn(a, b):
    return jnp.dot(a, b, preferred_element_type=F32)


def dot_nt(a, b):
    return lax.dot_general(a, b, (((1,), (1,)), ((), ())), preferred_element_type=F32)


def dot_tn(a, b):
    return lax.dot_general(a, b, (((0,), (0,)), ((), ())), preferred_element_type=F32)


class Place:
    def __init__(self, nd, nt):
        self.nd, self.nt = nd, nt
        self.nx = 2 if nd % 2 == 0 else 1
        self.ny = nd // self.nx
        self.nz = nt // 2
        self.dp = lax.axis_index("dp")
        self.t = lax.axis_index("tensor")
        self.y = self.dp // self.nx
        self.x = lax.rem(self.dp, self.nx)
        self.z = self.t // 2
        self.c = lax.rem(self.t, 2)

    def x_peer(self):
        return self.y * self.nx + (1 - self.x)

    def y_peer(self, step):
        return lax.rem(self.y + step, self.ny) * self.nx + self.x

    def xy_peer(self, step):
        return lax.rem(self.y + step, self.ny) * self.nx + (1 - self.x)

    def sibling(self):
        return self.z * 2 + (1 - self.c)


def remote(src, dst, send, recv, dp, t):
    return pltpu.make_async_remote_copy(src, dst, send, recv, device_id=(dp, t), device_id_type=MESH)


def greet(at, dps=True, zs=True, core=True):
    bar = pltpu.get_barrier_semaphore()
    count = 0
    targets = []
    if dps:
        targets.append((at.x_peer(), at.t))
        targets += [(at.y_peer(s), at.t) for s in range(1, at.ny)]
    if core:
        targets.append((at.dp, at.sibling()))
    for target in targets:
        pl.semaphore_signal(bar, inc=1, device_id=target, device_id_type=MESH)
        count += 1
    if zs:
        @pl.when(at.z > 0)
        def _():
            pl.semaphore_signal(bar, inc=1, device_id=(at.dp, at.t - 2), device_id_type=MESH)

        @pl.when(at.z < at.nz - 1)
        def _():
            pl.semaphore_signal(bar, inc=1, device_id=(at.dp, at.t + 2), device_id_type=MESH)

        count = count + (at.z > 0).astype(jnp.int32) + (at.z < at.nz - 1).astype(jnp.int32)
    pl.semaphore_wait(bar, count)


def far_first(k, z, nz):
    j = nz - 1 - k
    m = jnp.minimum(z, nz - 1 - z)
    s = (j + 1) // 2
    two = jnp.where(lax.rem(j, 2) == 1, z - s, z + s)
    one = jnp.where(z < nz - 1 - z, j, nz - 1 - j)
    return jnp.where(j <= 2 * m, two, one)


def near_first(k, z, nz):
    return far_first(nz - 1 - k, z, nz)


class Gather:
    def __init__(self, at, src, dst, xs, ys, xf, yf, recv, kind):
        self.at, self.src, self.dst, self.kind = at, src, dst, kind
        self.xs, self.ys, self.xf, self.yf, self.recv = xs, ys, xf, yf, recv

    def own(self):
        at = self.at
        out = [remote(self.src, self.dst(at.dp), self.xs, self.recv.at[at.dp], at.x_peer(), at.t)]
        for s in range(1, at.ny):
            out.append(remote(self.src, self.dst(at.dp), self.ys.at[s - 1], self.recv.at[at.dp], at.y_peer(s), at.t))
        return out

    def passed(self):
        at = self.at
        out = []
        for s in range(1, at.ny):
            if self.kind == 0:
                o = at.x_peer()
                out.append(remote(self.dst(o), self.dst(o), self.yf.at[s - 1], self.recv.at[o], at.y_peer(s), at.t))
            else:
                o = at.y_peer(s)
                out.append(remote(self.dst(o), self.dst(o), self.xf.at[s - 1], self.recv.at[o], at.x_peer(), at.t))
        return out

    def arrived(self, o):
        remote(self.src, self.dst(o), self.xs, self.recv.at[o], self.at.x_peer(), self.at.t).wait_recv()

    def start(self):
        for cp in self.own():
            cp.start()

    def forward(self):
        at = self.at
        if self.kind == 0:
            self.arrived(at.x_peer())
        else:
            for s in range(1, at.ny):
                self.arrived(at.y_peer(s))
        for cp in self.passed():
            cp.start()

    def finish(self):
        at = self.at
        if self.kind == 0:
            for s in range(1, at.ny):
                self.arrived(at.y_peer(s))
        else:
            self.arrived(at.x_peer())
        for s in range(1, at.ny):
            self.arrived(at.xy_peer(s))

    def either(self, name):
        kind = self.kind
        for value in range(2):
            self.kind = value
            pl.when(kind == value)(getattr(self, name))
        self.kind = kind

    def finish_any(self):
        self.either("finish")

    def forward_any(self):
        self.either("forward")

    def drain_any(self):
        self.either("drain")

    def drain(self):
        for cp in self.own() + self.passed():
            cp.wait_send()


def mlp_kernel(nd, nt, xn_in, dy_in, w_all, w_in,
               dxn_out, mine_g, land_g, mine_u, land_u, down_out, out_out,
               both, wts, act, psend, pown, precv, zrecv, bsend, bown, bland,
               lsem, wx, wy, wxf, wyf, wr, ar, ac, asr, asl, ps, pr, zs, zr, bs, br, osem, dsem, p1l, p1s, p1r):
    at = Place(nd, nt)
    nz, nx, ny = at.nz, at.nx, at.ny
    R, D = xn_in.shape
    F, Dd = w_in.shape
    Fh = F // 2
    CH = zs.shape[1]
    CR = R // CH
    rows = lambda t: pl.ds(pl.multiple_of(t * R, R), R)
    dcols = lambda o: pl.ds(pl.multiple_of(o * Dd, Dd), Dd)
    xall, dyv = both.at[0], both.at[1]

    own_loads = [
        pltpu.make_async_copy(xn_in, xall.at[rows(at.t)], lsem.at[0]),
        pltpu.make_async_copy(dy_in, dyv, lsem.at[1]),
        pltpu.make_async_copy(w_all, wts.at[pl.ds(0, 2)], lsem.at[2]),
        pltpu.make_async_copy(w_in, wts.at[2, :, dcols(at.dp)], lsem.at[3]),
    ]
    for cp in own_loads:
        cp.start()
    greet(at)

    gathers = []
    for p in range(2):
        half = pl.ds(p * Fh, Fh)
        gathers.append(Gather(at, w_in.at[half], lambda o, half=half: wts.at[2, half, dcols(o)],
                              wx.at[p], wy.at[p], wxf.at[p], wyf.at[p], wr.at[p], p))

    def right(o):
        return remote(xall.at[rows(o)], xall.at[rows(o)], asr.at[o], ar.at[o], at.dp, at.t + 2)

    def left(o):
        return remote(xall.at[rows(o)], xall.at[rows(o)], asl.at[o], ar.at[o], at.dp, at.t - 2)

    def across(o):
        return remote(xall.at[rows(o)], xall.at[rows(o)], ac.at[o], ar.at[o], at.dp, at.sibling())

    own_loads[0].wait()
    pl.when(at.z < nz - 1)(lambda: right(at.t).start())
    pl.when(at.z > 0)(lambda: left(at.t).start())
    across(at.t).start()
    for g in gathers:
        g.start()

    def line_step(s):
        @pl.when(at.z - s >= 0)
        def _():
            o = at.t - 2 * s
            across(o).wait_recv()
            pl.when(at.z < nz - 1)(lambda: right(o).start())
            across(o).start()

        @pl.when(at.z + s < nz)
        def _():
            o = at.t + 2 * s
            across(o).wait_recv()
            pl.when(at.z > 0)(lambda: left(o).start())
            across(o).start()

    for g in gathers:
        g.forward()
    for cp in own_loads[1:]:
        cp.wait()

    is_end = (at.z == 0) | (at.z == nz - 1)
    piece = lambda c: pl.ds(pl.multiple_of(c * CR, CR), CR)

    def swap(d):
        return remote(psend, precv.at[d], ps.at[0], pr.at[d], at.dp, at.sibling())

    def push_right(d, c):
        return remote(pown.at[d, piece(c)], zrecv.at[d, piece(c)], zs.at[d, c], zr.at[d, c], at.dp, at.t + 2)

    def push_left(d, c):
        slot = jnp.where(d == at.z - 1, nz, d)
        return remote(pown.at[d, piece(c)], zrecv.at[slot, piece(c)], zs.at[d, c], zr.at[slot, c], at.dp, at.t - 2)

    def came(slot, c):
        remote(pown.at[0, piece(c)], zrecv.at[slot, piece(c)], zs.at[0, c], zr.at[slot, c], at.dp, at.sibling()).wait_recv()

    def relay(d, c, push):
        pl.when(c == 0)(lambda: swap(d).wait_recv())

        @pl.when(is_end)
        def _():
            pown[d, piece(c)] = (pown[d, piece(c)].astype(F32) + precv[d, piece(c)].astype(F32)).astype(LOW)

        @pl.when(jnp.logical_not(is_end))
        def _():
            came(d, c)
            pown[d, piece(c)] = (pown[d, piece(c)].astype(F32) + precv[d, piece(c)].astype(F32)
                                 + zrecv[d, piece(c)].astype(F32)).astype(LOW)

        push(d, c).start()

    lower = at.z < nz - 1 - at.z

    def near_relay(s, c):
        pl.when(lower & (s > at.z))(lambda: relay(s, c, push_right))
        pl.when(jnp.logical_not(lower) & (nz - 1 - s < at.z))(lambda: relay(nz - 1 - s, c, push_left))

    def far_relay(s, c):
        pl.when(jnp.logical_not(lower) & (s > at.z))(lambda: relay(s, c, push_right))
        pl.when(lower & (nz - 1 - s < at.z))(lambda: relay(nz - 1 - s, c, push_left))

    def relays(s, c):
        pl.when(s > at.z)(lambda: relay(s, c, push_right))
        pl.when(nz - 1 - s < at.z)(lambda: relay(nz - 1 - s, c, push_left))

    def branch_swap(j):
        return remote(bsend, bland.at[j], bs.at[0], br.at[j], at.dp, at.sibling())

    def branch_copy(slot, j):
        return pltpu.make_async_copy(bown.at[slot], out_out.at[j], osem.at[slot])

    def turn(k):
        return near_first(jnp.where(k < 2, 1 - k, k), at.z, nz)

    def branch_sum(k):
        j = turn(k)
        slot = lax.rem(k, 2)
        branch_swap(j).wait_recv()

        def part(c, _):
            bown[slot, piece(c)] = (bown[slot, piece(c)].astype(F32) + bland[j, piece(c)].astype(F32)).astype(LOW)
            return 0

        lax.fori_loop(0, CH, part, 0)
        branch_copy(slot, j).start()

    def forward(j):
        r = pl.ds(pl.multiple_of(j * 2 * R, 2 * R), 2 * R)
        for lo in range(0, F, 256):
            part = pl.ds(lo, min(256, F - lo))
            gate, up = dot_nt(xall[r, :], wts[0, part, :]), dot_nt(xall[r, :], wts[1, part, :])
            dmid = dot_nt(dyv[r, :], wts[2, part, :])
            sig = 1.0 / (1.0 + jnp.exp(-gate))
            silu = gate * sig
            act[2, r, part] = (silu * up).astype(LOW)
            act[1, r, part] = (dmid * silu).astype(LOW)
            act[0, r, part] = (dmid * up * (sig * (1.0 + gate * (1.0 - sig)))).astype(LOW)

    def block(k, _):
        pl.when(k >= 2)(lambda: line_step(k))
        j = turn(k)
        across(2 * j + 1 - at.c).wait_recv()
        slot = lax.rem(k, 2)
        forward(j)
        pl.when(k >= 1)(lambda: swap(j).wait_send())
        r = pl.ds(pl.multiple_of(j * 2 * R, 2 * R), 2 * R)

        def back(o, _):
            cols = dcols(o)
            v = dot_nn(act[0, r, :], wts[0, :, cols]) + dot_nn(act[1, r, :], wts[1, :, cols])
            first = at.c == 0
            psend[:, cols] = jnp.where(first, v[R:], v[:R]).astype(LOW)
            pown[j, :, cols] = jnp.where(first, v[:R], v[R:]).astype(LOW)
            return 0

        lax.fori_loop(0, nd, back, 0)
        swap(j).start()
        s = jnp.where(is_end, jnp.where(k < 2, 1 - k, k), k - 1)

        @pl.when((s >= 1) & (is_end | (s < nz - 2)))
        def _():
            lax.fori_loop(0, CH, lambda c, _: (relays(s, c), 0)[1], 0)

        pl.when(k >= 1)(lambda: branch_sum(k - 1))
        pl.when(k >= 1)(lambda: branch_swap(j).wait_send())
        pl.when(k >= 2)(lambda: branch_copy(slot, j).wait())

        def branch(o, _):
            cols = dcols(o)
            v = dot_nn(act[2, r, :], wts[2, :, cols])
            first = at.c == 0
            bsend[:, cols] = jnp.where(first, v[R:], v[:R]).astype(LOW)
            bown[slot, :, cols] = jnp.where(first, v[:R], v[R:]).astype(LOW)
            return 0

        lax.fori_loop(0, nd, branch, 0)
        branch_swap(j).start()
        return 0

    if nz > 1:
        line_step(1)
    for g in gathers:
        g.finish()
    lax.fori_loop(0, nz, block, 0)
    swap(0).wait_send()
    branch_swap(0).wait_send()
    branch_sum(jnp.int32(nz - 1))
    for g in gathers:
        g.drain()

    outs = ((mine_g, land_g), (mine_u, land_u))

    def source(n, o):
        return wts.at[n, :, dcols(o)]

    def down_copy(o):
        return pltpu.make_async_copy(wts.at[2, :, dcols(o)], down_out.at[:, dcols(o)], dsem.at[o])

    def hop(n, o):
        mine, land = outs[n]
        yy, xx = o // nx, lax.rem(o, nx)
        if n % 2 == 0:
            step = lax.rem(yy - at.y + ny, ny)
            slot = (step - 1) * nx + xx
            stays, place, peer = yy == at.y, xx, yy * nx + at.x
        else:
            slot, stays, place, peer = yy, xx == at.x, yy, at.y * nx + xx
        local = pltpu.make_async_copy(source(n, o), mine.at[place], p1l.at[n, place])
        slot = jnp.where(stays, 0, slot)
        away = remote(source(n, o), land.at[slot], p1s.at[n, slot], p1r.at[n, slot], jnp.where(stays, at.x_peer(), peer), at.t)
        return stays, local, away

    def order(n, i):
        if n % 2 == 0:
            return lax.rem(at.y + 1 + i // nx, ny) * nx + lax.rem(i, nx)
        return lax.rem(i, ny) * nx + jnp.where(i < ny, 1 - at.x, at.x)

    def send(n, o):
        stays, local, away = hop(n, o)
        pl.when(stays)(lambda: local.start())
        pl.when(jnp.logical_not(stays))(lambda: away.start())

    def settle(n):
        def one(i, _):
            stays, local, away = hop(n, order(n, i))

            @pl.when(stays)
            def _():
                local.wait()

            @pl.when(jnp.logical_not(stays))
            def _():
                away.wait_send()
                away.wait_recv()

            return 0

        lax.fori_loop(0, nd, one, 0)

    def wgrad(p, _):
        n, i = p // nd, lax.rem(p, nd)
        middle = jnp.logical_not(is_end)
        early, late = p - 1, p // 2 - 3
        pl.when(middle & (early >= 0) & (early < CH))(lambda: relays(jnp.int32(nz - 2), early))
        turn_now = middle & (lax.rem(p, 2) == 0) & (late >= 0) & (late < CH - 1)
        pl.when(turn_now)(lambda: near_relay(jnp.int32(nz - 1), late))
        pl.when(turn_now & (late >= 1))(lambda: far_relay(jnp.int32(nz - 1), late - 1))
        o = jnp.where(n == 1, order(1, i), order(0, i))
        for lo in range(0, F, 384):
            part = pl.ds(lo, min(384, F - lo))
            wts[n, part, dcols(o)] = dot_tn(act[n, :, part], both[n // 2, :, dcols(o)]).astype(LOW)
        pl.when(n == 0)(lambda: send(0, o))
        pl.when(n == 1)(lambda: send(1, o))
        pl.when(n == 2)(lambda: down_copy(o).start())
        return 0

    lax.fori_loop(0, 3 * nd, wgrad, 0)

    @pl.when(jnp.logical_not(is_end))
    def _():
        near_relay(jnp.int32(nz - 1), jnp.int32(CH - 1))
        far_relay(jnp.int32(nz - 1), jnp.int32(CH - 2))
        far_relay(jnp.int32(nz - 1), jnp.int32(CH - 1))

    for slot in range(2):
        branch_copy(slot, 0).wait()

    swap(at.z).wait_recv()
    for c in range(CH):
        part = pl.ds(c * CR, CR)
        pl.when(at.z > 0)(lambda c=c: came(at.z, c))
        pl.when(at.z < nz - 1)(lambda c=c: came(nz, c))
        total = pown[at.z, part].astype(F32) + precv[at.z, part].astype(F32)
        total = total + jnp.where(at.z > 0, zrecv[at.z, part].astype(F32), 0.0)
        total = total + jnp.where(at.z < nz - 1, zrecv[nz, part].astype(F32), 0.0)
        dxn_out[part, :] = total.astype(LOW)

    for zz in range(nz):
        o = 2 * zz + at.c

        @pl.when(zz != at.z)
        def _(zz=zz):
            for c in range(CH):
                push_right(jnp.int32(zz), c).wait_send()

        across(o).wait_send()
        pl.when((at.z < nz - 1) & (zz <= at.z))(lambda o=o: right(o).wait_send())
        pl.when((at.z > 0) & (zz >= at.z))(lambda o=o: left(o).wait_send())
    for n in range(2):
        settle(n)
    for o in range(nd):
        down_copy(o).wait()


def mlp(nd, nt, xn, dy_all, w_all, w):
    R, D = xn.shape
    S = dy_all.shape[0]
    F, Dd = w.shape
    nz = nt // 2
    ny = nd // 2
    ch = 4
    dma = lambda *s: pltpu.SemaphoreType.DMA(s)
    shape = lambda *s: jax.ShapeDtypeStruct(s, LOW)
    b = lambda *s: pltpu.VMEM(s, LOW)
    slots = max(2 * (ny - 1), ny)
    hbm = pl.BlockSpec(memory_space=pltpu.HBM)
    vm = pl.BlockSpec(memory_space=pltpu.VMEM)
    return pl.pallas_call(
        functools.partial(mlp_kernel, nd, nt),
        out_shape=(
            shape(R, D),
            shape(2, F, Dd), shape(2 * (ny - 1), F, Dd), shape(ny, F, Dd), shape(ny, F, Dd),
            shape(F, D),
            shape(nz, R, D),
        ),
        in_specs=[hbm] * 4,
        out_specs=(vm,) + (hbm,) * 6,
        scratch_shapes=[
            b(2, S, D), b(3, F, D), b(3, S, F),
            b(R, D), b(nz, R, D), b(nz, R, D), b(nz + 1, R, D), b(R, D), b(2, R, D), b(nz, R, D),
            dma(4), dma(2), dma(2, ny - 1), dma(2, ny - 1), dma(2, ny - 1), dma(2, nd),
            dma(nt), dma(nt), dma(nt), dma(nt), dma(1), dma(nz), dma(nz, ch), dma(nz + 1, ch), dma(1), dma(nz), dma(2), dma(nd),
            dma(2, max(2, ny)), dma(2, slots), dma(2, slots),
        ],
        compiler_params=pltpu.CompilerParams(collective_id=1, has_side_effects=True, vmem_limit_bytes=63 << 20),
        cost_estimate=pl.CostEstimate(flops=12 * S * D * F, bytes_accessed=40 << 20, transcendentals=S * F),
        name="mlp",
    )(xn, dy_all, w_all, w)


def swap_halves(u):
    h = u.shape[-1] // 2
    return jnp.concatenate([u[:, h:], u[:, :h]], axis=1)


def greet_all(at):
    bar = pltpu.get_barrier_semaphore()
    for s in range(1, at.nd):
        pl.semaphore_signal(bar, inc=1, device_id=(lax.rem(at.dp + s, at.nd), at.t), device_id_type=MESH)
    for s in range(1, at.nt):
        pl.semaphore_signal(bar, inc=1, device_id=(at.dp, lax.rem(at.t + s, at.nt)), device_id_type=MESH)
    pl.semaphore_wait(bar, at.nd - 1 + at.nt - 1)


class Line:
    def __init__(self, at, view, right, left, recv, across=None):
        self.at, self.view, self.rs, self.ls, self.recv, self.across = at, view, right, left, recv, across

    def right(self, o):
        return remote(self.view(o), self.view(o), self.rs.at[o], self.recv.at[o], self.at.dp, self.at.t + 2)

    def left(self, o):
        return remote(self.view(o), self.view(o), self.ls.at[o], self.recv.at[o], self.at.dp, self.at.t - 2)

    def pass_on(self, o, to_right, to_left):
        at = self.at
        if to_right:
            pl.when(at.z < at.nz - 1)(lambda: self.right(o).start())
        if to_left:
            pl.when(at.z > 0)(lambda: self.left(o).start())
        if self.across is not None:
            self.across(o).start()

    def start(self):
        self.pass_on(self.at.z, True, True)

    def arrived(self, o):
        remote(self.view(o), self.view(o), self.rs.at[o], self.recv.at[o], self.at.dp, self.at.sibling()).wait_recv()

    def step(self, s):
        at = self.at

        @pl.when(at.z - s >= 0)
        def _():
            self.arrived(at.z - s)
            self.pass_on(at.z - s, True, False)

        @pl.when(at.z + s < at.nz)
        def _():
            self.arrived(at.z + s)
            self.pass_on(at.z + s, False, True)

    def drain(self):
        at = self.at
        for o in range(at.nz):
            pl.when((at.z < at.nz - 1) & (o <= at.z))(lambda o=o: self.right(o).wait_send())
            pl.when((at.z > 0) & (o >= at.z))(lambda o=o: self.left(o).wait_send())
            if self.across is not None:
                self.across(o).wait_send()


def attend_kernel(nd, nt, tok, gain, wq_in, wkv_in, wo_in, cosf, sins, lo_row, dy_in, w_in,
                  h1_out, xn2_out, gfull, lse_out,
                  xn1_out, wq_out, wo_out, wkv_out, kv_out, q_out, o_out, dy_all, w_all,
                  xn1, wq, wo, wkv, kvs, qs, os_, acc, pback, precv,
                  lsem, gs, gr, vx, vy, vxf, vyf, vr, qx, qy, qxf, qyf, qr, ox, oy, oxf, oyf, orr,
                  qlr, qll, qlv, olr, oll, olv, klr, kll, klv, klc, klcr, cs, cr, outs,
                  ylr, yll, ylv, ylc, mx, my, mxf, myf, mr, fsem):
    at = Place(nd, nt)
    nz = at.nz
    R, D = tok.shape
    Dd, HC = wq_in.shape
    rows = lambda t: pl.ds(pl.multiple_of(t * R, R), R)
    drows = lambda o: pl.ds(pl.multiple_of(o * Dd, Dd), Dd)
    hcols = lambda j: pl.ds(pl.multiple_of(j * HC, HC), HC)

    loads = [
        pltpu.make_async_copy(wkv_in, wkv.at[drows(at.dp)], lsem.at[0]),
        pltpu.make_async_copy(wq_in, wq.at[at.z, drows(at.dp)], lsem.at[1]),
        pltpu.make_async_copy(wo_in, wo.at[at.dp, hcols(at.z)], lsem.at[2]),
    ]
    for cp in loads:
        cp.start()
    gfull[at.dp] = gain[...]
    greet_all(at)

    def gain_copy(s):
        return remote(gain, gfull.at[at.dp], gs.at[s - 1], gr.at[s - 1], lax.rem(at.dp + s, nd), at.t)

    for s in range(1, nd):
        gain_copy(s).start()
    Dh = Dd // 2
    gkv = [Gather(at, wkv_in.at[pl.ds(p * Dh, Dh)], lambda o, p=p: wkv.at[pl.ds(pl.multiple_of(o * Dd + p * Dh, Dh), Dh)],
                  vx.at[p], vy.at[p], vxf.at[p], vyf.at[p], vr.at[p], p) for p in range(2)]

    def gq(k):
        j = near_first(k, at.z, nz)
        return Gather(at, wq.at[j, drows(at.dp)], lambda o: wq.at[j, drows(o)], qx.at[k], qy.at[k], qxf.at[k], qyf.at[k], qr.at[k], lax.rem(k, 2) if not isinstance(k, int) else k % 2)

    def go(k):
        j = near_first(k, at.z, nz)
        return Gather(at, wo.at[at.dp, hcols(j)], lambda o: wo.at[o, hcols(j)], ox.at[k], oy.at[k], oxf.at[k], oyf.at[k], orr.at[k], lax.rem(k, 2) if not isinstance(k, int) else k % 2)

    lq = Line(at, lambda o: wq.at[o, drows(at.dp)], qlr, qll, qlv)
    lo = Line(at, lambda o: wo.at[at.dp, hcols(o)], olr, oll, olv)

    def kv_view(o):
        return kvs.at[rows(2 * o + at.c)]

    def kv_across(o):
        return remote(kv_view(o), kv_view(o), klc.at[o], klcr.at[o], at.dp, at.sibling())

    lkv = Line(at, kv_view, klr, kll, klv, kv_across)

    for_mlp = [pltpu.make_async_copy(dy_in, dy_all.at[rows(at.t)], fsem.at[0]),
               pltpu.make_async_copy(w_in.at[0], w_all.at[0, :, drows(at.dp)], fsem.at[1]),
               pltpu.make_async_copy(w_in.at[1], w_all.at[1, :, drows(at.dp)], fsem.at[2])]
    for cp in for_mlp:
        cp.start()
    gw = [Gather(at, w_in.at[p], lambda o, p=p: w_all.at[p, :, drows(o)], mx.at[p], my.at[p], mxf.at[p], myf.at[p], mr.at[p], p)
          for p in range(2)]

    def dy_view(o):
        return dy_all.at[rows(2 * o + at.c)]

    def dy_across(o):
        return remote(dy_view(o), dy_view(o), ylc.at[o], ylv.at[1, o], at.dp, at.sibling())

    ldy = Line(at, dy_view, ylr, yll, ylv.at[0], dy_across)
    for g in gkv:
        g.start()
    loads[1].wait()
    lq.start()
    gq(0).start()

    for s in range(1, nd):
        gain_copy(s).wait_recv()

    def scaled(v, row, write):
        r = lax.rsqrt(jnp.mean(v * v, axis=-1, keepdims=True) + EPSILON)
        for o in range(nd):
            cols = pl.ds(o * Dd, Dd)
            write(cols, (v[:, o * Dd:(o + 1) * Dd] * r * gfull[o, row:row + 1, :]).astype(LOW))

    mine = rows(at.c)

    def put_xn1(cols, v):
        xn1[mine, cols] = v

    scaled(tok[...].astype(F32), 0, put_xn1)
    xn1_across = remote(xn1.at[mine], xn1.at[mine], cs.at[0], cr.at[0], at.dp, at.sibling())
    xn1_across.start()

    for g in gkv:
        g.forward()
    loads[0].wait()
    for g in gkv:
        g.finish()
    kvpre = dot_nn(xn1[mine, :], wkv[...])
    kk = kvpre[:, :HD]
    kvs[rows(at.t), pl.ds(0, HD)] = (kk * cosf[mine, :] + swap_halves(kk) * sins[mine, :]).astype(LOW)
    kvs[rows(at.t), pl.ds(HD, HD)] = kvpre[:, HD:].astype(LOW)
    lkv.start()
    loads[2].wait()
    lo.start()
    for s in range(1, nz):
        lq.step(s)
        gq(s).start()
        gq(s - 1).forward()
        lkv.step(s)
    gq(nz - 1).forward()
    xn1_across.wait_recv()
    go(0).start()
    for s in range(1, nz):
        lo.step(s)
        go(s).start()
    for_mlp[0].wait()
    ldy.start()
    for o in range(nz):
        kv_across(o).wait_recv()

    scale = 1.0 / math.sqrt(HD)
    KT = 2 * R
    here = at.z * KT + lax.broadcasted_iota(jnp.int32, (1, KT), 1)
    low_row = lo_row[0:1, :]

    def pair(k, _):
        j = near_first(k, at.z, nz)
        g = gq(k)
        g.finish_any()
        qpre = dot_nn(xn1[...], wq[j])
        for hh in range(HC // HD):
            u = qpre[:, hh * HD:(hh + 1) * HD]
            qs[:, pl.ds(pl.multiple_of(j * HC + hh * HD, HD), HD)] = (u * cosf[...] + swap_halves(u) * sins[...]).astype(LOW)

        for hh in range(HC // HD):
            cols = pl.ds(pl.multiple_of(j * HC + hh * HD, HD), HD)
            qh = qs[:, cols]
            acc[...] = jnp.zeros_like(acc)

            def tile(b, carry):
                top, total = carry
                kr = pl.ds(pl.multiple_of(b * KT, KT), KT)
                s = dot_nt(kvs[kr, pl.ds(0, HD)], qh)
                place = b * KT + lax.broadcasted_iota(jnp.int32, (KT, KT), 0)
                s = jnp.where((place >= low_row) & (place <= here), s * scale, MASKED)
                new_top = jnp.maximum(top, jnp.max(s, axis=0, keepdims=True))
                p = jnp.exp(s - new_top)
                fade = jnp.exp(top - new_top)
                acc[...] = acc[...] * fade + dot_tn(kvs[kr, pl.ds(HD, HD)], p.astype(LOW))
                return new_top, total * fade + jnp.sum(p, axis=0, keepdims=True)

            top, total = lax.fori_loop(0, at.z + 1, tile, (jnp.full((1, KT), MASKED, F32), jnp.zeros((1, KT), F32)))
            os_[:, cols] = (acc[...] / total).T.astype(LOW)
            lse_out[pl.ds(j * (HC // HD) + hh, 1), :] = top + jnp.log(total)
        go(k).forward_any()
        return 0

    lax.fori_loop(0, nz, pair, 0)
    for g in gw:
        g.start()
    ldy.step(1)
    keep = [
        pltpu.make_async_copy(xn1, xn1_out, outs.at[0]),
        pltpu.make_async_copy(wq, wq_out, outs.at[1]),
        pltpu.make_async_copy(wkv, wkv_out, outs.at[2]),
        pltpu.make_async_copy(kvs, kv_out, outs.at[3]),
        pltpu.make_async_copy(qs, q_out, outs.at[4]),
        pltpu.make_async_copy(os_, o_out, outs.at[5]),
    ]
    for cp in keep:
        cp.start()

    lax.fori_loop(0, nz, lambda k, _: (go(k).finish_any(), 0)[1], 0)
    keep.append(pltpu.make_async_copy(wo, wo_out, outs.at[6]))
    keep[-1].start()
    theirs = rows(1 - at.c)
    for o in range(nd):
        pback[:, pl.ds(o * Dd, Dd)] = dot_nn(os_[theirs, :], wo[o]).astype(LOW)
    back = remote(pback, precv, cs.at[1], cr.at[1], at.dp, at.sibling())
    back.start()
    for o in range(nd):
        cols = pl.ds(o * Dd, Dd)
        h1_out[:, cols] = tok[:, cols].astype(F32) + dot_nn(os_[mine, :], wo[o])
    back.wait_recv()
    h1_out[...] = h1_out[...] + precv[...].astype(F32)

    def put_xn2(cols, v):
        xn2_out[:, cols] = v

    scaled(h1_out[...], 1, put_xn2)
    for g in gw:
        g.forward()
    for s in range(2, nz):
        ldy.step(s)
    for g in gw:
        g.finish()
    for o in range(nz):
        dy_across(o).wait_recv()
    for cp in for_mlp[1:]:
        cp.wait()
    for g in gw:
        g.drain()
    ldy.drain()

    for s in range(1, nd):
        gain_copy(s).wait_send()
    for g in gkv:
        g.drain()
    xn1_across.wait_send()
    back.wait_send()
    lq.drain()
    lo.drain()
    lkv.drain()

    def drain(k, _):
        gq(k).drain_any()
        go(k).drain_any()
        return 0

    lax.fori_loop(0, nz, drain, 0)
    for cp in keep:
        cp.wait()


def attend(nd, nt, tok, gain, wq, wkv, wo, cosf, sins, lo, dy, w):
    R, D = tok.shape
    Dd, HC = wq.shape
    S = R * nt
    nz, ny = nt // 2, nd // 2
    dma = lambda *s: pltpu.SemaphoreType.DMA(s)
    hbm = pl.BlockSpec(memory_space=pltpu.HBM)
    vm = pl.BlockSpec(memory_space=pltpu.VMEM)
    shapes = [((R, D), F32), ((R, D), LOW), ((nd, 8, Dd), F32), ((nz * (HC // HD), 2 * R), F32),
              ((2 * R, D), LOW), ((nz, D, HC), LOW), ((nd, nz * HC, Dd), LOW), ((D, 2 * HD), LOW), ((S, 2 * HD), LOW),
              ((2 * R, nz * HC), LOW), ((2 * R, nz * HC), LOW)]
    gathered = [((S, D), LOW), ((2, w.shape[1], D), LOW)]
    yg = lambda n: [dma(n), dma(n, ny - 1), dma(n, ny - 1), dma(n, ny - 1), dma(n, nd)]
    return pl.pallas_call(
        functools.partial(attend_kernel, nd, nt),
        out_shape=tuple(jax.ShapeDtypeStruct(*s) for s in shapes + gathered),
        in_specs=[vm, vm, hbm, hbm, hbm, vm, vm, vm, hbm, hbm],
        out_specs=(vm, vm, vm, vm) + (hbm,) * 9,
        scratch_shapes=[pltpu.VMEM(*s) for s in shapes[4:]] + [pltpu.VMEM((HD, 2 * R), F32), pltpu.VMEM((R, D), LOW), pltpu.VMEM((R, D), LOW)]
        + [dma(3), dma(nd - 1), dma(nd - 1)] + yg(2) + yg(nz) + yg(nz)
        + [dma(nz)] * 3 + [dma(nz)] * 3 + [dma(nz)] * 5 + [dma(2), dma(2), dma(7)]
        + [dma(nz), dma(nz), dma(2, nz), dma(nz)] + yg(2) + [dma(3)],
        compiler_params=pltpu.CompilerParams(collective_id=2, has_side_effects=True, vmem_limit_bytes=63 << 20),
        cost_estimate=pl.CostEstimate(flops=20 << 30, bytes_accessed=40 << 20, transcendentals=8 * 512 * 2048),
        name="attend",
    )(tok, gain, wq, wkv, wo, cosf, sins, lo, dy, w)


class Scatter:
    def __init__(self, at, kind, view, land, land2, ss, rs, ss2, rs2):
        self.at, self.kind, self.view = at, kind, view
        self.land, self.land2 = land, land2
        self.ss, self.rs, self.ss2, self.rs2 = ss, rs, ss2, rs2

    def first(self):
        at = self.at
        out = []
        if self.kind == 0:
            for s in range(1, at.ny):
                for xx in range(at.nx):
                    slot = (s - 1) * at.nx + xx
                    o = lax.rem(at.y + s, at.ny) * at.nx + xx
                    out.append(remote(self.view(o), self.land(slot), self.ss.at[slot], self.rs.at[slot], at.y_peer(s), at.t))
        else:
            for yy in range(at.ny):
                o = yy * at.nx + 1 - at.x
                out.append(remote(self.view(o), self.land(yy), self.ss.at[yy], self.rs.at[yy], at.x_peer(), at.t))
        return out

    def second(self):
        at = self.at
        if self.kind == 0:
            return [remote(self.view(at.x_peer()), self.land2(0), self.ss2.at[0], self.rs2.at[0], at.x_peer(), at.t)]
        return [remote(self.view(at.y_peer(s)), self.land2(s - 1), self.ss2.at[s - 1], self.rs2.at[s - 1], at.y_peer(s), at.t)
                for s in range(1, at.ny)]

    def start(self):
        for cp in self.first():
            cp.start()

    def add(self, o, slots):
        total = self.view(o)[...].astype(F32)
        for slot in slots:
            total = total + self.land(slot)[...].astype(F32)
        self.view(o)[...] = total.astype(LOW)

    def middle(self):
        at = self.at
        for cp in self.first():
            cp.wait_recv()
        if self.kind == 0:
            self.add(at.x_peer(), [(s - 1) * at.nx + 1 - at.x for s in range(1, at.ny)])
        else:
            for s in range(1, at.ny):
                self.add(at.y_peer(s), [lax.rem(at.y + s, at.ny)])
        for cp in self.second():
            cp.start()
        if self.kind == 0:
            self.add(at.dp, [(s - 1) * at.nx + at.x for s in range(1, at.ny)])
        else:
            self.add(at.dp, [at.y])

    def total(self):
        total = self.view(self.at.dp)[...].astype(F32)
        for i, cp in enumerate(self.second()):
            cp.wait_recv()
            total = total + self.land2(i)[...].astype(F32)
        return total

    def drain(self):
        for cp in self.first() + self.second():
            cp.wait_send()

    def either(self, name, put=None):
        kind = self.kind
        for value in range(2):
            self.kind = value
            call = getattr(self, name)
            if put is None:
                pl.when(kind == value)(call)
            else:
                pl.when(kind == value)(lambda call=call: put(call()))
        self.kind = kind


def grads_kernel(nd, nt, dy, tok, gfull, cosf, sins, lo_row, lse, later,
                 h1_in, dxn2_in, xn1_in, wq_in, wo_in, wkv_in, kv_in, q_in, o_in,
                 mine_g, land_g, mine_u, land_u, down_in,
                 tgrad, gq_out, go_out, gkv_out, gg_out, norm_out, keep_g, keep_u, keep_d, keep_e, got_g, got_u, got_d, got_e,
                 xn1, wq, wo, wkv, kvs, qs, os_, dos, dh1b, dxn1, dkv, dq,
                 bg, bu, bd, be, lg, lu, ld, le, tg, tu, td, te,
                 ql, ql2, ol, ol2, qz, oz, qlz, olz, kvb, kland, kz, xrecv, wl, wcl, wd2, w2, w2l, wfin, gl, gpart, u2, u2l, gfin, share, norms, normd,
                 lsem, xsem, fs, fr, qss, qsr, qss2, qsr2, oss, osr, oss2, osr2, qzs, qzr, ozs, ozr,
                 ks, kr, kzs, kzr, ws, wr, wcs, wcr, w2s, w2r, w3s, w3r, us, ur, u2s, u2r, u3s, u3r, ns, nr, n2s, n2r, outs, hs, hr):
    at = Place(nd, nt)
    nz, nx, ny = at.nz, at.nx, at.ny
    R, D = tok.shape
    Dd = wo.shape[2]
    HC = wq.shape[2]
    Ds = wl.shape[1]
    NH = HC // HD
    KT = 2 * R
    S = kvs.shape[0]
    rows = lambda t: pl.ds(pl.multiple_of(t * R, R), R)
    drows = lambda o: pl.ds(pl.multiple_of(o * Dd, Dd), Dd)
    hcols = lambda j: pl.ds(pl.multiple_of(j * HC, HC), HC)
    mine, theirs = rows(at.c), rows(1 - at.c)
    scale = 1.0 / math.sqrt(HD)

    Fh = bd.shape[1]
    pieces = [(bg, mine_g), (bu, mine_u), (tg, land_g), (tu, land_u),
              (wo, wo_in), (os_, o_in), (qs, q_in), (kvs, kv_in), (xn1, xn1_in), (wq, wq_in), (wkv, wkv_in),
              (dxn1.at[pl.ds(0, R)], h1_in), (xrecv, dxn2_in)]
    down = lambda n, o: down_in.at[pl.ds(n * Fh, Fh), drows(o)]
    pieces += [(bd.at[xx], down(0, at.y * nx + xx)) for xx in range(nx)]
    pieces += [(be.at[yy], down(1, yy * nx + at.x)) for yy in range(ny)]
    loads = [pltpu.make_async_copy(src, dst, lsem.at[i]) for i, (dst, src) in enumerate(pieces)]
    for cp in loads[11:13] + loads[:11] + loads[13:]:
        cp.start()
    greet_all(at)

    down_hops = []
    for s in range(1, ny):
        for xx in range(nx):
            slot = (s - 1) * nx + xx
            o = lax.rem(at.y + s, ny) * nx + xx
            down_hops.append(remote(down(0, o), td.at[slot], hs.at[0, slot], hr.at[0, slot], at.y_peer(s), at.t))
    for yy in range(ny):
        down_hops.append(remote(down(1, yy * nx + 1 - at.x), te.at[yy], hs.at[1, yy], hr.at[1, yy], at.x_peer(), at.t))
    for cp in down_hops:
        cp.start()

    def rms_back(v_of, e_of, row, put):
        chunks = [pl.ds(o * Dd, Dd) for o in range(nd)]
        squares = jnp.zeros((R, 1), F32)
        inner = jnp.zeros((R, 1), F32)
        for o, cols in enumerate(chunks):
            v = v_of(cols)
            squares = squares + jnp.sum(v * v, axis=-1, keepdims=True)
            inner = inner + jnp.sum(e_of(cols) * gfull[o, row:row + 1, :] * v, axis=-1, keepdims=True)
        r = lax.rsqrt(squares / D + EPSILON)
        inner = inner * (r * r * r) / D
        for o, cols in enumerate(chunks):
            v, e = v_of(cols), e_of(cols)
            gpart[row:row + 1, cols] = jnp.sum(e * v * r, axis=0, keepdims=True)
            put(cols, r * (e * gfull[o, row:row + 1, :]) - v * inner)

    gpart[...] = jnp.zeros_like(gpart)

    def put_dh1(cols, v):
        total = dy[:, cols].astype(F32) + v
        tgrad[:, cols] = total
        dh1b[mine, cols] = total.astype(LOW)

    loads[11].wait()
    loads[12].wait()
    rms_back(lambda cols: dxn1[pl.ds(0, R), cols], lambda cols: xrecv[:, cols].astype(F32), 1, put_dh1)
    swap_dh1 = remote(dh1b.at[mine], dh1b.at[mine], xsem.at[0], xsem.at[1], at.dp, at.sibling())
    swap_dh1.start()

    for i in range(4, 11):
        loads[i].wait()
    swap_dh1.wait_recv()
    def do_pair(j, _):
        acc = dot_nt(dh1b[:, pl.ds(0, Dd)], wo[0, hcols(j), :])
        for o in range(1, nd):
            acc = acc + dot_nt(dh1b[:, pl.ds(o * Dd, Dd)], wo[o, hcols(j), :])
        dos[:, hcols(j)] = acc.astype(LOW)
        return 0

    lax.fori_loop(0, nz, do_pair, 0)

    def kind_of(k):
        return k % 2 if isinstance(k, int) else lax.rem(k, 2)

    def so(k):
        j = far_first(k, at.z, nz)
        return Scatter(at, kind_of(k), lambda o: wo.at[o, hcols(j)], lambda i: ol.at[k, i], lambda i: ol2.at[k, i],
                       oss.at[k], osr.at[k], oss2.at[k], osr2.at[k])

    def sq(k):
        j = far_first(k, at.z, nz)
        return Scatter(at, kind_of(k), lambda o: wq.at[j, drows(o)], lambda i: ql.at[k, i], lambda i: ql2.at[k, i],
                       qss.at[k], qsr.at[k], qss2.at[k], qsr2.at[k])

    def wo_unit(k, _):
        j = far_first(k, at.z, nz)

        def part(o, _):
            wo[o, hcols(j), :] = dot_tn(os_[:, hcols(j)], dh1b[:, drows(o)]).astype(LOW)
            return 0

        lax.fori_loop(0, nd, part, 0)
        so(k).either("start")
        return 0

    lax.fori_loop(0, nz, wo_unit, 0)

    def zpush(k, buf, land, ss, rs):
        j = far_first(k, at.z, nz)
        return remote(buf.at[k], land.at[at.z], ss.at[k], rs.at[at.z], at.dp, 2 * j + at.c)

    def o_total(k):
        def put(v):
            oz[k] = v.astype(LOW)

        so(k).either("total", put)
        pl.when(k < nz - 1)(lambda: zpush(k, oz, olz, ozs, ozr).start())

    def q_total(k):
        def put(v):
            qz[k] = v.astype(LOW)

        sq(k).either("total", put)
        pl.when(k < nz - 1)(lambda: zpush(k, qz, qlz, qzs, qzr).start())

    dkv[...] = jnp.zeros_like(dkv)
    dxn1[...] = jnp.zeros_like(dxn1)
    here = at.z * KT + lax.broadcasted_iota(jnp.int32, (1, KT), 1)
    low_row = lo_row[0:1, :]

    def unit(k, _):
        j = far_first(k, at.z, nz)
        for hh in range(NH):
            cols = pl.ds(pl.multiple_of(j * HC + hh * HD, HD), HD)
            hid = j * NH + hh
            lrow = lse[pl.ds(hid, 1), :]
            qh = qs[:, cols]
            doh = dos[:, cols]
            delta = jnp.sum((doh.astype(F32) * os_[:, cols].astype(F32)).T, axis=0, keepdims=True)
            dq[...] = jnp.zeros_like(dq)

            def tile(b, _):
                kr_ = pl.ds(pl.multiple_of(b * KT, KT), KT)
                kt = kvs[kr_, pl.ds(0, HD)]
                vt = kvs[kr_, pl.ds(HD, HD)]
                s = dot_nt(kt, qh)
                place = b * KT + lax.broadcasted_iota(jnp.int32, (KT, KT), 0)
                s = jnp.where((place >= low_row) & (place <= here), s * scale, MASKED)
                p = jnp.exp(s - lrow)
                dkv[kr_, pl.ds(HD, HD)] += dot_nn(p.astype(LOW), doh)
                ds = (p * (dot_nt(vt, doh) - delta)).astype(LOW)
                dkv[kr_, pl.ds(0, HD)] += dot_nn(ds, qh)
                dq[...] += dot_tn(ds, kt)
                return 0

            lax.fori_loop(0, at.z + 1, tile, 0)
            u = dq[...] * scale
            qs[:, cols] = (u * cosf[...] - swap_halves(u) * sins[...]).astype(LOW)
        dqp = qs[:, hcols(j)]

        def back(o, _):
            dxn1[:, drows(o)] += dot_nt(dqp, wq[j, drows(o), :])
            wq[j, drows(o), :] = dot_tn(xn1[:, drows(o)], dqp).astype(LOW)
            return 0

        lax.fori_loop(0, nd, back, 0)
        sq(k).either("start")
        pl.when(k >= 1)(lambda: so(k - 1).either("middle"))
        pl.when(k >= 2)(lambda: o_total(k - 2))
        return 0

    lax.fori_loop(0, nz, unit, 0)

    dkv[:, pl.ds(0, HD)] = dkv[:, pl.ds(0, HD)] * scale
    kvb[...] = dkv[...].astype(LOW)
    kswap = [remote(kvb.at[rows(2 * zz + 1 - at.c)], kland.at[zz], ks.at[zz], kr.at[zz], at.dp, at.sibling()) for zz in range(nz)]
    for cp in kswap:
        cp.start()
    swap_dh1.wait_send()
    dh1b[mine, :] = dxn1[theirs, :].astype(LOW)
    xswap = remote(dh1b.at[mine], xrecv, xsem.at[2], xsem.at[3], at.dp, at.sibling())
    xswap.start()

    def kpush(s):
        zz = lax.rem(at.z + s, nz)
        return remote(kvb.at[rows(2 * zz + at.c)], kz.at[s - 1], kzs.at[s - 1], kzr.at[s - 1], at.dp, 2 * zz + at.c)

    k_last = jnp.int32(nz - 1)
    so(k_last).either("middle")
    for s in range(1, nz + 1):
        zz = lax.rem(at.z + s, nz)
        r = rows(2 * zz + at.c)
        remote(kvb.at[rows(0)], kland.at[zz], ks.at[zz], kr.at[zz], at.dp, at.sibling()).wait_recv()
        dkv[r, :] = dkv[r, :] + kland[zz].astype(F32)
        if s < nz:
            kvb[r, :] = dkv[r, :].astype(LOW)
            kpush(s).start()

    lax.fori_loop(0, max(nz - 2, 1), lambda k, _: (sq(k).either("middle"), 0)[1], 0)
    if nz >= 2:
        o_total(jnp.int32(nz - 2))
    total = dkv[rows(at.t), :] + later[...].astype(F32)
    for s in range(1, nz):
        kpush(s).wait_recv()
        total = total + kz[s - 1].astype(F32)
    dk = total[:, :HD]
    dk = dk * cosf[mine, :] - swap_halves(dk) * sins[mine, :]
    dkvp = jnp.concatenate([dk, total[:, HD:]], axis=1).astype(LOW)


    slices = lambda t: pl.ds(pl.multiple_of(t * Ds, Ds), Ds)

    def wswap(zz):
        return remote(wd2.at[slices(2 * zz + 1 - at.c)], wcl.at[zz], wcs.at[zz], wcr.at[zz], at.dp, at.sibling())

    def wpush(s):
        zz = lax.rem(at.z + s, nz)
        return remote(wd2.at[slices(2 * zz + at.c)], wl.at[s - 1], ws.at[s - 1], wr.at[s - 1], at.dp, 2 * zz + at.c)

    def upush(s):
        tt = lax.rem(at.t + s, nt)
        return remote(gpart.at[:, slices(tt)], gl.at[at.t], us.at[s - 1], ur.at[at.t], at.dp, tt)

    for o in range(nd):
        wd2[pl.ds(o * Dd, Dd), :] = dot_tn(xn1[mine, pl.ds(o * Dd, Dd)], dkvp).astype(LOW)
    for zz in range(nz):
        wswap(zz).start()
    lax.fori_loop(max(nz - 2, 1), nz, lambda k, _: (sq(k).either("middle"), 0)[1], 0)
    big = []
    for n, (buf, got, second) in enumerate([(bg, tg, lg), (bu, tu, lu), (bd, td, ld), (be, te, le)]):
        if n < 2:
            loads[n].wait()
            loads[2 + n].wait()
        elif n == 2:
            for cp in loads[13:]:
                cp.wait()
            for cp in down_hops:
                cp.wait_recv()
        if n % 2 == 0:
            keep, keep_slots = at.x, [(s - 1) * nx + at.x for s in range(1, ny)]
            away = [(1 - at.x, [(s - 1) * nx + 1 - at.x for s in range(1, ny)], at.x_peer())]
        else:
            keep, keep_slots = at.y, [at.y]
            away = [(lax.rem(at.y + s, ny), [lax.rem(at.y + s, ny)], at.y_peer(s)) for s in range(1, ny)]
        copies = []
        for i, (place, slots, peer) in enumerate(away):
            total = buf[place].astype(F32)
            for slot in slots:
                total = total + got[slot].astype(F32)
            buf[place] = total.astype(LOW)
            copies.append(remote(buf.at[place], second.at[i], fs.at[n, i], fr.at[n, i], peer, at.t))
            copies[-1].start()
        total = buf[keep].astype(F32)
        for slot in keep_slots:
            total = total + got[slot].astype(F32)
        buf[keep] = total.astype(LOW)
        big.append((buf, keep, second, copies))

    for s in range(1, nz + 1):
        zz = lax.rem(at.z + s, nz)
        r = slices(2 * zz + at.c)
        remote(wd2.at[slices(0)], wcl.at[zz], wcs.at[zz], wcr.at[zz], at.dp, at.sibling()).wait_recv()
        wd2[r, :] = (wd2[r, :].astype(F32) + wcl[zz].astype(F32)).astype(LOW)
        if s < nz:
            wpush(s).start()
    o_total(k_last)

    xswap.wait_recv()
    for o in range(nd):
        cols = pl.ds(o * Dd, Dd)
        dxn1[mine, cols] = dxn1[mine, cols] + xrecv[:, cols].astype(F32) + dot_nt(dkvp, wkv[cols, :])

    def put_tokens(cols, v):
        tgrad[:, cols] = tgrad[:, cols] + v

    rms_back(lambda cols: tok[:, cols].astype(F32), lambda cols: dxn1[mine, cols], 0, put_tokens)
    for s in range(1, nt):
        upush(s).start()

    lax.fori_loop(0, max(nz - 2, 1), lambda k, _: (q_total(k), 0)[1], 0)

    per = nt // nd
    gl[at.t] = gpart[:, slices(at.t)]
    wsum = wd2[slices(at.t), :].astype(F32)
    for s in range(1, nz):
        wpush(s).wait_recv()
        wsum = wsum + wl[s - 1].astype(F32)
    for s in range(1, nt):
        o = lax.rem(at.t + s, nt)
        remote(gpart.at[:, pl.ds(0, Ds)], gl.at[o], us.at[s - 1], ur.at[o], at.dp, o).wait_recv()
    usum = gl[0]
    for o in range(1, nt):
        usum = usum + gl[o]
    owner = at.t // per
    is_owner = at.dp == owner
    slot = jnp.where(is_owner, at.t - at.dp * per, 0)
    w2[...] = wsum.astype(LOW)
    u2[...] = usum
    to = jnp.where(is_owner, lax.rem(at.dp + 1, nd), owner)
    give_w = remote(w2, w2l.at[at.dp], w2s.at[0], w2r.at[at.dp], to, at.t)
    give_u = remote(u2, u2l.at[at.dp], u2s.at[0], u2r.at[at.dp], to, at.t)

    def spread(q, i, t):
        return [remote(wfin.at[q], wfin.at[q], w3s.at[q, i], w3r.at[q], at.dp, t),
                remote(gfin.at[q], gfin.at[q], u3s.at[q, i], u3r.at[q], at.dp, t)]

    def spread_along(s):
        return spread(slot, s, 2 * lax.rem(at.z + s, nz) + at.c)

    @pl.when(jnp.logical_not(is_owner))
    def _():
        give_w.start()
        give_u.start()

    lax.fori_loop(max(nz - 2, 1), nz, lambda k, _: (q_total(k), 0)[1], 0)

    def square(v):
        return jnp.sum(v * v, axis=(0, 1), keepdims=True)

    share[...] = jnp.zeros_like(share)

    @pl.when(is_owner)
    def _():
        w2l[at.dp] = w2[...]
        u2l[at.dp] = u2[...]
        for s in range(1, nd):
            o = lax.rem(at.dp + s, nd)
            remote(w2, w2l.at[o], w2s.at[0], w2r.at[o], o, at.t).wait_recv()
            remote(u2, u2l.at[o], u2s.at[0], u2r.at[o], o, at.t).wait_recv()
        wtot = w2l[0].astype(F32)
        utot = u2l[0]
        for o in range(1, nd):
            wtot = wtot + w2l[o].astype(F32)
            utot = utot + u2l[o]
        wfin[slot] = wtot.astype(LOW)
        gfin[slot] = utot
        shared = square(wtot.astype(LOW).astype(F32)) + square(utot)
        share[...] = jnp.broadcast_to(shared, share.shape)
        for s in range(1, nz):
            for cp in spread_along(s):
                cp.start()

    squares = jnp.zeros((1, 1), F32)
    out_copies = []
    for n, (buf, keep, second, copies) in enumerate(big):
        total = buf[keep].astype(F32)
        for i, cp in enumerate(copies):
            cp.wait_recv()
            total = total + second[i].astype(F32)
        squares = squares + square(total)
        out_copies.append(pltpu.make_async_copy(second, (got_g, got_u, got_d, got_e)[n], outs.at[n]))
        out_copies.append(pltpu.make_async_copy(buf.at[keep], (keep_g, keep_u, keep_d, keep_e)[n], outs.at[4 + n]))
        for cp in out_copies[-2:]:
            cp.start()
    own_k = nz - 1
    for buf, land, ss, rs, out in ((oz, olz, ozs, ozr, go_out), (qz, qlz, qzs, qzr, gq_out)):
        total = buf[own_k].astype(F32)
        for s in range(1, nz):
            zz = lax.rem(at.z + s, nz)
            remote(buf.at[0], land.at[zz], ss.at[0], rs.at[zz], at.dp, at.sibling()).wait_recv()
            total = total + land[zz].astype(F32)
        squares = squares + square(total)
        out[...] = total
    squares = squares + share[0:1, 0:1]

    norms[at.t] = jnp.broadcast_to(squares, norms.shape[1:])

    def npush(s):
        return remote(norms.at[at.t], norms.at[at.t], ns.at[s - 1], nr.at[at.t], at.dp, lax.rem(at.t + s, nt))

    def n2push(s):
        return remote(normd.at[at.dp], normd.at[at.dp], n2s.at[s - 1], n2r.at[at.dp], lax.rem(at.dp + s, nd), at.t)

    for s in range(1, nt):
        npush(s).start()
    for s in range(1, nt):
        o = lax.rem(at.t + s, nt)
        remote(norms.at[o], norms.at[o], ns.at[s - 1], nr.at[o], at.dp, o).wait_recv()
    group = norms[0]
    for o in range(1, nt):
        group = group + norms[o]
    normd[at.dp] = group
    for s in range(1, nd):
        n2push(s).start()
    for s in range(1, nd):
        o = lax.rem(at.dp + s, nd)
        remote(normd.at[o], normd.at[o], n2s.at[s - 1], n2r.at[o], o, at.t).wait_recv()
    group = normd[0]
    for o in range(1, nd):
        group = group + normd[o]
    norm_out[...] = jnp.sqrt(group)

    for q in range(per):
        t_from = at.dp * per + q
        same = at.c == lax.rem(t_from, 2)

        def slice_came(q=q):
            for cp in spread(q, 0, at.sibling()):
                cp.wait_recv()

        pl.when(at.t != t_from)(slice_came)

        @pl.when(same)
        def _(q=q):
            for cp in spread(q, 0, at.sibling()):
                cp.start()

        gkv_out[pl.ds(q * Ds, Ds), :] = wfin[q].astype(F32)
        gg_out[:, pl.ds(q * Ds, Ds)] = gfin[q]

        @pl.when(same)
        def _(q=q):
            for cp in spread(q, 0, at.sibling()):
                cp.wait_send()

    for cp in out_copies:
        cp.wait()
    for cp in down_hops:
        cp.wait_send()
    xswap.wait_send()
    for _, _, _, copies in big:
        for cp in copies:
            cp.wait_send()
    for cp in kswap:
        cp.wait_send()
    for s in range(1, nz):
        kpush(s).wait_send()
    for zz in range(nz):
        wswap(zz).wait_send()
    for s in range(1, nz):
        wpush(s).wait_send()
    for s in range(1, nt):
        upush(s).wait_send()
        npush(s).wait_send()
    for s in range(1, nd):
        n2push(s).wait_send()

    def drain(k, _):
        so(k).either("drain")
        sq(k).either("drain")

        @pl.when(k < nz - 1)
        def _():
            zpush(k, oz, olz, ozs, ozr).wait_send()
            zpush(k, qz, qlz, qzs, qzr).wait_send()

        return 0

    lax.fori_loop(0, nz, drain, 0)

    @pl.when(jnp.logical_not(is_owner))
    def _():
        give_w.wait_send()
        give_u.wait_send()

    @pl.when(is_owner)
    def _():
        for s in range(1, nz):
            for cp in spread_along(s):
                cp.wait_send()


def grads(nd, nt, small, big_in, pieces):
    R, D = small[1].shape
    nz, ny = nt // 2, nd // 2
    h1, dxn2, xn1, wq, wo, wkv, kv, q, o = big_in
    Dd, HC = wo.shape[2], wq.shape[2]
    F = pieces[0].shape[1]
    Fh = F // 2
    S = R * nt
    Ds = D // nt
    W2 = 2 * HD
    slots = max(2 * (ny - 1), ny)
    hops = max(1, ny - 1)
    dma = lambda *s: pltpu.SemaphoreType.DMA(s)
    hbm = pl.BlockSpec(memory_space=pltpu.HBM)
    vm = pl.BlockSpec(memory_space=pltpu.VMEM)
    b = lambda *s: pltpu.VMEM(s, LOW)
    f = lambda *s: pltpu.VMEM(s, F32)
    shapes = [(R, D), (Dd, HC), (HC, Dd), (Dd, W2), (8, Dd), (8, 128)]
    lows = [(F, Dd), (F, Dd), (Fh, Dd), (Fh, Dd), (1, F, Dd), (hops, F, Dd), (1, Fh, Dd), (hops, Fh, Dd)]
    return pl.pallas_call(
        functools.partial(grads_kernel, nd, nt),
        out_shape=tuple([jax.ShapeDtypeStruct(s, F32) for s in shapes] + [jax.ShapeDtypeStruct(s, LOW) for s in lows]),
        in_specs=[vm] * 8 + [hbm] * 14,
        out_specs=(vm,) * 6 + (hbm,) * 8,
        scratch_shapes=[
            b(2 * R, D), b(nz, D, HC), b(nd, nz * HC, Dd), b(D, W2), b(S, W2), b(2 * R, nz * HC), b(2 * R, nz * HC), b(2 * R, nz * HC),
            b(2 * R, D), f(2 * R, D), f(S, W2), f(2 * R, HD),
            b(2, F, Dd), b(ny, F, Dd), b(2, Fh, Dd), b(ny, Fh, Dd),
            b(1, F, Dd), b(hops, F, Dd), b(1, Fh, Dd), b(hops, Fh, Dd),
            b(2 * (ny - 1), F, Dd), b(ny, F, Dd), b(2 * (ny - 1), Fh, Dd), b(ny, Fh, Dd),
            b(nz, slots, Dd, HC), b(nz, hops, Dd, HC), b(nz, slots, HC, Dd), b(nz, hops, HC, Dd),
            b(nz, Dd, HC), b(nz, HC, Dd), b(nz, Dd, HC), b(nz, HC, Dd),
            b(S, W2), b(nz, R, W2), b(nz, R, W2), b(R, D),
            b(nz, Ds, W2), b(nz, Ds, W2), b(D, W2), b(Ds, W2), b(nd, Ds, W2), b(nt // nd, Ds, W2),
            f(nt, 8, Ds), f(8, D), f(8, Ds), f(nd, 8, Ds), f(nt // nd, 8, Ds), f(8, 128), f(nt, 8, 128), f(nd, 8, 128),
            dma(13 + 2 + ny), dma(4), dma(4, hops), dma(4, hops),
            dma(nz, slots), dma(nz, slots), dma(nz, hops), dma(nz, hops), dma(nz, slots), dma(nz, slots), dma(nz, hops), dma(nz, hops),
            dma(nz), dma(nz), dma(nz), dma(nz),
            dma(nz), dma(nz), dma(nz), dma(nz),
            dma(nz), dma(nz), dma(nz), dma(nz), dma(1), dma(nd), dma(nt // nd, nz), dma(nt // nd),
            dma(nt), dma(nt), dma(1), dma(nd), dma(nt // nd, nz), dma(nt // nd),
            dma(nt), dma(nt), dma(nd), dma(nd), dma(8), dma(2, slots), dma(2, slots),
        ],
        compiler_params=pltpu.CompilerParams(collective_id=3, has_side_effects=True, vmem_limit_bytes=63 << 20),
        cost_estimate=pl.CostEstimate(flops=30 << 30, bytes_accessed=40 << 20, transcendentals=8 * 512 * 2048),
        name="grads",
    )(*small, *big_in, *pieces)


def advance(grad_raw, weight, moment, average, factor, rate):
    average_decay = min(AVERAGE_TOP, (1.0 + STEP) / (10.0 + STEP))
    clipped = grad_raw * factor
    moment_new = MOMENTUM * moment + clipped
    weight_new = weight - rate * (clipped + MOMENTUM * moment_new)
    average_new = average_decay * average + (1.0 - average_decay) * weight_new
    return (clipped, moment_new, average_new, weight_new, weight_new.astype(jnp.bfloat16))


def local(
    tokens,
    cotangent,
    kv_later,
    lengths,
    query_weight,
    query_moment,
    query_average,
    keyvalue_weight,
    keyvalue_moment,
    keyvalue_average,
    output_weight,
    output_moment,
    output_average,
    gateup_weight,
    gateup_moment,
    gateup_average,
    down_weight,
    down_moment,
    down_average,
    norm_gains,
    gains_moment,
    gains_average,
):
    masters = (query_weight, keyvalue_weight, output_weight, gateup_weight, down_weight, norm_gains)
    low_query, low_kv, low_output, _, _, low_gains = (w.astype(LOW) for w in masters)
    low_gateup = jnp.swapaxes(gateup_weight, 1, 2).astype(LOW)
    low_down = down_weight.astype(LOW)
    nd, nt = lax.axis_size("dp"), lax.axis_size("tensor")
    row_count = tokens.shape[0]
    pair_rows = 2 * row_count

    doc_lengths = lengths[0]
    endings = jnp.cumsum(doc_lengths)
    beginnings = endings - doc_lengths
    places = (lax.axis_index("tensor") // 2) * pair_rows + jnp.arange(pair_rows, dtype=jnp.int32)
    segment = jnp.sum((places[:, None] >= endings[None, :]).astype(jnp.int32), axis=1)
    picked = segment[:, None] == jnp.arange(doc_lengths.shape[0], dtype=jnp.int32)[None, :]
    first = jnp.sum(jnp.where(picked, beginnings[None, :], 0), axis=1).astype(jnp.int32)
    half_size = HD // 2
    frequency = jnp.exp(jnp.arange(half_size, dtype=F32) * (-2.0 * math.log(ROPE_BASE) / HD))
    angles = (places - first).astype(F32)[:, None] * frequency[None, :]
    cosine, sine = jnp.cos(angles), jnp.sin(angles)
    cosine_full = jnp.concatenate([cosine, cosine], axis=1)
    sine_full = jnp.concatenate([-sine, sine], axis=1)
    first_rows = jnp.broadcast_to(first[None, :], (8, pair_rows))
    gain_rows = jnp.pad(low_gains.astype(F32), ((0, 6), (0, 0)))

    hidden_one, normed_two, gains_all, lse, normed_one, all_query, all_output, all_kv, kv_rows, queries, attended, grad_rows, gate_up = attend(
        nd, nt, tokens, gain_rows, low_query, low_kv, low_output, cosine_full, sine_full, first_rows,
        cotangent, low_gateup
    )
    grad_normed_two, *pieces, mlp_rows = mlp(nd, nt, normed_two, grad_rows, gate_up, low_down)
    cores = [list(range(core, nt, 2)) for core in range(2)]
    mlp_own = lax.psum_scatter(mlp_rows, "tensor", scatter_dimension=0, axis_index_groups=cores, tiled=False)
    mixed = hidden_one + mlp_own.astype(F32)
    tokens_grad, own_query, own_output, grad_keyvalue, gains_sum, norm_tile, *halves = grads(
        nd,
        nt,
        (cotangent, tokens, gains_all, cosine_full, sine_full, first_rows, lse, kv_later),
        (hidden_one, grad_normed_two, normed_one, all_query, all_output, all_kv, kv_rows, queries, attended),
        pieces,
    )
    whole = [kept.astype(F32) + jnp.sum(got.astype(F32), axis=0) for kept, got in zip(halves[:4], halves[4:])]
    own_gateup = jnp.swapaxes(jnp.stack(whole[:2]), 1, 2)
    own_down = jnp.concatenate(whole[2:], axis=0)
    grad_gains = gains_sum[:2]
    grad_norm = norm_tile[0, 0]
    factor = jnp.minimum(1.0, CLIP / (grad_norm + 1e-06))
    query_set = advance(
        own_query, query_weight, query_moment, query_average, factor, LEARNING_RATES[0]
    )
    keyvalue_set = advance(
        grad_keyvalue, keyvalue_weight, keyvalue_moment, keyvalue_average, factor, LEARNING_RATES[1]
    )
    output_set = advance(
        own_output, output_weight, output_moment, output_average, factor, LEARNING_RATES[2]
    )
    gateup_set = advance(
        own_gateup, gateup_weight, gateup_moment, gateup_average, factor, LEARNING_RATES[3]
    )
    down_set = advance(own_down, down_weight, down_moment, down_average, factor, LEARNING_RATES[4])
    gains_set = advance(
        grad_gains, norm_gains, gains_moment, gains_average, factor, LEARNING_RATES[5]
    )
    return (
        mixed,
        mixed.astype(jnp.bfloat16),
        tokens_grad,
        grad_norm,
        query_set[0],
        query_set[1],
        query_set[2],
        query_set[3],
        query_set[4],
        keyvalue_set[0],
        keyvalue_set[1],
        keyvalue_set[2],
        keyvalue_set[3],
        keyvalue_set[4],
        output_set[0],
        output_set[1],
        output_set[2],
        output_set[3],
        output_set[4],
        gateup_set[0],
        gateup_set[1],
        gateup_set[2],
        gateup_set[3],
        gateup_set[4],
        down_set[0],
        down_set[1],
        down_set[2],
        down_set[3],
        down_set[4],
        gains_set[0],
        gains_set[1],
        gains_set[2],
        gains_set[3],
        gains_set[4],
    )


def solution(mesh):
    return jax.shard_map(
        local,
        mesh=mesh,
        in_specs=(
            P(("dp", "tensor"), None),
            P(("dp", "tensor"), None),
            P(("dp", "tensor"), None),
            P("dp", None),
            P("dp", "tensor"),
            P("dp", "tensor"),
            P("dp", "tensor"),
            P("dp", None),
            P("dp", None),
            P("dp", None),
            P("tensor", "dp"),
            P("tensor", "dp"),
            P("tensor", "dp"),
            P(None, "dp", "tensor"),
            P(None, "dp", "tensor"),
            P(None, "dp", "tensor"),
            P("tensor", "dp"),
            P("tensor", "dp"),
            P("tensor", "dp"),
            P(None, "dp"),
            P(None, "dp"),
            P(None, "dp"),
        ),
        out_specs=(
            P(("dp", "tensor"), None),
            P(("dp", "tensor"), None),
            P(("dp", "tensor"), None),
            P(),
            P("dp", "tensor"),
            P("dp", "tensor"),
            P("dp", "tensor"),
            P("dp", "tensor"),
            P("dp", "tensor"),
            P("dp", None),
            P("dp", None),
            P("dp", None),
            P("dp", None),
            P("dp", None),
            P("tensor", "dp"),
            P("tensor", "dp"),
            P("tensor", "dp"),
            P("tensor", "dp"),
            P("tensor", "dp"),
            P(None, "dp", "tensor"),
            P(None, "dp", "tensor"),
            P(None, "dp", "tensor"),
            P(None, "dp", "tensor"),
            P(None, "dp", "tensor"),
            P("tensor", "dp"),
            P("tensor", "dp"),
            P("tensor", "dp"),
            P("tensor", "dp"),
            P("tensor", "dp"),
            P(None, "dp"),
            P(None, "dp"),
            P(None, "dp"),
            P(None, "dp"),
            P(None, "dp"),
        ),
        check_vma=False,
    )
```

```python
import functools
import math

import jax
import jax.numpy as jnp
from jax import lax
from jax.experimental import pallas as pl
from jax.experimental.pallas import tpu as pltpu
from jax.sharding import PartitionSpec as P

HD = 128
STEP = 10


EPSILON = 1e-05
MASKED = -1000000000.0
CLIP = 1.0
MOMENTUM = 0.9
LEARNING_RATES = (12.0, 12.0, 480.0, 48.0, 12.0, 960.0)
AVERAGE_TOP = 0.999
ROPE_BASE = 10000.0
MESH = pl.DeviceIdType.MESH
LOW = jnp.bfloat16
F32 = jnp.float32


def dot_nn(a, b):
    return jnp.dot(a, b, preferred_element_type=F32)


def dot_nt(a, b):
    return lax.dot_general(a, b, (((1,), (1,)), ((), ())), preferred_element_type=F32)


def dot_tn(a, b):
    return lax.dot_general(a, b, (((0,), (0,)), ((), ())), preferred_element_type=F32)


class Place:
    def __init__(self, nd, nt):
        self.nd, self.nt = nd, nt
        self.nx = 2 if nd % 2 == 0 else 1
        self.ny = nd // self.nx
        self.nz = nt // 2
        self.dp = lax.axis_index("dp")
        self.t = lax.axis_index("tensor")
        self.y = self.dp // self.nx
        self.x = lax.rem(self.dp, self.nx)
        self.z = self.t // 2
        self.c = lax.rem(self.t, 2)

    def x_peer(self):
        return self.y * self.nx + (1 - self.x)

    def y_peer(self, step):
        return lax.rem(self.y + step, self.ny) * self.nx + self.x

    def xy_peer(self, step):
        return lax.rem(self.y + step, self.ny) * self.nx + (1 - self.x)

    def sibling(self):
        return self.z * 2 + (1 - self.c)


def remote(src, dst, send, recv, dp, t):
    return pltpu.make_async_remote_copy(src, dst, send, recv, device_id=(dp, t), device_id_type=MESH)


def greet(at, dps=True, zs=True, core=True):
    bar = pltpu.get_barrier_semaphore()
    count = 0
    targets = []
    if dps:
        targets.append((at.x_peer(), at.t))
        targets += [(at.y_peer(s), at.t) for s in range(1, at.ny)]
    if core:
        targets.append((at.dp, at.sibling()))
    for target in targets:
        pl.semaphore_signal(bar, inc=1, device_id=target, device_id_type=MESH)
        count += 1
    if zs:
        @pl.when(at.z > 0)
        def _():
            pl.semaphore_signal(bar, inc=1, device_id=(at.dp, at.t - 2), device_id_type=MESH)

        @pl.when(at.z < at.nz - 1)
        def _():
            pl.semaphore_signal(bar, inc=1, device_id=(at.dp, at.t + 2), device_id_type=MESH)

        count = count + (at.z > 0).astype(jnp.int32) + (at.z < at.nz - 1).astype(jnp.int32)
    pl.semaphore_wait(bar, count)


def far_first(k, z, nz):
    j = nz - 1 - k
    m = jnp.minimum(z, nz - 1 - z)
    s = (j + 1) // 2
    two = jnp.where(lax.rem(j, 2) == 1, z - s, z + s)
    one = jnp.where(z < nz - 1 - z, j, nz - 1 - j)
    return jnp.where(j <= 2 * m, two, one)


def near_first(k, z, nz):
    return far_first(nz - 1 - k, z, nz)


class Gather:
    def __init__(self, at, src, dst, xs, ys, xf, yf, recv, kind):
        self.at, self.src, self.dst, self.kind = at, src, dst, kind
        self.xs, self.ys, self.xf, self.yf, self.recv = xs, ys, xf, yf, recv

    def own(self):
        at = self.at
        out = [remote(self.src, self.dst(at.dp), self.xs, self.recv.at[at.dp], at.x_peer(), at.t)]
        for s in range(1, at.ny):
            out.append(remote(self.src, self.dst(at.dp), self.ys.at[s - 1], self.recv.at[at.dp], at.y_peer(s), at.t))
        return out

    def passed(self):
        at = self.at
        out = []
        for s in range(1, at.ny):
            if self.kind == 0:
                o = at.x_peer()
                out.append(remote(self.dst(o), self.dst(o), self.yf.at[s - 1], self.recv.at[o], at.y_peer(s), at.t))
            else:
                o = at.y_peer(s)
                out.append(remote(self.dst(o), self.dst(o), self.xf.at[s - 1], self.recv.at[o], at.x_peer(), at.t))
        return out

    def arrived(self, o):
        remote(self.src, self.dst(o), self.xs, self.recv.at[o], self.at.x_peer(), self.at.t).wait_recv()

    def start(self):
        for cp in self.own():
            cp.start()

    def forward(self):
        at = self.at
        if self.kind == 0:
            self.arrived(at.x_peer())
        else:
            for s in range(1, at.ny):
                self.arrived(at.y_peer(s))
        for cp in self.passed():
            cp.start()

    def finish(self):
        at = self.at
        if self.kind == 0:
            for s in range(1, at.ny):
                self.arrived(at.y_peer(s))
        else:
            self.arrived(at.x_peer())
        for s in range(1, at.ny):
            self.arrived(at.xy_peer(s))

    def either(self, name):
        kind = self.kind
        for value in range(2):
            self.kind = value
            pl.when(kind == value)(getattr(self, name))
        self.kind = kind

    def finish_any(self):
        self.either("finish")

    def forward_any(self):
        self.either("forward")

    def drain_any(self):
        self.either("drain")

    def drain(self):
        for cp in self.own() + self.passed():
            cp.wait_send()


def mlp_kernel(nd, nt, xn_in, dy_in, w_all, w_in,
               dxn_out, mine_g, land_g, mine_u, land_u, down_out, out_out,
               both, wts, act, psend, pown, precv, zrecv, bsend, bown, bland,
               lsem, wx, wy, wxf, wyf, wr, ar, ac, asr, asl, ps, pr, zs, zr, bs, br, osem, dsem, p1l, p1s, p1r):
    at = Place(nd, nt)
    nz, nx, ny = at.nz, at.nx, at.ny
    R, D = xn_in.shape
    F, Dd = w_in.shape
    Fh = F // 2
    CH = zs.shape[1]
    CR = R // CH
    rows = lambda t: pl.ds(pl.multiple_of(t * R, R), R)
    dcols = lambda o: pl.ds(pl.multiple_of(o * Dd, Dd), Dd)
    xall, dyv = both.at[0], both.at[1]

    own_loads = [
        pltpu.make_async_copy(xn_in, xall.at[rows(at.t)], lsem.at[0]),
        pltpu.make_async_copy(dy_in, dyv, lsem.at[1]),
        pltpu.make_async_copy(w_all, wts.at[pl.ds(0, 2)], lsem.at[2]),
        pltpu.make_async_copy(w_in, wts.at[2, :, dcols(at.dp)], lsem.at[3]),
    ]
    for cp in own_loads:
        cp.start()
    greet(at)

    gathers = []
    for p in range(2):
        half = pl.ds(p * Fh, Fh)
        gathers.append(Gather(at, w_in.at[half], lambda o, half=half: wts.at[2, half, dcols(o)],
                              wx.at[p], wy.at[p], wxf.at[p], wyf.at[p], wr.at[p], p))

    def right(o):
        return remote(xall.at[rows(o)], xall.at[rows(o)], asr.at[o], ar.at[o], at.dp, at.t + 2)

    def left(o):
        return remote(xall.at[rows(o)], xall.at[rows(o)], asl.at[o], ar.at[o], at.dp, at.t - 2)

    def across(o):
        return remote(xall.at[rows(o)], xall.at[rows(o)], ac.at[o], ar.at[o], at.dp, at.sibling())

    own_loads[0].wait()
    pl.when(at.z < nz - 1)(lambda: right(at.t).start())
    pl.when(at.z > 0)(lambda: left(at.t).start())
    across(at.t).start()
    for g in gathers:
        g.start()

    def line_step(s):
        @pl.when(at.z - s >= 0)
        def _():
            o = at.t - 2 * s
            across(o).wait_recv()
            pl.when(at.z < nz - 1)(lambda: right(o).start())
            across(o).start()

        @pl.when(at.z + s < nz)
        def _():
            o = at.t + 2 * s
            across(o).wait_recv()
            pl.when(at.z > 0)(lambda: left(o).start())
            across(o).start()

    for g in gathers:
        g.forward()
    for cp in own_loads[1:]:
        cp.wait()

    is_end = (at.z == 0) | (at.z == nz - 1)
    piece = lambda c: pl.ds(pl.multiple_of(c * CR, CR), CR)

    def swap(d):
        return remote(psend, precv.at[d], ps.at[0], pr.at[d], at.dp, at.sibling())

    def push_right(d, c):
        return remote(pown.at[d, piece(c)], zrecv.at[d, piece(c)], zs.at[d, c], zr.at[d, c], at.dp, at.t + 2)

    def push_left(d, c):
        slot = jnp.where(d == at.z - 1, nz, d)
        return remote(pown.at[d, piece(c)], zrecv.at[slot, piece(c)], zs.at[d, c], zr.at[slot, c], at.dp, at.t - 2)

    def came(slot, c):
        remote(pown.at[0, piece(c)], zrecv.at[slot, piece(c)], zs.at[0, c], zr.at[slot, c], at.dp, at.sibling()).wait_recv()

    def relay(d, c, push):
        pl.when(c == 0)(lambda: swap(d).wait_recv())

        @pl.when(is_end)
        def _():
            pown[d, piece(c)] = (pown[d, piece(c)].astype(F32) + precv[d, piece(c)].astype(F32)).astype(LOW)

        @pl.when(jnp.logical_not(is_end))
        def _():
            came(d, c)
            pown[d, piece(c)] = (pown[d, piece(c)].astype(F32) + precv[d, piece(c)].astype(F32)
                                 + zrecv[d, piece(c)].astype(F32)).astype(LOW)

        push(d, c).start()

    lower = at.z < nz - 1 - at.z

    def near_relay(s, c):
        pl.when(lower & (s > at.z))(lambda: relay(s, c, push_right))
        pl.when(jnp.logical_not(lower) & (nz - 1 - s < at.z))(lambda: relay(nz - 1 - s, c, push_left))

    def far_relay(s, c):
        pl.when(jnp.logical_not(lower) & (s > at.z))(lambda: relay(s, c, push_right))
        pl.when(lower & (nz - 1 - s < at.z))(lambda: relay(nz - 1 - s, c, push_left))

    def relays(s, c):
        pl.when(s > at.z)(lambda: relay(s, c, push_right))
        pl.when(nz - 1 - s < at.z)(lambda: relay(nz - 1 - s, c, push_left))

    def branch_swap(j):
        return remote(bsend, bland.at[j], bs.at[0], br.at[j], at.dp, at.sibling())

    def branch_copy(slot, j):
        return pltpu.make_async_copy(bown.at[slot], out_out.at[j], osem.at[slot])

    def turn(k):
        return near_first(jnp.where(k < 2, 1 - k, k), at.z, nz)

    def branch_sum(k):
        j = turn(k)
        slot = lax.rem(k, 2)
        branch_swap(j).wait_recv()

        def part(c, _):
            bown[slot, piece(c)] = (bown[slot, piece(c)].astype(F32) + bland[j, piece(c)].astype(F32)).astype(LOW)
            return 0

        lax.fori_loop(0, CH, part, 0)
        branch_copy(slot, j).start()

    def forward(j):
        r = pl.ds(pl.multiple_of(j * 2 * R, 2 * R), 2 * R)
        for lo in range(0, F, 256):
            part = pl.ds(lo, min(256, F - lo))
            gate, up = dot_nt(xall[r, :], wts[0, part, :]), dot_nt(xall[r, :], wts[1, part, :])
            dmid = dot_nt(dyv[r, :], wts[2, part, :])
            sig = 1.0 / (1.0 + jnp.exp(-gate))
            silu = gate * sig
            act[2, r, part] = (silu * up).astype(LOW)
            act[1, r, part] = (dmid * silu).astype(LOW)
            act[0, r, part] = (dmid * up * (sig * (1.0 + gate * (1.0 - sig)))).astype(LOW)

    def block(k, _):
        pl.when(k >= 2)(lambda: line_step(k))
        j = turn(k)
        across(2 * j + 1 - at.c).wait_recv()
        slot = lax.rem(k, 2)
        forward(j)
        pl.when(k >= 1)(lambda: swap(j).wait_send())
        r = pl.ds(pl.multiple_of(j * 2 * R, 2 * R), 2 * R)

        def back(o, _):
            cols = dcols(o)
            v = dot_nn(act[0, r, :], wts[0, :, cols]) + dot_nn(act[1, r, :], wts[1, :, cols])
            first = at.c == 0
            psend[:, cols] = jnp.where(first, v[R:], v[:R]).astype(LOW)
            pown[j, :, cols] = jnp.where(first, v[:R], v[R:]).astype(LOW)
            return 0

        lax.fori_loop(0, nd, back, 0)
        swap(j).start()
        s = jnp.where(is_end, jnp.where(k < 2, 1 - k, k), k - 1)

        @pl.when((s >= 1) & (is_end | (s < nz - 2)))
        def _():
            lax.fori_loop(0, CH, lambda c, _: (relays(s, c), 0)[1], 0)

        pl.when(k >= 1)(lambda: branch_sum(k - 1))
        pl.when(k >= 1)(lambda: branch_swap(j).wait_send())
        pl.when(k >= 2)(lambda: branch_copy(slot, j).wait())

        def branch(o, _):
            cols = dcols(o)
            v = dot_nn(act[2, r, :], wts[2, :, cols])
            first = at.c == 0
            bsend[:, cols] = jnp.where(first, v[R:], v[:R]).astype(LOW)
            bown[slot, :, cols] = jnp.where(first, v[:R], v[R:]).astype(LOW)
            return 0

        lax.fori_loop(0, nd, branch, 0)
        branch_swap(j).start()
        return 0

    if nz > 1:
        line_step(1)
    for g in gathers:
        g.finish()
    lax.fori_loop(0, nz, block, 0)
    swap(0).wait_send()
    branch_swap(0).wait_send()
    branch_sum(jnp.int32(nz - 1))
    for g in gathers:
        g.drain()

    outs = ((mine_g, land_g), (mine_u, land_u))

    def source(n, o):
        return wts.at[n, :, dcols(o)]

    def down_copy(o):
        return pltpu.make_async_copy(wts.at[2, :, dcols(o)], down_out.at[:, dcols(o)], dsem.at[o])

    def hop(n, o):
        mine, land = outs[n]
        yy, xx = o // nx, lax.rem(o, nx)
        if n % 2 == 0:
            step = lax.rem(yy - at.y + ny, ny)
            slot = (step - 1) * nx + xx
            stays, place, peer = yy == at.y, xx, yy * nx + at.x
        else:
            slot, stays, place, peer = yy, xx == at.x, yy, at.y * nx + xx
        local = pltpu.make_async_copy(source(n, o), mine.at[place], p1l.at[n, place])
        slot = jnp.where(stays, 0, slot)
        away = remote(source(n, o), land.at[slot], p1s.at[n, slot], p1r.at[n, slot], jnp.where(stays, at.x_peer(), peer), at.t)
        return stays, local, away

    def order(n, i):
        if n % 2 == 0:
            return lax.rem(at.y + 1 + i // nx, ny) * nx + lax.rem(i, nx)
        return lax.rem(i, ny) * nx + jnp.where(i < ny, 1 - at.x, at.x)

    def send(n, o):
        stays, local, away = hop(n, o)
        pl.when(stays)(lambda: local.start())
        pl.when(jnp.logical_not(stays))(lambda: away.start())

    def settle(n):
        def one(i, _):
            stays, local, away = hop(n, order(n, i))

            @pl.when(stays)
            def _():
                local.wait()

            @pl.when(jnp.logical_not(stays))
            def _():
                away.wait_send()
                away.wait_recv()

            return 0

        lax.fori_loop(0, nd, one, 0)

    def wgrad(p, _):
        n, i = p // nd, lax.rem(p, nd)
        middle = jnp.logical_not(is_end)
        early, late = p - 1, p // 2 - 3
        pl.when(middle & (early >= 0) & (early < CH))(lambda: relays(jnp.int32(nz - 2), early))
        turn_now = middle & (lax.rem(p, 2) == 0) & (late >= 0) & (late < CH - 1)
        pl.when(turn_now)(lambda: near_relay(jnp.int32(nz - 1), late))
        pl.when(turn_now & (late >= 1))(lambda: far_relay(jnp.int32(nz - 1), late - 1))
        o = jnp.where(n == 1, order(1, i), order(0, i))
        for lo in range(0, F, 384):
            part = pl.ds(lo, min(384, F - lo))
            wts[n, part, dcols(o)] = dot_tn(act[n, :, part], both[n // 2, :, dcols(o)]).astype(LOW)
        pl.when(n == 0)(lambda: send(0, o))
        pl.when(n == 1)(lambda: send(1, o))
        pl.when(n == 2)(lambda: down_copy(o).start())
        return 0

    lax.fori_loop(0, 3 * nd, wgrad, 0)

    @pl.when(jnp.logical_not(is_end))
    def _():
        near_relay(jnp.int32(nz - 1), jnp.int32(CH - 1))
        far_relay(jnp.int32(nz - 1), jnp.int32(CH - 2))
        far_relay(jnp.int32(nz - 1), jnp.int32(CH - 1))

    for slot in range(2):
        branch_copy(slot, 0).wait()

    swap(at.z).wait_recv()
    for c in range(CH):
        part = pl.ds(c * CR, CR)
        pl.when(at.z > 0)(lambda c=c: came(at.z, c))
        pl.when(at.z < nz - 1)(lambda c=c: came(nz, c))
        total = pown[at.z, part].astype(F32) + precv[at.z, part].astype(F32)
        total = total + jnp.where(at.z > 0, zrecv[at.z, part].astype(F32), 0.0)
        total = total + jnp.where(at.z < nz - 1, zrecv[nz, part].astype(F32), 0.0)
        dxn_out[part, :] = total.astype(LOW)

    for zz in range(nz):
        o = 2 * zz + at.c

        @pl.when(zz != at.z)
        def _(zz=zz):
            for c in range(CH):
                push_right(jnp.int32(zz), c).wait_send()

        across(o).wait_send()
        pl.when((at.z < nz - 1) & (zz <= at.z))(lambda o=o: right(o).wait_send())
        pl.when((at.z > 0) & (zz >= at.z))(lambda o=o: left(o).wait_send())
    for n in range(2):
        settle(n)
    for o in range(nd):
        down_copy(o).wait()


def mlp(nd, nt, xn, dy_all, w_all, w):
    R, D = xn.shape
    S = dy_all.shape[0]
    F, Dd = w.shape
    nz = nt // 2
    ny = nd // 2
    ch = 4
    dma = lambda *s: pltpu.SemaphoreType.DMA(s)
    shape = lambda *s: jax.ShapeDtypeStruct(s, LOW)
    b = lambda *s: pltpu.VMEM(s, LOW)
    slots = max(2 * (ny - 1), ny)
    hbm = pl.BlockSpec(memory_space=pltpu.HBM)
    vm = pl.BlockSpec(memory_space=pltpu.VMEM)
    return pl.pallas_call(
        functools.partial(mlp_kernel, nd, nt),
        out_shape=(
            shape(R, D),
            shape(2, F, Dd), shape(2 * (ny - 1), F, Dd), shape(ny, F, Dd), shape(ny, F, Dd),
            shape(F, D),
            shape(nz, R, D),
        ),
        in_specs=[hbm] * 4,
        out_specs=(vm,) + (hbm,) * 6,
        scratch_shapes=[
            b(2, S, D), b(3, F, D), b(3, S, F),
            b(R, D), b(nz, R, D), b(nz, R, D), b(nz + 1, R, D), b(R, D), b(2, R, D), b(nz, R, D),
            dma(4), dma(2), dma(2, ny - 1), dma(2, ny - 1), dma(2, ny - 1), dma(2, nd),
            dma(nt), dma(nt), dma(nt), dma(nt), dma(1), dma(nz), dma(nz, ch), dma(nz + 1, ch), dma(1), dma(nz), dma(2), dma(nd),
            dma(2, max(2, ny)), dma(2, slots), dma(2, slots),
        ],
        compiler_params=pltpu.CompilerParams(collective_id=1, has_side_effects=True, vmem_limit_bytes=63 << 20),
        cost_estimate=pl.CostEstimate(flops=12 * S * D * F, bytes_accessed=40 << 20, transcendentals=S * F),
        name="mlp",
    )(xn, dy_all, w_all, w)


def swap_halves(u):
    h = u.shape[-1] // 2
    return jnp.concatenate([u[:, h:], u[:, :h]], axis=1)


def greet_all(at):
    bar = pltpu.get_barrier_semaphore()
    for s in range(1, at.nd):
        pl.semaphore_signal(bar, inc=1, device_id=(lax.rem(at.dp + s, at.nd), at.t), device_id_type=MESH)
    for s in range(1, at.nt):
        pl.semaphore_signal(bar, inc=1, device_id=(at.dp, lax.rem(at.t + s, at.nt)), device_id_type=MESH)
    pl.semaphore_wait(bar, at.nd - 1 + at.nt - 1)


class Line:
    def __init__(self, at, view, right, left, recv, across=None):
        self.at, self.view, self.rs, self.ls, self.recv, self.across = at, view, right, left, recv, across

    def right(self, o):
        return remote(self.view(o), self.view(o), self.rs.at[o], self.recv.at[o], self.at.dp, self.at.t + 2)

    def left(self, o):
        return remote(self.view(o), self.view(o), self.ls.at[o], self.recv.at[o], self.at.dp, self.at.t - 2)

    def pass_on(self, o, to_right, to_left):
        at = self.at
        if to_right:
            pl.when(at.z < at.nz - 1)(lambda: self.right(o).start())
        if to_left:
            pl.when(at.z > 0)(lambda: self.left(o).start())
        if self.across is not None:
            self.across(o).start()

    def start(self):
        self.pass_on(self.at.z, True, True)

    def arrived(self, o):
        remote(self.view(o), self.view(o), self.rs.at[o], self.recv.at[o], self.at.dp, self.at.sibling()).wait_recv()

    def step(self, s):
        at = self.at

        @pl.when(at.z - s >= 0)
        def _():
            self.arrived(at.z - s)
            self.pass_on(at.z - s, True, False)

        @pl.when(at.z + s < at.nz)
        def _():
            self.arrived(at.z + s)
            self.pass_on(at.z + s, False, True)

    def drain(self):
        at = self.at
        for o in range(at.nz):
            pl.when((at.z < at.nz - 1) & (o <= at.z))(lambda o=o: self.right(o).wait_send())
            pl.when((at.z > 0) & (o >= at.z))(lambda o=o: self.left(o).wait_send())
            if self.across is not None:
                self.across(o).wait_send()


def attend_kernel(nd, nt, tok, gain, wq_in, wkv_in, wo_in, cosf, sins, lo_row, dy_in, w_in,
                  h1_out, xn2_out, gfull, lse_out,
                  xn1_out, wq_out, wo_out, wkv_out, kv_out, q_out, o_out, dy_all, w_all,
                  xn1, wq, wo, wkv, kvs, qs, os_, acc, pback, precv,
                  lsem, gs, gr, vx, vy, vxf, vyf, vr, qx, qy, qxf, qyf, qr, ox, oy, oxf, oyf, orr,
                  qlr, qll, qlv, olr, oll, olv, klr, kll, klv, klc, klcr, cs, cr, outs,
                  ylr, yll, ylv, ylc, mx, my, mxf, myf, mr, fsem):
    at = Place(nd, nt)
    nz = at.nz
    R, D = tok.shape
    Dd, HC = wq_in.shape
    rows = lambda t: pl.ds(pl.multiple_of(t * R, R), R)
    drows = lambda o: pl.ds(pl.multiple_of(o * Dd, Dd), Dd)
    hcols = lambda j: pl.ds(pl.multiple_of(j * HC, HC), HC)

    loads = [
        pltpu.make_async_copy(wkv_in, wkv.at[drows(at.dp)], lsem.at[0]),
        pltpu.make_async_copy(wq_in, wq.at[at.z, drows(at.dp)], lsem.at[1]),
        pltpu.make_async_copy(wo_in, wo.at[at.dp, hcols(at.z)], lsem.at[2]),
    ]
    for cp in loads:
        cp.start()
    gfull[at.dp] = gain[...]
    greet_all(at)

    def gain_copy(s):
        return remote(gain, gfull.at[at.dp], gs.at[s - 1], gr.at[s - 1], lax.rem(at.dp + s, nd), at.t)

    for s in range(1, nd):
        gain_copy(s).start()
    Dh = Dd // 2
    gkv = [Gather(at, wkv_in.at[pl.ds(p * Dh, Dh)], lambda o, p=p: wkv.at[pl.ds(pl.multiple_of(o * Dd + p * Dh, Dh), Dh)],
                  vx.at[p], vy.at[p], vxf.at[p], vyf.at[p], vr.at[p], p) for p in range(2)]

    def gq(k):
        j = near_first(k, at.z, nz)
        return Gather(at, wq.at[j, drows(at.dp)], lambda o: wq.at[j, drows(o)], qx.at[k], qy.at[k], qxf.at[k], qyf.at[k], qr.at[k], lax.rem(k, 2) if not isinstance(k, int) else k % 2)

    def go(k):
        j = near_first(k, at.z, nz)
        return Gather(at, wo.at[at.dp, hcols(j)], lambda o: wo.at[o, hcols(j)], ox.at[k], oy.at[k], oxf.at[k], oyf.at[k], orr.at[k], lax.rem(k, 2) if not isinstance(k, int) else k % 2)

    lq = Line(at, lambda o: wq.at[o, drows(at.dp)], qlr, qll, qlv)
    lo = Line(at, lambda o: wo.at[at.dp, hcols(o)], olr, oll, olv)

    def kv_view(o):
        return kvs.at[rows(2 * o + at.c)]

    def kv_across(o):
        return remote(kv_view(o), kv_view(o), klc.at[o], klcr.at[o], at.dp, at.sibling())

    lkv = Line(at, kv_view, klr, kll, klv, kv_across)

    for_mlp = [pltpu.make_async_copy(dy_in, dy_all.at[rows(at.t)], fsem.at[0]),
               pltpu.make_async_copy(w_in.at[0], w_all.at[0, :, drows(at.dp)], fsem.at[1]),
               pltpu.make_async_copy(w_in.at[1], w_all.at[1, :, drows(at.dp)], fsem.at[2])]
    for cp in for_mlp:
        cp.start()
    gw = [Gather(at, w_in.at[p], lambda o, p=p: w_all.at[p, :, drows(o)], mx.at[p], my.at[p], mxf.at[p], myf.at[p], mr.at[p], p)
          for p in range(2)]

    def dy_view(o):
        return dy_all.at[rows(2 * o + at.c)]

    def dy_across(o):
        return remote(dy_view(o), dy_view(o), ylc.at[o], ylv.at[1, o], at.dp, at.sibling())

    ldy = Line(at, dy_view, ylr, yll, ylv.at[0], dy_across)
    for g in gkv:
        g.start()
    loads[1].wait()
    lq.start()
    gq(0).start()

    for s in range(1, nd):
        gain_copy(s).wait_recv()

    def scaled(v, row, write):
        r = lax.rsqrt(jnp.mean(v * v, axis=-1, keepdims=True) + EPSILON)
        for o in range(nd):
            cols = pl.ds(o * Dd, Dd)
            write(cols, (v[:, o * Dd:(o + 1) * Dd] * r * gfull[o, row:row + 1, :]).astype(LOW))

    mine = rows(at.c)

    def put_xn1(cols, v):
        xn1[mine, cols] = v

    scaled(tok[...].astype(F32), 0, put_xn1)
    xn1_across = remote(xn1.at[mine], xn1.at[mine], cs.at[0], cr.at[0], at.dp, at.sibling())
    xn1_across.start()

    for g in gkv:
        g.forward()
    loads[0].wait()
    for g in gkv:
        g.finish()
    kvpre = dot_nn(xn1[mine, :], wkv[...])
    kk = kvpre[:, :HD]
    kvs[rows(at.t), pl.ds(0, HD)] = (kk * cosf[mine, :] + swap_halves(kk) * sins[mine, :]).astype(LOW)
    kvs[rows(at.t), pl.ds(HD, HD)] = kvpre[:, HD:].astype(LOW)
    lkv.start()
    loads[2].wait()
    lo.start()
    for s in range(1, nz):
        lq.step(s)
        gq(s).start()
        gq(s - 1).forward()
        lkv.step(s)
    gq(nz - 1).forward()
    xn1_across.wait_recv()
    go(0).start()
    for s in range(1, nz):
        lo.step(s)
        go(s).start()
    for_mlp[0].wait()
    ldy.start()
    for o in range(nz):
        kv_across(o).wait_recv()

    scale = 1.0 / math.sqrt(HD)
    KT = 2 * R
    here = at.z * KT + lax.broadcasted_iota(jnp.int32, (1, KT), 1)
    low_row = lo_row[0:1, :]

    def pair(k, _):
        j = near_first(k, at.z, nz)
        g = gq(k)
        g.finish_any()
        qpre = dot_nn(xn1[...], wq[j])
        for hh in range(HC // HD):
            u = qpre[:, hh * HD:(hh + 1) * HD]
            qs[:, pl.ds(pl.multiple_of(j * HC + hh * HD, HD), HD)] = (u * cosf[...] + swap_halves(u) * sins[...]).astype(LOW)

        for hh in range(HC // HD):
            cols = pl.ds(pl.multiple_of(j * HC + hh * HD, HD), HD)
            qh = qs[:, cols]
            acc[...] = jnp.zeros_like(acc)

            def tile(b, carry):
                top, total = carry
                kr = pl.ds(pl.multiple_of(b * KT, KT), KT)
                s = dot_nt(kvs[kr, pl.ds(0, HD)], qh)
                place = b * KT + lax.broadcasted_iota(jnp.int32, (KT, KT), 0)
                s = jnp.where((place >= low_row) & (place <= here), s * scale, MASKED)
                new_top = jnp.maximum(top, jnp.max(s, axis=0, keepdims=True))
                p = jnp.exp(s - new_top)
                fade = jnp.exp(top - new_top)
                acc[...] = acc[...] * fade + dot_tn(kvs[kr, pl.ds(HD, HD)], p.astype(LOW))
                return new_top, total * fade + jnp.sum(p, axis=0, keepdims=True)

            top, total = lax.fori_loop(0, at.z + 1, tile, (jnp.full((1, KT), MASKED, F32), jnp.zeros((1, KT), F32)))
            os_[:, cols] = (acc[...] / total).T.astype(LOW)
            lse_out[pl.ds(j * (HC // HD) + hh, 1), :] = top + jnp.log(total)
        go(k).forward_any()
        return 0

    lax.fori_loop(0, nz, pair, 0)
    for g in gw:
        g.start()
    ldy.step(1)
    keep = [
        pltpu.make_async_copy(xn1, xn1_out, outs.at[0]),
        pltpu.make_async_copy(wq, wq_out, outs.at[1]),
        pltpu.make_async_copy(wkv, wkv_out, outs.at[2]),
        pltpu.make_async_copy(kvs, kv_out, outs.at[3]),
        pltpu.make_async_copy(qs, q_out, outs.at[4]),
        pltpu.make_async_copy(os_, o_out, outs.at[5]),
    ]
    for cp in keep:
        cp.start()

    lax.fori_loop(0, nz, lambda k, _: (go(k).finish_any(), 0)[1], 0)
    keep.append(pltpu.make_async_copy(wo, wo_out, outs.at[6]))
    keep[-1].start()
    theirs = rows(1 - at.c)
    for o in range(nd):
        pback[:, pl.ds(o * Dd, Dd)] = dot_nn(os_[theirs, :], wo[o]).astype(LOW)
    back = remote(pback, precv, cs.at[1], cr.at[1], at.dp, at.sibling())
    back.start()
    for o in range(nd):
        cols = pl.ds(o * Dd, Dd)
        h1_out[:, cols] = tok[:, cols].astype(F32) + dot_nn(os_[mine, :], wo[o])
    back.wait_recv()
    h1_out[...] = h1_out[...] + precv[...].astype(F32)

    def put_xn2(cols, v):
        xn2_out[:, cols] = v

    scaled(h1_out[...], 1, put_xn2)
    for g in gw:
        g.forward()
    for s in range(2, nz):
        ldy.step(s)
    for g in gw:
        g.finish()
    for o in range(nz):
        dy_across(o).wait_recv()
    for cp in for_mlp[1:]:
        cp.wait()
    for g in gw:
        g.drain()
    ldy.drain()

    for s in range(1, nd):
        gain_copy(s).wait_send()
    for g in gkv:
        g.drain()
    xn1_across.wait_send()
    back.wait_send()
    lq.drain()
    lo.drain()
    lkv.drain()

    def drain(k, _):
        gq(k).drain_any()
        go(k).drain_any()
        return 0

    lax.fori_loop(0, nz, drain, 0)
    for cp in keep:
        cp.wait()


def attend(nd, nt, tok, gain, wq, wkv, wo, cosf, sins, lo, dy, w):
    R, D = tok.shape
    Dd, HC = wq.shape
    S = R * nt
    nz, ny = nt // 2, nd // 2
    dma = lambda *s: pltpu.SemaphoreType.DMA(s)
    hbm = pl.BlockSpec(memory_space=pltpu.HBM)
    vm = pl.BlockSpec(memory_space=pltpu.VMEM)
    shapes = [((R, D), F32), ((R, D), LOW), ((nd, 8, Dd), F32), ((nz * (HC // HD), 2 * R), F32),
              ((2 * R, D), LOW), ((nz, D, HC), LOW), ((nd, nz * HC, Dd), LOW), ((D, 2 * HD), LOW), ((S, 2 * HD), LOW),
              ((2 * R, nz * HC), LOW), ((2 * R, nz * HC), LOW)]
    gathered = [((S, D), LOW), ((2, w.shape[1], D), LOW)]
    yg = lambda n: [dma(n), dma(n, ny - 1), dma(n, ny - 1), dma(n, ny - 1), dma(n, nd)]
    return pl.pallas_call(
        functools.partial(attend_kernel, nd, nt),
        out_shape=tuple(jax.ShapeDtypeStruct(*s) for s in shapes + gathered),
        in_specs=[vm, vm, hbm, hbm, hbm, vm, vm, vm, hbm, hbm],
        out_specs=(vm, vm, vm, vm) + (hbm,) * 9,
        scratch_shapes=[pltpu.VMEM(*s) for s in shapes[4:]] + [pltpu.VMEM((HD, 2 * R), F32), pltpu.VMEM((R, D), LOW), pltpu.VMEM((R, D), LOW)]
        + [dma(3), dma(nd - 1), dma(nd - 1)] + yg(2) + yg(nz) + yg(nz)
        + [dma(nz)] * 3 + [dma(nz)] * 3 + [dma(nz)] * 5 + [dma(2), dma(2), dma(7)]
        + [dma(nz), dma(nz), dma(2, nz), dma(nz)] + yg(2) + [dma(3)],
        compiler_params=pltpu.CompilerParams(collective_id=2, has_side_effects=True, vmem_limit_bytes=63 << 20),
        cost_estimate=pl.CostEstimate(flops=20 << 30, bytes_accessed=40 << 20, transcendentals=8 * 512 * 2048),
        name="attend",
    )(tok, gain, wq, wkv, wo, cosf, sins, lo, dy, w)


class Scatter:
    def __init__(self, at, kind, view, land, land2, ss, rs, ss2, rs2):
        self.at, self.kind, self.view = at, kind, view
        self.land, self.land2 = land, land2
        self.ss, self.rs, self.ss2, self.rs2 = ss, rs, ss2, rs2

    def first(self):
        at = self.at
        out = []
        if self.kind == 0:
            for s in range(1, at.ny):
                for xx in range(at.nx):
                    slot = (s - 1) * at.nx + xx
                    o = lax.rem(at.y + s, at.ny) * at.nx + xx
                    out.append(remote(self.view(o), self.land(slot), self.ss.at[slot], self.rs.at[slot], at.y_peer(s), at.t))
        else:
            for yy in range(at.ny):
                o = yy * at.nx + 1 - at.x
                out.append(remote(self.view(o), self.land(yy), self.ss.at[yy], self.rs.at[yy], at.x_peer(), at.t))
        return out

    def second(self):
        at = self.at
        if self.kind == 0:
            return [remote(self.view(at.x_peer()), self.land2(0), self.ss2.at[0], self.rs2.at[0], at.x_peer(), at.t)]
        return [remote(self.view(at.y_peer(s)), self.land2(s - 1), self.ss2.at[s - 1], self.rs2.at[s - 1], at.y_peer(s), at.t)
                for s in range(1, at.ny)]

    def start(self):
        for cp in self.first():
            cp.start()

    def add(self, o, slots):
        total = self.view(o)[...].astype(F32)
        for slot in slots:
            total = total + self.land(slot)[...].astype(F32)
        self.view(o)[...] = total.astype(LOW)

    def middle(self):
        at = self.at
        for cp in self.first():
            cp.wait_recv()
        if self.kind == 0:
            self.add(at.x_peer(), [(s - 1) * at.nx + 1 - at.x for s in range(1, at.ny)])
        else:
            for s in range(1, at.ny):
                self.add(at.y_peer(s), [lax.rem(at.y + s, at.ny)])
        for cp in self.second():
            cp.start()
        if self.kind == 0:
            self.add(at.dp, [(s - 1) * at.nx + at.x for s in range(1, at.ny)])
        else:
            self.add(at.dp, [at.y])

    def total(self):
        total = self.view(self.at.dp)[...].astype(F32)
        for i, cp in enumerate(self.second()):
            cp.wait_recv()
            total = total + self.land2(i)[...].astype(F32)
        return total

    def drain(self):
        for cp in self.first() + self.second():
            cp.wait_send()

    def either(self, name, put=None):
        kind = self.kind
        for value in range(2):
            self.kind = value
            call = getattr(self, name)
            if put is None:
                pl.when(kind == value)(call)
            else:
                pl.when(kind == value)(lambda call=call: put(call()))
        self.kind = kind


def grads_kernel(nd, nt, dy, tok, gfull, cosf, sins, lo_row, lse, later,
                 h1_in, dxn2_in, xn1_in, wq_in, wo_in, wkv_in, kv_in, q_in, o_in,
                 mine_g, land_g, mine_u, land_u, down_in,
                 tgrad, gq_out, go_out, gkv_out, gg_out, norm_out, keep_g, keep_u, keep_d, keep_e, got_g, got_u, got_d, got_e,
                 xn1, wq, wo, wkv, kvs, qs, os_, dos, dh1b, dxn1, dkv, dq,
                 bg, bu, bd, be, lg, lu, ld, le, tg, tu, td, te,
                 ql, ql2, ol, ol2, qz, oz, qlz, olz, kvb, kland, kz, xrecv, wl, wcl, wd2, w2, w2l, wfin, gl, gpart, u2, u2l, gfin, share, norms, normd,
                 lsem, xsem, fs, fr, qss, qsr, qss2, qsr2, oss, osr, oss2, osr2, qzs, qzr, ozs, ozr,
                 ks, kr, kzs, kzr, ws, wr, wcs, wcr, w2s, w2r, w3s, w3r, us, ur, u2s, u2r, u3s, u3r, ns, nr, n2s, n2r, outs, hs, hr):
    at = Place(nd, nt)
    nz, nx, ny = at.nz, at.nx, at.ny
    R, D = tok.shape
    Dd = wo.shape[2]
    HC = wq.shape[2]
    Ds = wl.shape[1]
    NH = HC // HD
    KT = 2 * R
    S = kvs.shape[0]
    rows = lambda t: pl.ds(pl.multiple_of(t * R, R), R)
    drows = lambda o: pl.ds(pl.multiple_of(o * Dd, Dd), Dd)
    hcols = lambda j: pl.ds(pl.multiple_of(j * HC, HC), HC)
    mine, theirs = rows(at.c), rows(1 - at.c)
    scale = 1.0 / math.sqrt(HD)

    Fh = bd.shape[1]
    pieces = [(bg, mine_g), (bu, mine_u), (tg, land_g), (tu, land_u),
              (wo, wo_in), (os_, o_in), (qs, q_in), (kvs, kv_in), (xn1, xn1_in), (wq, wq_in), (wkv, wkv_in),
              (dxn1.at[pl.ds(0, R)], h1_in), (xrecv, dxn2_in)]
    down = lambda n, o: down_in.at[pl.ds(n * Fh, Fh), drows(o)]
    pieces += [(bd.at[xx], down(0, at.y * nx + xx)) for xx in range(nx)]
    pieces += [(be.at[yy], down(1, yy * nx + at.x)) for yy in range(ny)]
    loads = [pltpu.make_async_copy(src, dst, lsem.at[i]) for i, (dst, src) in enumerate(pieces)]
    for cp in loads[11:13] + loads[:11] + loads[13:]:
        cp.start()
    greet_all(at)

    down_hops = []
    for s in range(1, ny):
        for xx in range(nx):
            slot = (s - 1) * nx + xx
            o = lax.rem(at.y + s, ny) * nx + xx
            down_hops.append(remote(down(0, o), td.at[slot], hs.at[0, slot], hr.at[0, slot], at.y_peer(s), at.t))
    for yy in range(ny):
        down_hops.append(remote(down(1, yy * nx + 1 - at.x), te.at[yy], hs.at[1, yy], hr.at[1, yy], at.x_peer(), at.t))
    for cp in down_hops:
        cp.start()

    def rms_back(v_of, e_of, row, put):
        chunks = [pl.ds(o * Dd, Dd) for o in range(nd)]
        squares = jnp.zeros((R, 1), F32)
        inner = jnp.zeros((R, 1), F32)
        for o, cols in enumerate(chunks):
            v = v_of(cols)
            squares = squares + jnp.sum(v * v, axis=-1, keepdims=True)
            inner = inner + jnp.sum(e_of(cols) * gfull[o, row:row + 1, :] * v, axis=-1, keepdims=True)
        r = lax.rsqrt(squares / D + EPSILON)
        inner = inner * (r * r * r) / D
        for o, cols in enumerate(chunks):
            v, e = v_of(cols), e_of(cols)
            gpart[row:row + 1, cols] = jnp.sum(e * v * r, axis=0, keepdims=True)
            put(cols, r * (e * gfull[o, row:row + 1, :]) - v * inner)

    gpart[...] = jnp.zeros_like(gpart)

    def put_dh1(cols, v):
        total = dy[:, cols].astype(F32) + v
        tgrad[:, cols] = total
        dh1b[mine, cols] = total.astype(LOW)

    loads[11].wait()
    loads[12].wait()
    rms_back(lambda cols: dxn1[pl.ds(0, R), cols], lambda cols: xrecv[:, cols].astype(F32), 1, put_dh1)
    swap_dh1 = remote(dh1b.at[mine], dh1b.at[mine], xsem.at[0], xsem.at[1], at.dp, at.sibling())
    swap_dh1.start()

    for i in range(4, 11):
        loads[i].wait()
    swap_dh1.wait_recv()
    def do_pair(j, _):
        acc = dot_nt(dh1b[:, pl.ds(0, Dd)], wo[0, hcols(j), :])
        for o in range(1, nd):
            acc = acc + dot_nt(dh1b[:, pl.ds(o * Dd, Dd)], wo[o, hcols(j), :])
        dos[:, hcols(j)] = acc.astype(LOW)
        return 0

    lax.fori_loop(0, nz, do_pair, 0)

    def kind_of(k):
        return k % 2 if isinstance(k, int) else lax.rem(k, 2)

    def so(k):
        j = far_first(k, at.z, nz)
        return Scatter(at, kind_of(k), lambda o: wo.at[o, hcols(j)], lambda i: ol.at[k, i], lambda i: ol2.at[k, i],
                       oss.at[k], osr.at[k], oss2.at[k], osr2.at[k])

    def sq(k):
        j = far_first(k, at.z, nz)
        return Scatter(at, kind_of(k), lambda o: wq.at[j, drows(o)], lambda i: ql.at[k, i], lambda i: ql2.at[k, i],
                       qss.at[k], qsr.at[k], qss2.at[k], qsr2.at[k])

    def wo_unit(k, _):
        j = far_first(k, at.z, nz)

        def part(o, _):
            wo[o, hcols(j), :] = dot_tn(os_[:, hcols(j)], dh1b[:, drows(o)]).astype(LOW)
            return 0

        lax.fori_loop(0, nd, part, 0)
        so(k).either("start")
        return 0

    lax.fori_loop(0, nz, wo_unit, 0)

    def zpush(k, buf, land, ss, rs):
        j = far_first(k, at.z, nz)
        return remote(buf.at[k], land.at[at.z], ss.at[k], rs.at[at.z], at.dp, 2 * j + at.c)

    def o_total(k):
        def put(v):
            oz[k] = v.astype(LOW)

        so(k).either("total", put)
        pl.when(k < nz - 1)(lambda: zpush(k, oz, olz, ozs, ozr).start())

    def q_total(k):
        def put(v):
            qz[k] = v.astype(LOW)

        sq(k).either("total", put)
        pl.when(k < nz - 1)(lambda: zpush(k, qz, qlz, qzs, qzr).start())

    dkv[...] = jnp.zeros_like(dkv)
    dxn1[...] = jnp.zeros_like(dxn1)
    here = at.z * KT + lax.broadcasted_iota(jnp.int32, (1, KT), 1)
    low_row = lo_row[0:1, :]

    def unit(k, _):
        j = far_first(k, at.z, nz)
        for hh in range(NH):
            cols = pl.ds(pl.multiple_of(j * HC + hh * HD, HD), HD)
            hid = j * NH + hh
            lrow = lse[pl.ds(hid, 1), :]
            qh = qs[:, cols]
            doh = dos[:, cols]
            delta = jnp.sum((doh.astype(F32) * os_[:, cols].astype(F32)).T, axis=0, keepdims=True)
            dq[...] = jnp.zeros_like(dq)

            def tile(b, _):
                kr_ = pl.ds(pl.multiple_of(b * KT, KT), KT)
                kt = kvs[kr_, pl.ds(0, HD)]
                vt = kvs[kr_, pl.ds(HD, HD)]
                s = dot_nt(kt, qh)
                place = b * KT + lax.broadcasted_iota(jnp.int32, (KT, KT), 0)
                s = jnp.where((place >= low_row) & (place <= here), s * scale, MASKED)
                p = jnp.exp(s - lrow)
                dkv[kr_, pl.ds(HD, HD)] += dot_nn(p.astype(LOW), doh)
                ds = (p * (dot_nt(vt, doh) - delta)).astype(LOW)
                dkv[kr_, pl.ds(0, HD)] += dot_nn(ds, qh)
                dq[...] += dot_tn(ds, kt)
                return 0

            lax.fori_loop(0, at.z + 1, tile, 0)
            u = dq[...] * scale
            qs[:, cols] = (u * cosf[...] - swap_halves(u) * sins[...]).astype(LOW)
        dqp = qs[:, hcols(j)]

        def back(o, _):
            dxn1[:, drows(o)] += dot_nt(dqp, wq[j, drows(o), :])
            wq[j, drows(o), :] = dot_tn(xn1[:, drows(o)], dqp).astype(LOW)
            return 0

        lax.fori_loop(0, nd, back, 0)
        sq(k).either("start")
        pl.when(k >= 1)(lambda: so(k - 1).either("middle"))
        pl.when(k >= 2)(lambda: o_total(k - 2))
        return 0

    lax.fori_loop(0, nz, unit, 0)

    dkv[:, pl.ds(0, HD)] = dkv[:, pl.ds(0, HD)] * scale
    kvb[...] = dkv[...].astype(LOW)
    kswap = [remote(kvb.at[rows(2 * zz + 1 - at.c)], kland.at[zz], ks.at[zz], kr.at[zz], at.dp, at.sibling()) for zz in range(nz)]
    for cp in kswap:
        cp.start()
    swap_dh1.wait_send()
    dh1b[mine, :] = dxn1[theirs, :].astype(LOW)
    xswap = remote(dh1b.at[mine], xrecv, xsem.at[2], xsem.at[3], at.dp, at.sibling())
    xswap.start()

    def kpush(s):
        zz = lax.rem(at.z + s, nz)
        return remote(kvb.at[rows(2 * zz + at.c)], kz.at[s - 1], kzs.at[s - 1], kzr.at[s - 1], at.dp, 2 * zz + at.c)

    k_last = jnp.int32(nz - 1)
    so(k_last).either("middle")
    for s in range(1, nz + 1):
        zz = lax.rem(at.z + s, nz)
        r = rows(2 * zz + at.c)
        remote(kvb.at[rows(0)], kland.at[zz], ks.at[zz], kr.at[zz], at.dp, at.sibling()).wait_recv()
        dkv[r, :] = dkv[r, :] + kland[zz].astype(F32)
        if s < nz:
            kvb[r, :] = dkv[r, :].astype(LOW)
            kpush(s).start()

    lax.fori_loop(0, max(nz - 2, 1), lambda k, _: (sq(k).either("middle"), 0)[1], 0)
    if nz >= 2:
        o_total(jnp.int32(nz - 2))
    total = dkv[rows(at.t), :] + later[...].astype(F32)
    for s in range(1, nz):
        kpush(s).wait_recv()
        total = total + kz[s - 1].astype(F32)
    dk = total[:, :HD]
    dk = dk * cosf[mine, :] - swap_halves(dk) * sins[mine, :]
    dkvp = jnp.concatenate([dk, total[:, HD:]], axis=1).astype(LOW)


    slices = lambda t: pl.ds(pl.multiple_of(t * Ds, Ds), Ds)

    def wswap(zz):
        return remote(wd2.at[slices(2 * zz + 1 - at.c)], wcl.at[zz], wcs.at[zz], wcr.at[zz], at.dp, at.sibling())

    def wpush(s):
        zz = lax.rem(at.z + s, nz)
        return remote(wd2.at[slices(2 * zz + at.c)], wl.at[s - 1], ws.at[s - 1], wr.at[s - 1], at.dp, 2 * zz + at.c)

    def upush(s):
        tt = lax.rem(at.t + s, nt)
        return remote(gpart.at[:, slices(tt)], gl.at[at.t], us.at[s - 1], ur.at[at.t], at.dp, tt)

    for o in range(nd):
        wd2[pl.ds(o * Dd, Dd), :] = dot_tn(xn1[mine, pl.ds(o * Dd, Dd)], dkvp).astype(LOW)
    for zz in range(nz):
        wswap(zz).start()
    lax.fori_loop(max(nz - 2, 1), nz, lambda k, _: (sq(k).either("middle"), 0)[1], 0)
    for s in range(1, nz + 1):
        zz = lax.rem(at.z + s, nz)
        r = slices(2 * zz + at.c)
        remote(wd2.at[slices(0)], wcl.at[zz], wcs.at[zz], wcr.at[zz], at.dp, at.sibling()).wait_recv()
        wd2[r, :] = (wd2[r, :].astype(F32) + wcl[zz].astype(F32)).astype(LOW)
        if s < nz:
            wpush(s).start()
    o_total(k_last)

    big = []
    for n, (buf, got, second) in enumerate([(bg, tg, lg), (bu, tu, lu), (bd, td, ld), (be, te, le)]):
        if n < 2:
            loads[n].wait()
            loads[2 + n].wait()
        elif n == 2:
            for cp in loads[13:]:
                cp.wait()
            for cp in down_hops:
                cp.wait_recv()
        if n % 2 == 0:
            keep, keep_slots = at.x, [(s - 1) * nx + at.x for s in range(1, ny)]
            away = [(1 - at.x, [(s - 1) * nx + 1 - at.x for s in range(1, ny)], at.x_peer())]
        else:
            keep, keep_slots = at.y, [at.y]
            away = [(lax.rem(at.y + s, ny), [lax.rem(at.y + s, ny)], at.y_peer(s)) for s in range(1, ny)]
        copies = []
        for i, (place, slots, peer) in enumerate(away):
            total = buf[place].astype(F32)
            for slot in slots:
                total = total + got[slot].astype(F32)
            buf[place] = total.astype(LOW)
            copies.append(remote(buf.at[place], second.at[i], fs.at[n, i], fr.at[n, i], peer, at.t))
            copies[-1].start()
        total = buf[keep].astype(F32)
        for slot in keep_slots:
            total = total + got[slot].astype(F32)
        buf[keep] = total.astype(LOW)
        big.append((buf, keep, second, copies))

    xswap.wait_recv()
    for o in range(nd):
        cols = pl.ds(o * Dd, Dd)
        dxn1[mine, cols] = dxn1[mine, cols] + xrecv[:, cols].astype(F32) + dot_nt(dkvp, wkv[cols, :])

    def put_tokens(cols, v):
        tgrad[:, cols] = tgrad[:, cols] + v

    rms_back(lambda cols: tok[:, cols].astype(F32), lambda cols: dxn1[mine, cols], 0, put_tokens)
    for s in range(1, nt):
        upush(s).start()

    lax.fori_loop(0, max(nz - 2, 1), lambda k, _: (q_total(k), 0)[1], 0)

    per = nt // nd
    gl[at.t] = gpart[:, slices(at.t)]
    wsum = wd2[slices(at.t), :].astype(F32)
    for s in range(1, nz):
        wpush(s).wait_recv()
        wsum = wsum + wl[s - 1].astype(F32)
    for s in range(1, nt):
        o = lax.rem(at.t + s, nt)
        remote(gpart.at[:, pl.ds(0, Ds)], gl.at[o], us.at[s - 1], ur.at[o], at.dp, o).wait_recv()
    usum = gl[0]
    for o in range(1, nt):
        usum = usum + gl[o]
    owner = at.t // per
    is_owner = at.dp == owner
    slot = jnp.where(is_owner, at.t - at.dp * per, 0)
    w2[...] = wsum.astype(LOW)
    u2[...] = usum
    to = jnp.where(is_owner, lax.rem(at.dp + 1, nd), owner)
    give_w = remote(w2, w2l.at[at.dp], w2s.at[0], w2r.at[at.dp], to, at.t)
    give_u = remote(u2, u2l.at[at.dp], u2s.at[0], u2r.at[at.dp], to, at.t)

    def spread(q, i, t):
        return [remote(wfin.at[q], wfin.at[q], w3s.at[q, i], w3r.at[q], at.dp, t),
                remote(gfin.at[q], gfin.at[q], u3s.at[q, i], u3r.at[q], at.dp, t)]

    def spread_along(s):
        return spread(slot, s, 2 * lax.rem(at.z + s, nz) + at.c)

    @pl.when(jnp.logical_not(is_owner))
    def _():
        give_w.start()
        give_u.start()

    lax.fori_loop(max(nz - 2, 1), nz, lambda k, _: (q_total(k), 0)[1], 0)

    def square(v):
        return jnp.sum(v * v, axis=(0, 1), keepdims=True)

    share[...] = jnp.zeros_like(share)

    @pl.when(is_owner)
    def _():
        w2l[at.dp] = w2[...]
        u2l[at.dp] = u2[...]
        for s in range(1, nd):
            o = lax.rem(at.dp + s, nd)
            remote(w2, w2l.at[o], w2s.at[0], w2r.at[o], o, at.t).wait_recv()
            remote(u2, u2l.at[o], u2s.at[0], u2r.at[o], o, at.t).wait_recv()
        wtot = w2l[0].astype(F32)
        utot = u2l[0]
        for o in range(1, nd):
            wtot = wtot + w2l[o].astype(F32)
            utot = utot + u2l[o]
        wfin[slot] = wtot.astype(LOW)
        gfin[slot] = utot
        shared = square(wtot.astype(LOW).astype(F32)) + square(utot)
        share[...] = jnp.broadcast_to(shared, share.shape)
        for s in range(1, nz):
            for cp in spread_along(s):
                cp.start()

    squares = jnp.zeros((1, 1), F32)
    out_copies = []
    for n, (buf, keep, second, copies) in enumerate(big):
        total = buf[keep].astype(F32)
        for i, cp in enumerate(copies):
            cp.wait_recv()
            total = total + second[i].astype(F32)
        squares = squares + square(total)
        out_copies.append(pltpu.make_async_copy(second, (got_g, got_u, got_d, got_e)[n], outs.at[n]))
        out_copies.append(pltpu.make_async_copy(buf.at[keep], (keep_g, keep_u, keep_d, keep_e)[n], outs.at[4 + n]))
        for cp in out_copies[-2:]:
            cp.start()
    own_k = nz - 1
    for buf, land, ss, rs, out in ((oz, olz, ozs, ozr, go_out), (qz, qlz, qzs, qzr, gq_out)):
        total = buf[own_k].astype(F32)
        for s in range(1, nz):
            zz = lax.rem(at.z + s, nz)
            remote(buf.at[0], land.at[zz], ss.at[0], rs.at[zz], at.dp, at.sibling()).wait_recv()
            total = total + land[zz].astype(F32)
        squares = squares + square(total)
        out[...] = total
    squares = squares + share[0:1, 0:1]

    norms[at.t] = jnp.broadcast_to(squares, norms.shape[1:])

    def npush(s):
        return remote(norms.at[at.t], norms.at[at.t], ns.at[s - 1], nr.at[at.t], at.dp, lax.rem(at.t + s, nt))

    def n2push(s):
        return remote(normd.at[at.dp], normd.at[at.dp], n2s.at[s - 1], n2r.at[at.dp], lax.rem(at.dp + s, nd), at.t)

    for s in range(1, nt):
        npush(s).start()
    for s in range(1, nt):
        o = lax.rem(at.t + s, nt)
        remote(norms.at[o], norms.at[o], ns.at[s - 1], nr.at[o], at.dp, o).wait_recv()
    group = norms[0]
    for o in range(1, nt):
        group = group + norms[o]
    normd[at.dp] = group
    for s in range(1, nd):
        n2push(s).start()
    for s in range(1, nd):
        o = lax.rem(at.dp + s, nd)
        remote(normd.at[o], normd.at[o], n2s.at[s - 1], n2r.at[o], o, at.t).wait_recv()
    group = normd[0]
    for o in range(1, nd):
        group = group + normd[o]
    norm_out[...] = jnp.sqrt(group)

    for q in range(per):
        t_from = at.dp * per + q
        same = at.c == lax.rem(t_from, 2)

        def slice_came(q=q):
            for cp in spread(q, 0, at.sibling()):
                cp.wait_recv()

        pl.when(at.t != t_from)(slice_came)

        @pl.when(same)
        def _(q=q):
            for cp in spread(q, 0, at.sibling()):
                cp.start()

        gkv_out[pl.ds(q * Ds, Ds), :] = wfin[q].astype(F32)
        gg_out[:, pl.ds(q * Ds, Ds)] = gfin[q]

        @pl.when(same)
        def _(q=q):
            for cp in spread(q, 0, at.sibling()):
                cp.wait_send()

    for cp in out_copies:
        cp.wait()
    for cp in down_hops:
        cp.wait_send()
    xswap.wait_send()
    for _, _, _, copies in big:
        for cp in copies:
            cp.wait_send()
    for cp in kswap:
        cp.wait_send()
    for s in range(1, nz):
        kpush(s).wait_send()
    for zz in range(nz):
        wswap(zz).wait_send()
    for s in range(1, nz):
        wpush(s).wait_send()
    for s in range(1, nt):
        upush(s).wait_send()
        npush(s).wait_send()
    for s in range(1, nd):
        n2push(s).wait_send()

    def drain(k, _):
        so(k).either("drain")
        sq(k).either("drain")

        @pl.when(k < nz - 1)
        def _():
            zpush(k, oz, olz, ozs, ozr).wait_send()
            zpush(k, qz, qlz, qzs, qzr).wait_send()

        return 0

    lax.fori_loop(0, nz, drain, 0)

    @pl.when(jnp.logical_not(is_owner))
    def _():
        give_w.wait_send()
        give_u.wait_send()

    @pl.when(is_owner)
    def _():
        for s in range(1, nz):
            for cp in spread_along(s):
                cp.wait_send()


def grads(nd, nt, small, big_in, pieces):
    R, D = small[1].shape
    nz, ny = nt // 2, nd // 2
    h1, dxn2, xn1, wq, wo, wkv, kv, q, o = big_in
    Dd, HC = wo.shape[2], wq.shape[2]
    F = pieces[0].shape[1]
    Fh = F // 2
    S = R * nt
    Ds = D // nt
    W2 = 2 * HD
    slots = max(2 * (ny - 1), ny)
    hops = max(1, ny - 1)
    dma = lambda *s: pltpu.SemaphoreType.DMA(s)
    hbm = pl.BlockSpec(memory_space=pltpu.HBM)
    vm = pl.BlockSpec(memory_space=pltpu.VMEM)
    b = lambda *s: pltpu.VMEM(s, LOW)
    f = lambda *s: pltpu.VMEM(s, F32)
    shapes = [(R, D), (Dd, HC), (HC, Dd), (Dd, W2), (8, Dd), (8, 128)]
    lows = [(F, Dd), (F, Dd), (Fh, Dd), (Fh, Dd), (1, F, Dd), (hops, F, Dd), (1, Fh, Dd), (hops, Fh, Dd)]
    return pl.pallas_call(
        functools.partial(grads_kernel, nd, nt),
        out_shape=tuple([jax.ShapeDtypeStruct(s, F32) for s in shapes] + [jax.ShapeDtypeStruct(s, LOW) for s in lows]),
        in_specs=[vm] * 8 + [hbm] * 14,
        out_specs=(vm,) * 6 + (hbm,) * 8,
        scratch_shapes=[
            b(2 * R, D), b(nz, D, HC), b(nd, nz * HC, Dd), b(D, W2), b(S, W2), b(2 * R, nz * HC), b(2 * R, nz * HC), b(2 * R, nz * HC),
            b(2 * R, D), f(2 * R, D), f(S, W2), f(2 * R, HD),
            b(2, F, Dd), b(ny, F, Dd), b(2, Fh, Dd), b(ny, Fh, Dd),
            b(1, F, Dd), b(hops, F, Dd), b(1, Fh, Dd), b(hops, Fh, Dd),
            b(2 * (ny - 1), F, Dd), b(ny, F, Dd), b(2 * (ny - 1), Fh, Dd), b(ny, Fh, Dd),
            b(nz, slots, Dd, HC), b(nz, hops, Dd, HC), b(nz, slots, HC, Dd), b(nz, hops, HC, Dd),
            b(nz, Dd, HC), b(nz, HC, Dd), b(nz, Dd, HC), b(nz, HC, Dd),
            b(S, W2), b(nz, R, W2), b(nz, R, W2), b(R, D),
            b(nz, Ds, W2), b(nz, Ds, W2), b(D, W2), b(Ds, W2), b(nd, Ds, W2), b(nt // nd, Ds, W2),
            f(nt, 8, Ds), f(8, D), f(8, Ds), f(nd, 8, Ds), f(nt // nd, 8, Ds), f(8, 128), f(nt, 8, 128), f(nd, 8, 128),
            dma(13 + 2 + ny), dma(4), dma(4, hops), dma(4, hops),
            dma(nz, slots), dma(nz, slots), dma(nz, hops), dma(nz, hops), dma(nz, slots), dma(nz, slots), dma(nz, hops), dma(nz, hops),
            dma(nz), dma(nz), dma(nz), dma(nz),
            dma(nz), dma(nz), dma(nz), dma(nz),
            dma(nz), dma(nz), dma(nz), dma(nz), dma(1), dma(nd), dma(nt // nd, nz), dma(nt // nd),
            dma(nt), dma(nt), dma(1), dma(nd), dma(nt // nd, nz), dma(nt // nd),
            dma(nt), dma(nt), dma(nd), dma(nd), dma(8), dma(2, slots), dma(2, slots),
        ],
        compiler_params=pltpu.CompilerParams(collective_id=3, has_side_effects=True, vmem_limit_bytes=63 << 20),
        cost_estimate=pl.CostEstimate(flops=30 << 30, bytes_accessed=40 << 20, transcendentals=8 * 512 * 2048),
        name="grads",
    )(*small, *big_in, *pieces)


def advance(grad_raw, weight, moment, average, factor, rate):
    average_decay = min(AVERAGE_TOP, (1.0 + STEP) / (10.0 + STEP))
    clipped = grad_raw * factor
    moment_new = MOMENTUM * moment + clipped
    weight_new = weight - rate * (clipped + MOMENTUM * moment_new)
    average_new = average_decay * average + (1.0 - average_decay) * weight_new
    return (clipped, moment_new, average_new, weight_new, weight_new.astype(jnp.bfloat16))


def local(
    tokens,
    cotangent,
    kv_later,
    lengths,
    query_weight,
    query_moment,
    query_average,
    keyvalue_weight,
    keyvalue_moment,
    keyvalue_average,
    output_weight,
    output_moment,
    output_average,
    gateup_weight,
    gateup_moment,
    gateup_average,
    down_weight,
    down_moment,
    down_average,
    norm_gains,
    gains_moment,
    gains_average,
):
    masters = (query_weight, keyvalue_weight, output_weight, gateup_weight, down_weight, norm_gains)
    low_query, low_kv, low_output, _, _, low_gains = (w.astype(LOW) for w in masters)
    low_gateup = jnp.swapaxes(gateup_weight, 1, 2).astype(LOW)
    low_down = down_weight.astype(LOW)
    nd, nt = lax.axis_size("dp"), lax.axis_size("tensor")
    row_count = tokens.shape[0]
    pair_rows = 2 * row_count

    doc_lengths = lengths[0]
    endings = jnp.cumsum(doc_lengths)
    beginnings = endings - doc_lengths
    places = (lax.axis_index("tensor") // 2) * pair_rows + jnp.arange(pair_rows, dtype=jnp.int32)
    segment = jnp.sum((places[:, None] >= endings[None, :]).astype(jnp.int32), axis=1)
    picked = segment[:, None] == jnp.arange(doc_lengths.shape[0], dtype=jnp.int32)[None, :]
    first = jnp.sum(jnp.where(picked, beginnings[None, :], 0), axis=1).astype(jnp.int32)
    half_size = HD // 2
    frequency = jnp.exp(jnp.arange(half_size, dtype=F32) * (-2.0 * math.log(ROPE_BASE) / HD))
    angles = (places - first).astype(F32)[:, None] * frequency[None, :]
    cosine, sine = jnp.cos(angles), jnp.sin(angles)
    cosine_full = jnp.concatenate([cosine, cosine], axis=1)
    sine_full = jnp.concatenate([-sine, sine], axis=1)
    first_rows = jnp.broadcast_to(first[None, :], (8, pair_rows))
    gain_rows = jnp.pad(low_gains.astype(F32), ((0, 6), (0, 0)))

    hidden_one, normed_two, gains_all, lse, normed_one, all_query, all_output, all_kv, kv_rows, queries, attended, grad_rows, gate_up = attend(
        nd, nt, tokens, gain_rows, low_query, low_kv, low_output, cosine_full, sine_full, first_rows,
        cotangent, low_gateup
    )
    grad_normed_two, *pieces, mlp_rows = mlp(nd, nt, normed_two, grad_rows, gate_up, low_down)
    cores = [list(range(core, nt, 2)) for core in range(2)]
    mlp_own = lax.psum_scatter(mlp_rows, "tensor", scatter_dimension=0, axis_index_groups=cores, tiled=False)
    mixed = hidden_one + mlp_own.astype(F32)
    tokens_grad, own_query, own_output, grad_keyvalue, gains_sum, norm_tile, *halves = grads(
        nd,
        nt,
        (cotangent, tokens, gains_all, cosine_full, sine_full, first_rows, lse, kv_later),
        (hidden_one, grad_normed_two, normed_one, all_query, all_output, all_kv, kv_rows, queries, attended),
        pieces,
    )
    whole = [kept.astype(F32) + jnp.sum(got.astype(F32), axis=0) for kept, got in zip(halves[:4], halves[4:])]
    own_gateup = jnp.swapaxes(jnp.stack(whole[:2]), 1, 2)
    own_down = jnp.concatenate(whole[2:], axis=0)
    grad_gains = gains_sum[:2]
    grad_norm = norm_tile[0, 0]
    factor = jnp.minimum(1.0, CLIP / (grad_norm + 1e-06))
    query_set = advance(
        own_query, query_weight, query_moment, query_average, factor, LEARNING_RATES[0]
    )
    keyvalue_set = advance(
        grad_keyvalue, keyvalue_weight, keyvalue_moment, keyvalue_average, factor, LEARNING_RATES[1]
    )
    output_set = advance(
        own_output, output_weight, output_moment, output_average, factor, LEARNING_RATES[2]
    )
    gateup_set = advance(
        own_gateup, gateup_weight, gateup_moment, gateup_average, factor, LEARNING_RATES[3]
    )
    down_set = advance(own_down, down_weight, down_moment, down_average, factor, LEARNING_RATES[4])
    gains_set = advance(
        grad_gains, norm_gains, gains_moment, gains_average, factor, LEARNING_RATES[5]
    )
    return (
        mixed,
        mixed.astype(jnp.bfloat16),
        tokens_grad,
        grad_norm,
        query_set[0],
        query_set[1],
        query_set[2],
        query_set[3],
        query_set[4],
        keyvalue_set[0],
        keyvalue_set[1],
        keyvalue_set[2],
        keyvalue_set[3],
        keyvalue_set[4],
        output_set[0],
        output_set[1],
        output_set[2],
        output_set[3],
        output_set[4],
        gateup_set[0],
        gateup_set[1],
        gateup_set[2],
        gateup_set[3],
        gateup_set[4],
        down_set[0],
        down_set[1],
        down_set[2],
        down_set[3],
        down_set[4],
        gains_set[0],
        gains_set[1],
        gains_set[2],
        gains_set[3],
        gains_set[4],
    )


def solution(mesh):
    return jax.shard_map(
        local,
        mesh=mesh,
        in_specs=(
            P(("dp", "tensor"), None),
            P(("dp", "tensor"), None),
            P(("dp", "tensor"), None),
            P("dp", None),
            P("dp", "tensor"),
            P("dp", "tensor"),
            P("dp", "tensor"),
            P("dp", None),
            P("dp", None),
            P("dp", None),
            P("tensor", "dp"),
            P("tensor", "dp"),
            P("tensor", "dp"),
            P(None, "dp", "tensor"),
            P(None, "dp", "tensor"),
            P(None, "dp", "tensor"),
            P("tensor", "dp"),
            P("tensor", "dp"),
            P("tensor", "dp"),
            P(None, "dp"),
            P(None, "dp"),
            P(None, "dp"),
        ),
        out_specs=(
            P(("dp", "tensor"), None),
            P(("dp", "tensor"), None),
            P(("dp", "tensor"), None),
            P(),
            P("dp", "tensor"),
            P("dp", "tensor"),
            P("dp", "tensor"),
            P("dp", "tensor"),
            P("dp", "tensor"),
            P("dp", None),
            P("dp", None),
            P("dp", None),
            P("dp", None),
            P("dp", None),
            P("tensor", "dp"),
            P("tensor", "dp"),
            P("tensor", "dp"),
            P("tensor", "dp"),
            P("tensor", "dp"),
            P(None, "dp", "tensor"),
            P(None, "dp", "tensor"),
            P(None, "dp", "tensor"),
            P(None, "dp", "tensor"),
            P(None, "dp", "tensor"),
            P("tensor", "dp"),
            P("tensor", "dp"),
            P("tensor", "dp"),
            P("tensor", "dp"),
            P("tensor", "dp"),
            P(None, "dp"),
            P(None, "dp"),
            P(None, "dp"),
            P(None, "dp"),
            P(None, "dp"),
        ),
        check_vma=False,
    )
```
